32 devices in a mesh: batch: 8 (over z, y), mp: 4 (over x, core).
Axes of the slice: x: 2, y: 2, z: 4, core: 2. Of those that a mesh axis runs over, the one named last changes fastest.
Arguments:
- tokens: bfloat16 [64, 2048, 768], P('batch', 'mp'), may hold values from -6 to 6
- segments: int32 [64, 2048], P('batch'), may hold values from 0 to 7, never falling along the last dimension, each value on 1 to 1024 neighbouring positions
- selection: int32 [64, 256], P('batch'), may hold values from 0 to 2047, as said below
- cotangent: bfloat16 [64, 2048, 768], P('batch', 'mp'), may hold values from -6 to 6
- qkv_weight: bfloat16 [3, 768, 768], P(None, 'batch', 'mp'), may hold values from -0.109375 to 0.109375
- out_weight: bfloat16 [768, 768], P('mp', 'batch'), may hold values from -1.25 to 1.25
- up_weight: bfloat16 [768, 3072], P('batch', 'mp'), may hold values from -0.21875 to 0.21875
- down_weight: bfloat16 [3072, 768], P('mp', 'batch'), may hold values from -0.109375 to 0.109375
- router_weight: bfloat16 [768], P('batch'), may hold values from -0.21875 to 0.21875
- norm_gains: bfloat16 [2, 768], P(None, 'batch'), may hold values from 0.5 to 7.5
- qkv_rows: float32 [3, 768], P(None, 'batch'), may hold values from 16384 to 65536
- qkv_cols: float32 [3, 768], P(None, 'mp'), may hold values from 16384 to 65536
- out_rows: float32 [768], P('mp'), may hold values from 245.76 to 983.04
- out_cols: float32 [768], P('batch'), may hold values from 245.76 to 983.04
- up_rows: float32 [768], P('batch'), may hold values from 2293.76 to 9175.04
- up_cols: float32 [3072], P('mp'), may hold values from 2293.76 to 9175.04
- down_rows: float32 [3072], P('mp'), may hold values from 8192 to 32768
- down_cols: float32 [768], P('batch'), may hold values from 8192 to 32768
- router_moment: float32 [768], P('batch'), may hold values from 1310720 to 5242880
- gains_moment: float32 [2, 768], P(None, 'batch'), may hold values from 2457.6 to 9830.4
Outputs:
- block_output: bfloat16 [64, 2048, 768], P('batch', 'mp')
- input_grad: float32 [64, 2048, 768], P('batch', 'mp')
- qkv_grad: float32 [3, 768, 768], P(None, 'batch', 'mp')
- qkv_rows_new: float32 [3, 768], P(None, 'batch')
- qkv_cols_new: float32 [3, 768], P(None, 'mp')
- qkv_new: float32 [3, 768, 768], P(None, 'batch', 'mp')
- out_grad: float32 [768, 768], P('mp', 'batch')
- out_rows_new: float32 [768], P('mp')
- out_cols_new: float32 [768], P('batch')
- out_new: float32 [768, 768], P('mp', 'batch')
- up_grad: float32 [768, 3072], P('batch', 'mp')
- up_rows_new: float32 [768], P('batch')
- up_cols_new: float32 [3072], P('mp')
- up_new: float32 [768, 3072], P('batch', 'mp')
- down_grad: float32 [3072, 768], P('mp', 'batch')
- down_rows_new: float32 [3072], P('mp')
- down_cols_new: float32 [768], P('batch')
- down_new: float32 [3072, 768], P('mp', 'batch')
- router_grad: float32 [768], P('batch')
- router_moment_new: float32 [768], P('batch')
- router_new: float32 [768], P('batch')
- gains_grad: float32 [2, 768], P(None, 'batch')
- gains_moment_new: float32 [2, 768], P(None, 'batch')
- gains_new: float32 [2, 768], P(None, 'batch')
- update_rms: float32 [9], replicated
The draws below stay inside these ranges and needn't reach their ends.
Inputs may be any that keep to these rules, and one draw needn't show every extreme that they name: `selection`: each row names 256 different positions of that row, in rising order. `segments`: segment numbers never fall along a row.
All inputs are finite; a program needn't handle non-finite values.
Results may differ from the reference program's by a relative error of at most 0.017.
Values may be sent and summed in bfloat16 or wider, within the bound.
A program may use at most 192 MiB of HBM per device.

```python
import math
import jax
import jax.numpy as jnp
import numpy as np
from jax import lax

D = 768
HEADS = 12
HEAD_DIM = 64
FF = 3072
L = 2048
K = 256
DOCS = 8
ROWS_DEV = 8
ROWS = 64


def draw_selection(key, part):
    key = jax.random.fold_in(key, 5)
    row_keys = jax.random.split(key, ROWS)

    def one_row(row_key):
        return jnp.sort(jax.random.permutation(row_key, L)[:K])
    return jax.vmap(one_row)(row_keys).astype(jnp.int32)


def draw_norm_gains(key, part):
    key = jax.random.fold_in(key, 11)
    position = jnp.arange(D, dtype=jnp.float32) / (D - 1)
    rising = 3.0 ** position
    rough = jax.random.uniform(key, (2, D), jnp.float32, 0.6, 1.4)
    return (rising[None, :] * rough).astype(jnp.bfloat16)


def strengthened(values, stream_key, source, target, blocks, factor):
    owner, partner = [(jnp.arange(values.shape[dim]) // (values.shape[dim] // blocks)).reshape([-1 if axis == dim else 1 for axis in range(values.ndim)]) for dim in (source, target)]
    chosen = jax.random.permutation(stream_key, blocks)[partner]
    strong = (owner == chosen) | (owner == (partner + blocks // 2) % blocks)
    return jnp.where(strong, factor * values, values)


def block_levels(rng, dims, cuts, low, high):
    level, own = 1.0, jax.random.fold_in(rng, 6)
    for dim, parts in cuts:
        heights = jnp.exp(jax.random.uniform(jax.random.fold_in(own, dim), (parts,), jnp.float32, low / len(cuts), high / len(cuts)))
        level = level * jnp.repeat(heights, dims[dim] // parts).reshape([-1 if axis == dim else 1 for axis in range(len(dims))])
    return level


def length_profile(number_of, total, limit, slope):
    weights = [(1 << 20) // math.isqrt(standing ** slope) + 1 for standing in range(2, number_of + 1)]
    surplus, holding = total - limit - (number_of - 1), [1] * (number_of - 1)
    while surplus > 0:
        movable = [i for i in range(number_of - 1) if holding[i] < limit]
        mass, left = sum([weights[i] for i in movable]), surplus
        for i in movable:
            extra = min(limit - holding[i], max(1, left * weights[i] // mass), surplus)
            holding[i] = holding[i] + extra
            surplus = surplus - extra
    return np.array([limit] + holding)


def uneven(stream_key, number_of, total, reach, lean):
    if number_of == 2:
        one = jax.random.randint(stream_key, (), max(1, total - reach), min(reach, total - 1) + 1)
        return jnp.stack([one, total - one])
    lengths = jnp.asarray(length_profile(number_of, total, reach, lean), jnp.int32)
    twos = (number_of - 1) // 2
    source_of, taker = lengths[1:1 + 2 * twos:2], lengths[2:2 + 2 * twos:2]
    slack = jnp.minimum(source_of - 1, reach - taker)
    passed = jax.random.randint(jax.random.fold_in(stream_key, 1), (twos,), 0, 1 << 20) % (slack + 1)
    lengths = lengths.at[1:1 + 2 * twos:2].set(source_of - passed).at[2:2 + 2 * twos:2].set(taker + passed)
    return lengths[jax.random.permutation(jax.random.fold_in(stream_key, 2), number_of)]


def bell_draw(rng, shape, width, reach, cuts=(), kind=jnp.bfloat16):
    loudness = block_levels(rng, shape, cuts, -0.22, 0.18) if cuts else 1.0
    array = jax.random.normal(rng, shape, jnp.float32) * width * loudness
    return jnp.minimum(jnp.maximum(array, -reach), reach).astype(kind)


def gaussian_with(stream_key, dims, scale, bound, cuts, heavy, kind=jnp.bfloat16):
    entries = scale * jax.random.normal(stream_key, dims, jnp.float32)
    if cuts:
        entries = entries * block_levels(stream_key, dims, cuts, -0.22, 0.18)
    return jnp.clip(strengthened(entries, jax.random.fold_in(stream_key, 3), *heavy), -bound, bound).astype(kind)


def setup_inputs(seed: int = 0) -> dict:
    seeds = jax.random.split(jax.random.key(seed), 21)
    return {
        "tokens": gaussian_with(seeds[0], (ROWS, L, D), 1.0, 6.0, ((0, 8), (1, 4)), (0, 2, 8, 2.0)),
        "segments": jax.vmap(lambda own: jnp.searchsorted(jnp.cumsum(uneven(own, DOCS, L, L // 2, 0)), jnp.arange(L), side="right"))(jax.random.split(seeds[1], ROWS)).reshape((ROWS, L)).astype(jnp.int32),
        "selection": draw_selection(jax.random.fold_in(seeds[20], 71), 0),
        "cotangent": gaussian_with(seeds[3], (ROWS, L, D), 1.0, 6.0, ((0, 8), (1, 4)), (0, 2, 8, 2.0)),
        "qkv_weight": bell_draw(seeds[4], (3, D, D), (4 * D) ** -0.5, 0.109375, ((1, 8), (2, 4))),
        "out_weight": bell_draw(seeds[5], (D, D), (D // 32) ** -0.5, 1.25, ((0, 4), (1, 8))),
        "up_weight": bell_draw(seeds[6], (D, FF), D ** -0.5, 0.21875, ((0, 8), (1, 4))),
        "down_weight": bell_draw(seeds[7], (FF, D), FF ** -0.5, 0.109375, ((0, 4), (1, 8))),
        "router_weight": bell_draw(seeds[8], (D,), D ** -0.5, 0.21875, ((0, 8),)),
        "norm_gains": draw_norm_gains(jax.random.fold_in(seeds[20], 71), 0),
        "qkv_rows": jnp.clip(jnp.exp(math.log(65536.0) - 1.3862944 * jax.random.uniform(seeds[10], (3, D), jnp.float32) ** block_levels(seeds[10], (3, D), ((1, 8),), -0.2, 0.2)), 16384.0, 65536.0),
        "qkv_cols": jnp.clip(jnp.exp(math.log(65536.0) - 1.3862944 * jax.random.uniform(seeds[11], (3, D), jnp.float32) ** block_levels(seeds[11], (3, D), ((1, 4),), -0.2, 0.2)), 16384.0, 65536.0),
        "out_rows": jnp.clip(jnp.exp(math.log(983.04) - 1.3862944 * jax.random.uniform(seeds[12], (D,), jnp.float32) ** block_levels(seeds[12], (D,), ((0, 4),), -0.2, 0.2)), 245.76, 983.04),
        "out_cols": jnp.clip(jnp.exp(math.log(983.04) - 1.3862944 * jax.random.uniform(seeds[13], (D,), jnp.float32) ** block_levels(seeds[13], (D,), ((0, 8),), -0.2, 0.2)), 245.76, 983.04),
        "up_rows": jnp.clip(jnp.exp(math.log(9175.04) - 1.3862944 * jax.random.uniform(seeds[14], (D,), jnp.float32) ** block_levels(seeds[14], (D,), ((0, 8),), -0.2, 0.2)), 2293.76, 9175.04),
        "up_cols": jnp.clip(jnp.exp(math.log(9175.04) - 1.3862944 * jax.random.uniform(seeds[15], (FF,), jnp.float32) ** block_levels(seeds[15], (FF,), ((0, 4),), -0.2, 0.2)), 2293.76, 9175.04),
        "down_rows": jnp.clip(jnp.exp(math.log(32768.0) - 1.3862944 * jax.random.uniform(seeds[16], (FF,), jnp.float32) ** block_levels(seeds[16], (FF,), ((0, 4),), -0.2, 0.2)), 8192.0, 32768.0),
        "down_cols": jnp.clip(jnp.exp(math.log(32768.0) - 1.3862944 * jax.random.uniform(seeds[17], (D,), jnp.float32) ** block_levels(seeds[17], (D,), ((0, 8),), -0.2, 0.2)), 8192.0, 32768.0),
        "router_moment": jnp.clip(jnp.exp(math.log(5242880) - 1.3862944 * jax.random.uniform(seeds[18], (D,), jnp.float32) ** block_levels(seeds[18], (D,), ((0, 8),), -0.2, 0.2)), 1310720, 5242880),
        "gains_moment": jnp.clip(jnp.exp(math.log(9830.4) - 1.3862944 * jax.random.uniform(seeds[19], (2, D), jnp.float32) ** block_levels(seeds[19], (2, D), ((1, 8),), -0.2, 0.2)), 2457.6, 9830.4),
    }


EPS_NORM = 1e-06
EPS_SQUARE = 1e-30
DECAY = 0.5
CLIP_RMS = 0.3
RATE = 1.0
MASKED = -1e+30

@jax.custom_vjp
def low(v):
    return lax.optimization_barrier(v.astype(jnp.bfloat16)).astype(jnp.float32)

@jax.custom_vjp
def low_back(v):
    return v

def low_keep(v):
    return (low(v), None)

def low_pass(kept, grad):
    return (grad,)

def back_keep(v):
    return (v, None)

def back_low(kept, grad):
    return (low(grad),)
low.defvjp(low_keep, low_pass)
low_back.defvjp(back_keep, back_low)

def rounded(values):
    return low_back(low(values))

def rms_norm(values, gain_vec):
    return values * lax.rsqrt(lax.optimization_barrier(jnp.mean(values * values, axis=-1, keepdims=True)) + EPS_NORM) * gain_vec

def block_forward(params, selected, allowed):
    qkv_float, out_float, up_float, down_float, router_float, gains_float = params
    highest = lax.Precision.HIGHEST
    row_count, pick_count, width_full = selected.shape
    router_gate = jax.nn.sigmoid(jnp.einsum('rkd,d->rk', selected, router_float, precision=highest))
    normed = low(rms_norm(selected, gains_float[0]))
    projected = rounded(jnp.einsum('rkd,cde->crke', normed, qkv_float, precision=highest))
    shaped = projected.reshape(3, row_count, pick_count, HEADS, HEAD_DIM)
    scores = low_back(jnp.einsum('rqhe,rkhe->rhqk', shaped[0], shaped[1], precision=highest) * HEAD_DIM ** (-0.5))
    masked = jnp.where(allowed, scores, MASKED)
    highest_score = lax.optimization_barrier(jnp.max(masked, axis=-1, keepdims=True))
    exponent = jnp.exp(masked - highest_score)
    attention = exponent / lax.optimization_barrier(jnp.sum(exponent, axis=-1, keepdims=True))
    attended = jnp.einsum('rhqk,rkhe->rqhe', low(attention), shaped[2], precision=highest)
    attended = rounded(attended.reshape(row_count, pick_count, HEADS * HEAD_DIM))
    branch_attn = low_back(jnp.einsum('rke,ed->rkd', attended, out_float, precision=highest))
    middle = selected + branch_attn
    normed_mid = low(rms_norm(middle, gains_float[1]))
    hidden = low_back(jnp.einsum('rkd,df->rkf', normed_mid, up_float, precision=highest))
    active = low(jax.nn.gelu(hidden))
    branch_mlp = low_back(jnp.einsum('rkf,fd->rkd', active, down_float, precision=highest))
    return selected + router_gate[..., None] * (branch_attn + branch_mlp)

def finish(direction, weight):
    update_norm = jnp.sqrt(jnp.mean(direction * direction))
    weight_norm = jnp.sqrt(jnp.mean(weight * weight))
    return (weight - RATE * weight_norm * direction / jnp.maximum(1.0, update_norm / CLIP_RMS), update_norm)

def factored(gradient, row_old, col_old, weight):
    square = gradient * gradient + EPS_SQUARE
    row_new = DECAY * row_old + (1.0 - DECAY) * lax.optimization_barrier(jnp.mean(square, axis=1))
    col_new = DECAY * col_old + (1.0 - DECAY) * lax.optimization_barrier(jnp.mean(square, axis=0))
    second = row_new[:, None] * col_new[None, :] / jnp.mean(row_new)
    direction = gradient * lax.rsqrt(second)
    new_weight, update_norm = finish(direction, weight)
    return (row_new, col_new, new_weight, update_norm)

def unfactored(gradient, moment, weight):
    moment_new = DECAY * moment + (1.0 - DECAY) * (gradient * gradient + EPS_SQUARE)
    direction = gradient * lax.rsqrt(moment_new)
    new_weight, update_norm = finish(direction, weight)
    return (moment_new, new_weight, update_norm)

def place_rows(target, chosen, values):
    return target.at[chosen].set(values)

def reference(tokens, segments, selection, cotangent, qkv_weight, out_weight, up_weight, down_weight, router_weight, norm_gains, qkv_rows, qkv_cols, out_rows, out_cols, up_rows, up_cols, down_rows, down_cols, router_moment, gains_moment):
    params = tuple((member.astype(jnp.float32) for member in (qkv_weight, out_weight, up_weight, down_weight, router_weight, norm_gains)))
    groups = ROWS // ROWS_DEV

    def regroup(array_in):
        return array_in.reshape((groups, ROWS_DEV) + array_in.shape[1:])

    def one_group(totals, batch_in):
        token_rows, segment_rows, chosen, cot_rows = batch_in
        selected = jnp.take_along_axis(token_rows, chosen[:, :, None], axis=1).astype(jnp.float32)
        picked_segments = jnp.take_along_axis(segment_rows, chosen, axis=1)
        allowed = (chosen[:, None, None, :] <= chosen[:, None, :, None]) & (picked_segments[:, None, None, :] == picked_segments[:, None, :, None])
        result, pullback = jax.vjp(lambda weights, inputs: block_forward(weights, inputs, allowed), params, selected)
        cot_selected = jnp.take_along_axis(cot_rows, chosen[:, :, None], axis=1).astype(jnp.float32)
        weight_grads, input_grads = pullback(cot_selected)
        outputs = jax.vmap(place_rows)(token_rows, chosen, result.astype(jnp.bfloat16))
        grad_rows = jax.vmap(place_rows)(cot_rows.astype(jnp.float32), chosen, input_grads)
        return (jax.tree.map(jnp.add, totals, weight_grads), (outputs, grad_rows))
    start = tuple((jnp.zeros_like(member) for member in params))
    totals, (outputs, grad_rows) = lax.scan(one_group, start, (regroup(tokens), regroup(segments), regroup(selection), regroup(cotangent)))
    block_output = outputs.reshape(tokens.shape)
    input_grad = grad_rows.reshape(tokens.shape)
    qkv_grad, out_grad, up_grad, down_grad, router_grad, gains_grad = totals
    qkv_float, out_float, up_float, down_float, router_float, gains_float = params
    qkv_pieces = [factored(qkv_grad[channel], qkv_rows[channel], qkv_cols[channel], qkv_float[channel]) for channel in range(3)]
    out_rows_new, out_cols_new, out_new, out_norm = factored(out_grad, out_rows, out_cols, out_float)
    up_rows_new, up_cols_new, up_new, up_norm = factored(up_grad, up_rows, up_cols, up_float)
    down_rows_new, down_cols_new, down_new, down_norm = factored(down_grad, down_rows, down_cols, down_float)
    router_moment_new, router_new, router_norm = unfactored(router_grad, router_moment, router_float)
    gain_pieces = [unfactored(gains_grad[channel], gains_moment[channel], gains_float[channel]) for channel in range(2)]
    update_rms = jnp.stack([pieces[3] for pieces in qkv_pieces] + [out_norm, up_norm, down_norm, router_norm] + [pieces[2] for pieces in gain_pieces])
    return (block_output, input_grad, qkv_grad, jnp.stack([pieces[0] for pieces in qkv_pieces]), jnp.stack([pieces[1] for pieces in qkv_pieces]), jnp.stack([pieces[2] for pieces in qkv_pieces]), out_grad, out_rows_new, out_cols_new, out_new, up_grad, up_rows_new, up_cols_new, up_new, down_grad, down_rows_new, down_cols_new, down_new, router_grad, router_moment_new, router_new, gains_grad, jnp.stack([pieces[0] for pieces in gain_pieces]), jnp.stack([pieces[1] for pieces in gain_pieces]), update_rms)
```

```python
import functools

import jax
import jax.numpy as jnp
from jax import lax
from jax.experimental import pallas as pl
from jax.experimental.pallas import tpu as pltpu
from jax.sharding import PartitionSpec as P


D = 768
HEAD_DIM = 64
FF = 3072
MICRO = 2


EPS_NORM = 1e-06
EPS_SQUARE = 1e-30
DECAY = 0.5
CLIP_RMS = 0.3
RATE = 1.0
MASKED = -1e30


def rms_parts(values):
    inverse = lax.rsqrt(jnp.mean(values * values, axis=1, keepdims=True) + EPS_NORM)
    return (values * inverse, inverse)


def norm_back(grad_norm, gain_vec, scaled, inverse):
    grad_scaled = grad_norm * gain_vec
    grad_input = inverse * (
        grad_scaled - scaled * jnp.mean(grad_scaled * scaled, axis=1, keepdims=True)
    )
    return (grad_input, jnp.sum(grad_norm * scaled, axis=0))


def spread_into(values, index, pieces):
    size_piece = values.shape[-1]
    shape_full = values.shape[:-1] + (size_piece * pieces,)
    return lax.dynamic_update_slice_in_dim(
        jnp.zeros(shape_full, jnp.float32), values, index * size_piece, values.ndim - 1
    )


def own_piece(values, index, size_piece):
    return lax.dynamic_slice_in_dim(values, index * size_piece, size_piece, values.ndim - 1)


def factor_terms(gradient, row_old, col_old, row_index, row_count, col_index, col_count):
    square = gradient * gradient + EPS_SQUARE
    rows_here, cols_here = gradient.shape[-2:]
    row_term = (1.0 - DECAY) * jnp.sum(square, axis=-1) / (
        cols_here * col_count
    ) + DECAY * row_old * (col_index == 0)
    col_term = (1.0 - DECAY) * jnp.sum(square, axis=-2) / (
        rows_here * row_count
    ) + DECAY * col_old * (row_index == 0)
    return (
        spread_into(row_term, row_index, row_count),
        spread_into(col_term, col_index, col_count),
    )


def factor_direction(gradient, row_full, col_full, row_index, col_index):
    rows_here, cols_here = gradient.shape[-2:]
    row_mine = own_piece(row_full, row_index, rows_here)
    col_mine = own_piece(col_full, col_index, cols_here)
    mean_row = jnp.mean(row_full, axis=-1)[..., None, None]
    second = row_mine[..., :, None] * col_mine[..., None, :] / mean_row
    return (gradient * lax.rsqrt(second), row_mine, col_mine)


def local_any(
    tokens,
    segments,
    selection,
    cotangent,
    qkv_weight,
    out_weight,
    up_weight,
    down_weight,
    router_weight,
    norm_gains,
    qkv_rows,
    qkv_cols,
    out_rows,
    out_cols,
    up_rows,
    up_cols,
    down_rows,
    down_cols,
    router_moment,
    gains_moment,
):
    qkv_all, out_all, up_all, down_all, router_all, gains_all = (
        lax.all_gather(qkv_weight, "batch", axis=1, tiled=True),
        lax.all_gather(out_weight, "batch", axis=1, tiled=True),
        lax.all_gather(up_weight, "batch", axis=0, tiled=True),
        lax.all_gather(down_weight, "batch", axis=1, tiled=True),
        lax.all_gather(router_weight, "batch", axis=0, tiled=True),
        lax.all_gather(norm_gains, "batch", axis=1, tiled=True),
    )
    mp_index = lax.axis_index("mp")
    mp_count = lax.axis_size("mp")
    batch_index = lax.axis_index("batch")
    batch_count = lax.axis_size("batch")
    rows_dev, length_here, width_full = tokens.shape
    width_local = width_full // mp_count
    heads_local = qkv_all.shape[2] // HEAD_DIM
    per_micro = rows_dev // MICRO
    score_scale = HEAD_DIM ** (-0.5)
    gain_attn = gains_all[0].astype(jnp.float32)
    gain_mlp = gains_all[1].astype(jnp.float32)
    router_float = router_all.astype(jnp.float32)
    first_position = mp_index * length_here
    totals = None
    shards = None
    output_list = []
    grad_list = []
    for micro_index in range(MICRO):
        row_start = micro_index * per_micro
        row_stop = row_start + per_micro
        token_rows = tokens[row_start:row_stop]
        chosen = selection[row_start:row_stop]
        cot_rows = cotangent[row_start:row_stop]
        row_count, pick_count = chosen.shape
        token_count = row_count * pick_count
        local_position = chosen - first_position
        inside = (local_position >= 0) & (local_position < length_here)
        clipped = jnp.clip(local_position, 0, length_here - 1)
        zero_low = jnp.zeros((), jnp.bfloat16)
        token_term = jnp.where(
            inside[:, :, None],
            jnp.take_along_axis(token_rows, clipped[:, :, None], axis=1),
            zero_low,
        ).reshape(token_count, width_full)
        cot_term = jnp.where(
            inside[:, :, None], jnp.take_along_axis(cot_rows, clipped[:, :, None], axis=1), zero_low
        ).reshape(token_count, width_full)
        picked_float = lax.psum(token_term, "mp").astype(jnp.float32)
        cot_float = lax.psum(cot_term, "mp").astype(jnp.float32)
        picked_full = picked_float.astype(jnp.bfloat16)
        picked_local = lax.dynamic_slice_in_dim(picked_full, mp_index * width_local, width_local, 1)
        cot_local = lax.dynamic_slice_in_dim(cot_float, mp_index * width_local, width_local, 1)
        picked_segments = jnp.take_along_axis(segments[row_start:row_stop], chosen, axis=1)
        allowed = (chosen[:, None, None, :] <= chosen[:, None, :, None]) & (
            picked_segments[:, None, None, :] == picked_segments[:, None, :, None]
        )
        router_gate = jax.nn.sigmoid(
            jnp.dot(picked_full, router_all, preferred_element_type=jnp.float32)
        )
        scaled_attn, inverse_attn = rms_parts(picked_float)
        normed = (scaled_attn * gain_attn).astype(jnp.bfloat16)
        projected = jnp.einsum(
            "td,cde->cte", normed, qkv_all, preferred_element_type=jnp.float32
        ).astype(jnp.bfloat16)
        shaped = projected.reshape(3, row_count, pick_count, heads_local, HEAD_DIM)
        queries = shaped[0]
        key_rows = shaped[1]
        value_rows = shaped[2]
        scores = (
            jnp.einsum("rqhe,rkhe->rhqk", queries, key_rows, preferred_element_type=jnp.float32)
            * score_scale
        )
        masked = jnp.where(allowed, scores, MASKED)
        highest_score = jnp.max(masked, axis=-1, keepdims=True)
        exponent = jnp.exp(masked - highest_score)
        exp_total = jnp.sum(exponent, axis=-1, keepdims=True)
        log_total = highest_score + jnp.log(exp_total)
        attention_low = (exponent / exp_total).astype(jnp.bfloat16)
        attended = jnp.einsum(
            "rhqk,rkhe->rqhe", attention_low, value_rows, preferred_element_type=jnp.float32
        )
        attended = attended.reshape(token_count, heads_local * HEAD_DIM).astype(jnp.bfloat16)
        attn_local = lax.psum_scatter(
            jnp.dot(attended, out_all, preferred_element_type=jnp.float32),
            "mp",
            scatter_dimension=1,
            tiled=True,
        )
        middle_local = picked_local.astype(jnp.float32) + attn_local
        middle = lax.all_gather(middle_local, "mp", axis=1, tiled=True)
        scaled_mlp, inverse_mlp = rms_parts(middle)
        normed_mid = (scaled_mlp * gain_mlp).astype(jnp.bfloat16)
        hidden = jnp.dot(normed_mid, up_all, preferred_element_type=jnp.float32)
        active = jax.nn.gelu(hidden).astype(jnp.bfloat16)
        mlp_local = lax.psum_scatter(
            jnp.dot(active, down_all, preferred_element_type=jnp.float32).astype(jnp.bfloat16),
            "mp",
            scatter_dimension=1,
            tiled=True,
        ).astype(jnp.float32)
        branch_local = attn_local + mlp_local
        output_local = (
            picked_local.astype(jnp.float32) + router_gate[:, None] * branch_local
        ).astype(jnp.bfloat16)
        output_full = lax.all_gather(output_local, "mp", axis=1, tiled=True)
        grad_gate = lax.psum(jnp.sum(cot_local * branch_local, axis=1), "mp")
        direct = router_gate[:, None] * cot_float
        grad_mlp = direct.astype(jnp.bfloat16)
        down_part = jnp.einsum("tf,td->fd", active, grad_mlp, preferred_element_type=jnp.float32)
        grad_active = jnp.einsum(
            "td,fd->tf", grad_mlp, down_all, preferred_element_type=jnp.float32
        )
        gelu_values, gelu_pull = jax.vjp(jax.nn.gelu, hidden)
        grad_hidden = gelu_pull(grad_active)[0].astype(jnp.bfloat16)
        up_part = jnp.einsum(
            "td,tf->df", normed_mid, grad_hidden, preferred_element_type=jnp.float32
        )
        grad_normed_mid = lax.psum(
            jnp.einsum("tf,df->td", grad_hidden, up_all, preferred_element_type=jnp.float32), "mp"
        )
        grad_middle, gain_mlp_part = norm_back(grad_normed_mid, gain_mlp, scaled_mlp, inverse_mlp)
        grad_attn = (grad_middle + direct).astype(jnp.bfloat16)
        out_part = jnp.einsum("te,td->ed", attended, grad_attn, preferred_element_type=jnp.float32)
        grad_attended = jnp.einsum(
            "td,ed->te", grad_attn, out_all, preferred_element_type=jnp.float32
        ).astype(jnp.bfloat16)
        grad_attended = grad_attended.reshape(row_count, pick_count, heads_local, HEAD_DIM)
        scores_again = (
            jnp.einsum("rqhe,rkhe->rhqk", queries, key_rows, preferred_element_type=jnp.float32)
            * score_scale
        )
        attention = jnp.exp(jnp.where(allowed, scores_again, MASKED) - log_total)
        grad_values = jnp.einsum(
            "rhqk,rqhe->rkhe",
            attention.astype(jnp.bfloat16),
            grad_attended,
            preferred_element_type=jnp.float32,
        )
        grad_weights = jnp.einsum(
            "rqhe,rkhe->rhqk", grad_attended, value_rows, preferred_element_type=jnp.float32
        )
        grad_scores = (
            attention * (grad_weights - jnp.sum(attention * grad_weights, axis=-1, keepdims=True))
        ).astype(jnp.bfloat16)
        grad_queries = (
            jnp.einsum("rhqk,rkhe->rqhe", grad_scores, key_rows, preferred_element_type=jnp.float32)
            * score_scale
        )
        grad_keys = (
            jnp.einsum("rhqk,rqhe->rkhe", grad_scores, queries, preferred_element_type=jnp.float32)
            * score_scale
        )
        grad_projected = (
            jnp.stack([grad_queries, grad_keys, grad_values])
            .reshape(3, token_count, heads_local * HEAD_DIM)
            .astype(jnp.bfloat16)
        )
        qkv_part = jnp.einsum(
            "td,cte->cde", normed, grad_projected, preferred_element_type=jnp.float32
        )
        grad_normed = lax.psum(
            jnp.einsum(
                "cte,cde->td", grad_projected, qkv_all, preferred_element_type=jnp.float32
            ).astype(jnp.bfloat16),
            "mp",
        ).astype(jnp.float32)
        grad_norm_in, gain_attn_part = norm_back(grad_normed, gain_attn, scaled_attn, inverse_attn)
        grad_logit = grad_gate * router_gate * (1.0 - router_gate)
        router_part = jnp.dot(grad_logit, picked_float, precision=lax.Precision.HIGHEST)
        grad_full = cot_float + grad_middle + grad_norm_in + grad_logit[:, None] * router_float
        row_positions = jnp.arange(row_count)[:, None]
        write_index = jnp.where(inside, local_position, length_here)
        output_rows = token_rows.at[row_positions, write_index].set(
            output_full.reshape(row_count, pick_count, width_full), mode="drop"
        )
        grad_rows = (
            cot_rows.astype(jnp.float32)
            .at[row_positions, write_index]
            .set(grad_full.reshape(row_count, pick_count, width_full), mode="drop")
        )
        gradients = (
            qkv_part,
            out_part,
            up_part,
            down_part,
            router_part,
            jnp.stack([gain_attn_part, gain_mlp_part]),
        )
        gradients, output_rows, grad_rows = (gradients, output_rows, grad_rows)
        output_list.append(output_rows)
        grad_list.append(grad_rows)
        totals = gradients if totals is None else jax.tree.map(jnp.add, totals, gradients)
    shards = (
        lax.psum_scatter(totals[0], "batch", scatter_dimension=1, tiled=True),
        lax.psum_scatter(totals[1], "batch", scatter_dimension=1, tiled=True),
        lax.psum_scatter(totals[2], "batch", scatter_dimension=0, tiled=True),
        lax.psum_scatter(totals[3], "batch", scatter_dimension=1, tiled=True),
        lax.psum_scatter(totals[4], "batch", scatter_dimension=0, tiled=True),
        lax.psum_scatter(totals[5], "batch", scatter_dimension=1, tiled=True),
    )
    block_output = jnp.concatenate(output_list, axis=0)
    input_grad = jnp.concatenate(grad_list, axis=0)
    qkv_grad, out_grad, up_grad, down_grad, router_grad, gains_grad = shards
    first_mp = (mp_index == 0).astype(jnp.float32)
    qkv_old = qkv_weight.astype(jnp.float32)
    out_old = out_weight.astype(jnp.float32)
    up_old = up_weight.astype(jnp.float32)
    down_old = down_weight.astype(jnp.float32)
    router_old = router_weight.astype(jnp.float32)
    gains_old = norm_gains.astype(jnp.float32)
    qkv_row_term, qkv_col_term = factor_terms(
        qkv_grad, qkv_rows, qkv_cols, batch_index, batch_count, mp_index, mp_count
    )
    out_row_term, out_col_term = factor_terms(
        out_grad, out_rows, out_cols, mp_index, mp_count, batch_index, batch_count
    )
    up_row_term, up_col_term = factor_terms(
        up_grad, up_rows, up_cols, batch_index, batch_count, mp_index, mp_count
    )
    down_row_term, down_col_term = factor_terms(
        down_grad, down_rows, down_cols, mp_index, mp_count, batch_index, batch_count
    )
    weight_squares = jnp.concatenate(
        [
            jnp.sum(qkv_old * qkv_old, axis=(1, 2)),
            jnp.stack(
                [
                    jnp.sum(out_old * out_old),
                    jnp.sum(up_old * up_old),
                    jnp.sum(down_old * down_old),
                    first_mp * jnp.sum(router_old * router_old),
                ]
            ),
            first_mp * jnp.sum(gains_old * gains_old, axis=1),
        ]
    )
    (
        qkv_row_full,
        qkv_col_full,
        out_row_full,
        out_col_full,
        up_row_full,
        up_col_full,
        down_row_full,
        down_col_full,
        weight_sums,
    ) = lax.psum(
        (
            qkv_row_term,
            qkv_col_term,
            out_row_term,
            out_col_term,
            up_row_term,
            up_col_term,
            down_row_term,
            down_col_term,
            weight_squares,
        ),
        ("batch", "mp"),
    )
    qkv_dir, qkv_rows_new, qkv_cols_new = factor_direction(
        qkv_grad, qkv_row_full, qkv_col_full, batch_index, mp_index
    )
    out_dir, out_rows_new, out_cols_new = factor_direction(
        out_grad, out_row_full, out_col_full, mp_index, batch_index
    )
    up_dir, up_rows_new, up_cols_new = factor_direction(
        up_grad, up_row_full, up_col_full, batch_index, mp_index
    )
    down_dir, down_rows_new, down_cols_new = factor_direction(
        down_grad, down_row_full, down_col_full, mp_index, batch_index
    )
    router_moment_new = DECAY * router_moment + (1.0 - DECAY) * (
        router_grad * router_grad + EPS_SQUARE
    )
    router_dir = router_grad * lax.rsqrt(router_moment_new)
    gains_moment_new = DECAY * gains_moment + (1.0 - DECAY) * (gains_grad * gains_grad + EPS_SQUARE)
    gains_dir = gains_grad * lax.rsqrt(gains_moment_new)
    update_squares = jnp.concatenate(
        [
            jnp.sum(qkv_dir * qkv_dir, axis=(1, 2)),
            jnp.stack(
                [
                    jnp.sum(out_dir * out_dir),
                    jnp.sum(up_dir * up_dir),
                    jnp.sum(down_dir * down_dir),
                    first_mp * jnp.sum(router_dir * router_dir),
                ]
            ),
            first_mp * jnp.sum(gains_dir * gains_dir, axis=1),
        ]
    )
    update_sums = lax.psum(update_squares, ("batch", "mp"))
    entries = jnp.array([D * D, D * D, D * D, D * D, D * FF, FF * D, D, D, D], jnp.float32)
    update_rms = jnp.sqrt(update_sums / entries)
    weight_rms = jnp.sqrt(weight_sums / entries)
    factors = RATE * weight_rms / jnp.maximum(1.0, update_rms / CLIP_RMS)
    qkv_new = qkv_old - factors[0:3, None, None] * qkv_dir
    out_new = out_old - factors[3] * out_dir
    up_new = up_old - factors[4] * up_dir
    down_new = down_old - factors[5] * down_dir
    router_new = router_old - factors[6] * router_dir
    gains_new = gains_old - factors[7:9, None] * gains_dir
    return (
        block_output,
        input_grad,
        qkv_grad,
        qkv_rows_new,
        qkv_cols_new,
        qkv_new,
        out_grad,
        out_rows_new,
        out_cols_new,
        out_new,
        up_grad,
        up_rows_new,
        up_cols_new,
        up_new,
        down_grad,
        down_rows_new,
        down_cols_new,
        down_new,
        router_grad,
        router_moment_new,
        router_new,
        gains_grad,
        gains_moment_new,
        gains_new,
        update_rms,
    )


MESH=pl.DeviceIdType.MESH
BF=jnp.bfloat16; F32=jnp.float32

class Plane:
    def __init__(s):
        s.b=lax.axis_index("batch"); s.m=lax.axis_index("mp")
        s.z=s.b//2; s.y=lax.rem(s.b,2); s.x=s.m//2; s.c=lax.rem(s.m,2)
        s.left=(s.b-2,s.m); s.right=(s.b+2,s.m)
        s.ypeer=(s.z*2+1-s.y,s.m); s.xpeer=(s.b,(1-s.x)*2+s.c); s.core=(s.b,s.x*2+1-s.c)

def greet(peers):
    bar=pltpu.get_barrier_semaphore()
    for d in peers: pl.semaphore_signal(bar,inc=1,device_id=d,device_id_type=MESH)
    pl.semaphore_wait(bar,len(peers))

def gather_kernel(nz, rp, length_here, picks, w_ref, v_ref, tok_ref, cot_ref, sel_ref, W_ref, out_ref, vall_ref,
                  tokb, cotb, zbuf, ra, rb, rx, locsem, tsem, csem, rsem, ssem, xs, xr, vs, vr):
    p=Plane()
    nb=2*nz
    bpeers=[(lax.rem(p.b+k,nb),p.m) for k in range(1,nb)]
    greet(bpeers+[p.xpeer,p.core])
    def at(i,m,b): return W_ref.at[i,m,pl.ds(pl.multiple_of(b*rp,rp),rp)]
    groups=[((1-p.x)*2+1-p.c),((1-p.x)*2+p.c),(p.x*2+1-p.c),p.m]
    cps=[]
    own=[pltpu.make_async_copy(w_ref.at[i],at(i,p.m,p.b),locsem.at[i]) for i in range(3)]
    sends=[]
    def send(i,m,b,d,slot,src=None):
        cp=pltpu.make_async_remote_copy(src_ref=at(i,m,b) if src is None else src,dst_ref=at(i,m,b),
            send_sem=ssem.at[i,slot],recv_sem=rsem.at[i,m,b],device_id=d,device_id_type=MESH)
        cp.start()
        return cp
    def arrived(i,m,b):
        pltpu.make_async_remote_copy(src_ref=at(i,m,b),dst_ref=at(i,m,b),send_sem=ssem.at[i,0],recv_sem=rsem.at[i,m,b],
            device_id=p.core,device_id_type=MESH).wait_recv()
    class Ctr:
        def __init__(s): s.n={}
    ctr=[0,0,0]
    pend=[]
    def fwd(i,m,b,d,cond=None,src=None):
        slot=ctr[i]; ctr[i]+=1
        if cond is None:
            pend.append((None,send(i,m,b,d,slot,src)))
        else:
            @pl.when(cond)
            def _(): send(i,m,b,d,slot,src)
            pend.append((cond,(i,m,b,d,slot,src)))
    def done():
        for cond,x in pend:
            if cond is None: x.wait_send()
            else:
                i,m,b,d,slot,src=x
                @pl.when(cond)
                def _():
                    pltpu.make_async_remote_copy(src_ref=at(i,m,b) if src is None else src,dst_ref=at(i,m,b),
                        send_sem=ssem.at[i,slot],recv_sem=rsem.at[i,m,b],device_id=d,device_id_type=MESH).wait_send()
    mx=(1-p.x)*2+p.c
    mc=p.x*2+1-p.c
    yb=p.z*2+1-p.y
    def zpass(i,shards,t,extra):
        for (m,y) in shards:
            zl=p.z-1-t
            @pl.when(zl>=0)
            def _(): arrived(i,m,zl*2+y)
            fwd(i,m,zl*2+y,p.right,(zl>=0)&(p.z<nz-1))
            for d in extra: fwd(i,m,zl*2+y,d,zl>=0)
            zr=p.z+1+t
            @pl.when(zr<nz)
            def _(): arrived(i,m,zr*2+y)
            fwd(i,m,zr*2+y,p.left,(zr<nz)&(p.z>0))
            for d in extra: fwd(i,m,zr*2+y,d,zr<nz)
    for i in range(3): own[i].start()
    vall_ref[p.b]=v_ref[...]
    vcs=[pltpu.make_async_remote_copy(src_ref=v_ref,dst_ref=vall_ref.at[p.b],send_sem=vs.at[k],recv_sem=vr.at[k],device_id=d,device_id_type=MESH) for k,d in enumerate(bpeers)]
    for cp in vcs: cp.start()
    for i in (0,2,1):
        src=w_ref.at[i]
        if i!=LAST:
            fwd(i,p.m,p.b,p.right,p.z<nz-1,src); fwd(i,p.m,p.b,p.left,p.z>0,src)
            fwd(i,p.m,p.b,p.xpeer,None,src); fwd(i,p.m,p.b,p.ypeer,None,src)
        else:
            fwd(i,p.m,p.b,p.xpeer,None,src); fwd(i,p.m,p.b,p.ypeer,None,src)
            fwd(i,p.m,p.b,p.right,p.z<nz-1,src); fwd(i,p.m,p.b,p.left,p.z>0,src)
        fwd(i,p.m,p.b,p.core,None,src)
    for g in groups:
        for k in range(2):
            r=g*2+k
            a=pltpu.make_async_copy(tok_ref.at[r],tokb.at[r],tsem.at[r]); a.start()
            a=pltpu.make_async_copy(cot_ref.at[r],cotb.at[r],csem.at[r]); a.start()
    def pick(g,slot):
        for k in range(2):
            r=g*2+k
            pltpu.make_async_copy(tok_ref.at[r],tokb.at[r],tsem.at[r]).wait()
            pltpu.make_async_copy(cot_ref.at[r],cotb.at[r],csem.at[r]).wait()
            col=sel_ref[r]-p.m*length_here
            hot=(col==lax.broadcasted_iota(jnp.int32,(picks,length_here),1)).astype(F32).astype(BF)
            zbuf[slot,k*picks:(k+1)*picks,0:768]=jnp.dot(hot,tokb[r],preferred_element_type=F32).astype(BF)
            zbuf[slot,k*picks:(k+1)*picks,768:1536]=jnp.dot(hot,cotb[r],preferred_element_type=F32).astype(BF)
    def ship(slot,dst,n,d):
        return pltpu.make_async_remote_copy(src_ref=zbuf.at[slot],dst_ref=dst,send_sem=xs.at[n],recv_sem=xr.at[n],device_id=d,device_id_type=MESH)
    pick(groups[0],0)
    cb=ship(0,rb,0,p.core); cb.start()
    zx=[i for i in range(3) if i!=LAST]
    i=LAST
    arrived(i,mx,p.b); fwd(i,mx,p.b,p.ypeer); fwd(i,mx,p.b,p.right,p.z<nz-1); fwd(i,mx,p.b,p.left,p.z>0); fwd(i,mx,p.b,p.core)
    for i in zx: zpass(i,[(p.m,p.y)],0,[p.xpeer,p.ypeer,p.core])
    pick(groups[1],1)
    cb.wait_recv()
    zbuf[1]=zbuf[1]+rb[...]
    cx=ship(1,rx,1,p.xpeer); cx.start()
    i=LAST
    arrived(i,p.m,yb); fwd(i,p.m,yb,p.right,p.z<nz-1); fwd(i,p.m,yb,p.left,p.z>0); fwd(i,p.m,yb,p.core)
    arrived(i,mx,yb); fwd(i,mx,yb,p.right,p.z<nz-1); fwd(i,mx,yb,p.left,p.z>0); fwd(i,mx,yb,p.core)
    pick(groups[2],2)
    ca=ship(2,ra,2,p.core); ca.start()
    for i in zx: zpass(i,[(p.m,p.y)],1,[p.xpeer,p.ypeer,p.core])
    pick(groups[3],3)
    zpass(LAST,[(p.m,p.y),(mx,p.y)],0,[p.core])
    for i in zx:
        arrived(i,mx,p.b); fwd(i,mx,p.b,p.ypeer); fwd(i,mx,p.b,p.core)
    zpass(LAST,[(p.m,1-p.y),(mx,1-p.y)],0,[p.core])
    for i in zx: zpass(i,[(p.m,p.y)],2,[p.xpeer,p.ypeer,p.core])
    allsh=[(p.m,p.y),(mx,p.y),(p.m,1-p.y),(mx,1-p.y)]
    def xarr(i,t):
        zl=p.z-1-t
        @pl.when(zl>=0)
        def _(): arrived(i,mx,zl*2+p.y)
        fwd(i,mx,zl*2+p.y,p.ypeer,zl>=0); fwd(i,mx,zl*2+p.y,p.core,zl>=0)
        zr=p.z+1+t
        @pl.when(zr<nz)
        def _(): arrived(i,mx,zr*2+p.y)
        fwd(i,mx,zr*2+p.y,p.ypeer,zr<nz); fwd(i,mx,zr*2+p.y,p.core,zr<nz)
    zpass(LAST,allsh,1,[p.core])
    for i in zx:
        arrived(i,p.m,yb); fwd(i,p.m,yb,p.core)
        xarr(i,0)
    for i in zx: xarr(i,1)
    zpass(LAST,allsh,2,[p.core])
    for i in zx: xarr(i,2)
    for z in range(nz):
        for i in zx:
            for m in (p.m,mx):
                if m is p.m:
                    cond=p.z!=z
                    @pl.when(cond)
                    def _(): arrived(i,m,z*2+1-p.y)
                    fwd(i,m,z*2+1-p.y,p.core,cond)
                else:
                    arrived(i,m,z*2+1-p.y); fwd(i,m,z*2+1-p.y,p.core)
    ca.wait_recv(); cx.wait_recv()
    zbuf[3]=zbuf[3]+ra[...]+rx[...]
    fin=pltpu.make_async_copy(zbuf.at[3],out_ref,locsem.at[3]); fin.start()
    for i in range(3):
        for m in (mc,(1-p.x)*2+1-p.c):
            for b in range(2*nz): arrived(i,m,b)
    fin.wait()
    for cp in vcs: cp.wait()
    for o in own: o.wait()
    cb.wait_send(); cx.wait_send(); ca.wait_send()
    done()
LAST=0
def gather_call(wsh,vold,tokens,cot,selcol,B,picks):
    nz=B//2; rp=wsh.shape[1]
    rows,length_here,width=tokens.shape
    per=rows//4*picks
    D=pltpu.SemaphoreType.DMA
    return pl.pallas_call(functools.partial(gather_kernel,nz,rp,length_here,picks),
        out_shape=(jax.ShapeDtypeStruct((3,4,B*rp,768),BF),jax.ShapeDtypeStruct((per,2*width),BF),jax.ShapeDtypeStruct((B,8,128),F32)),
        in_specs=[pl.BlockSpec(memory_space=m) for m in (pl.ANY,pltpu.VMEM,pl.ANY,pl.ANY,pltpu.VMEM)],
        out_specs=(pl.BlockSpec(memory_space=pl.ANY),)*2+(pl.BlockSpec(memory_space=pltpu.VMEM),),
        scratch_shapes=[pltpu.VMEM((rows,length_here,width),BF),pltpu.VMEM((rows,length_here,width),BF),
            pltpu.VMEM((4,per,2*width),BF),pltpu.VMEM((per,2*width),BF),pltpu.VMEM((per,2*width),BF),pltpu.VMEM((per,2*width),BF),
            D((4,)),D((rows,)),D((rows,)),D((3,4,B)),D((3,120)),D((3,)),D((3,)),D((B,)),D((B,))],
        compiler_params=pltpu.CompilerParams(collective_id=0,has_side_effects=True,vmem_limit_bytes=56<<20),
        name="gather_all")(wsh,vold,tokens,cot,selcol)


BF=jnp.bfloat16; F32=jnp.float32
EPS_NORM=1e-6; MASKED=-1e30; HD=64
def nn(a,b): return jnp.dot(a,b,preferred_element_type=F32)
def nt(a,b): return lax.dot_general(a,b,(((1,),(1,)),((),())),preferred_element_type=F32)
def tn(a,b): return lax.dot_general(a,b,(((0,),(0,)),((),())),preferred_element_type=F32)
GC=0.7978845608028654; GA=0.044715
def block_kernel(picks, sel_ref, Wh_ref, vec_ref, seg_ref, segc_ref, Gh_ref, rows_ref, small_ref,
                 normed, P, probs, att, mid, ba, nm, act, dg, gm, gh, acc, nT, nmT, gmT, gaT, gatt, W_ref, gst, gob, wsem, gsem):
    vec=jnp.concatenate([vec_ref[b,:,0:768//vec_ref.shape[0]] for b in range(vec_ref.shape[0])],axis=1)
    router=vec[0:1,:]; gain0=vec[1:2,:]; gain1=vec[2:3,:]
    T=sel_ref.shape[0]; D=768
    def wcopy(i,m): return pltpu.make_async_copy(Wh_ref.at[i,m],W_ref.at[i,m],wsem.at[i,m])
    def gcopy(i,m,slot): return pltpu.make_async_copy(gst.at[slot],Gh_ref.at[i,m],gsem.at[slot])
    for i in range(3):
        for m in range(4): wcopy(i,m).start()
    x=sel_ref[:,0:D].astype(F32)
    gate=jax.nn.sigmoid(jnp.sum(x*router,axis=1,keepdims=True))
    inv=lax.rsqrt(jnp.mean(x*x,axis=1,keepdims=True)+EPS_NORM)
    nrm=(x*inv*gain0).astype(BF)
    normed[...]=nrm
    nT[...]=nrm.T
    gmv=(gate*sel_ref[:,D:].astype(F32)).astype(BF)
    gm[...]=gmv
    gmT[...]=gmv.T
    @pl.loop(0,4)
    def _(m):
        wcopy(0,m).wait()
        P[m]=nn(normed[...],W_ref[0,m]).astype(BF)
    scale=HD**-0.5
    qi=lax.broadcasted_iota(jnp.int32,(picks,picks),0); ki=lax.broadcasted_iota(jnp.int32,(picks,picks),1)
    def head(h): return h//3,(h%3)*HD
    @pl.loop(0,T//picks)
    def _(r):
        rs=pl.ds(pl.multiple_of(r*picks,picks),picks)
        ok=(ki<=qi)&(seg_ref[r]==segc_ref[r])
        for h2 in range(6):
            outs=[]
            for h in (2*h2,2*h2+1):
                m,o=head(h)
                q=P[m,rs,o:o+HD]; k=P[m,rs,192+o:192+o+HD]; v=P[m,rs,384+o:384+o+HD]
                s=jnp.where(ok,nt(q,k)*scale,MASKED)
                e=jnp.exp(s-jnp.max(s,axis=1,keepdims=True))
                p=(e/jnp.sum(e,axis=1,keepdims=True)).astype(BF)
                probs[r,h]=p
                outs.append(nn(p,v))
            att[rs,h2*128:(h2+1)*128]=jnp.concatenate(outs,axis=1).astype(BF)
    a=jnp.zeros((T,D),F32)
    for m in range(4):
        a=a+nt(att[:,m*192:(m+1)*192],W_ref[0,m,:,576:768])
    ba[...]=a
    mid[...]=sel_ref[:,0:D].astype(F32)+a
    mv=mid[...]
    inv2=lax.rsqrt(jnp.mean(mv*mv,axis=1,keepdims=True)+EPS_NORM)
    nmv=(mv*inv2*gain1).astype(BF)
    nm[...]=nmv
    nmT[...]=nmv.T
    acc[...]=jnp.zeros_like(acc)
    @pl.loop(0,4)
    def _(m):
        wcopy(1,m).wait()
        wcopy(2,m).wait()
        for t in range(3):
            cs=slice(t*256,(t+1)*256)
            h=nn(nm[...],W_ref[1,m,:,cs])
            th=jnp.tanh(GC*(h+GA*h*h*h))
            act[m,:,cs]=(0.5*h*(1.0+th)).astype(BF)
            dg[m,:,cs]=(0.5*(1.0+th)+0.5*h*(1.0-th*th)*(GC*(1.0+3.0*GA*h*h))).astype(BF)
        acc[...]+=nt(act[m],W_ref[2,m])
    x=sel_ref[:,0:D].astype(F32)
    dy=sel_ref[:,D:].astype(F32)
    br=ba[...]+acc[...]
    rows_ref[:,0:D]=(x+gate*br).astype(BF)
    ggate=jnp.sum(dy*br,axis=1,keepdims=True)
    glog=ggate*gate*(1.0-gate)
    acc[...]=jnp.zeros_like(acc)
    @pl.loop(0,4)
    def _(m):
        @pl.when(m>0)
        def _(): gcopy(2,m-1,0).wait()
        gst[0]=nn(gmT[...],act[m]).astype(BF)
        gcopy(2,m,0).start()
        for t in range(3):
            cs=slice(t*256,(t+1)*256)
            gh[m,:,cs]=(nn(gm[...],W_ref[2,m,:,cs])*dg[m,:,cs].astype(F32)).astype(BF)
        @pl.when(m>0)
        def _(): gcopy(1,m-1,1).wait()
        gst[1]=nn(nmT[...],gh[m]).astype(BF)
        gcopy(1,m,1).start()
        acc[...]+=nt(gh[m],W_ref[1,m])
    def back(e,gain,scaled,iv):
        eg=e*gain
        return iv*(eg-scaled*jnp.mean(eg*scaled,axis=1,keepdims=True)),jnp.sum(e*scaled,axis=0,keepdims=True)
    gmid,gain1g=back(acc[...],gain1,mid[...]*inv2,inv2)
    ga=(gmid+gate*sel_ref[:,D:].astype(F32)).astype(BF)
    mid[...]=gmid
    nm[...]=ga
    gaT[...]=ga.T
    for m in range(4):
        gatt[:,m*192:(m+1)*192]=nn(nm[...],W_ref[0,m,:,576:768]).astype(BF)
        gob[m]=nn(gaT[...],att[:,m*192:(m+1)*192]).astype(BF)
    @pl.loop(0,T//picks)
    def _(r):
        rs=pl.ds(pl.multiple_of(r*picks,picks),picks)
        for h in range(12):
            m,o=head(h)
            q=P[m,rs,o:o+HD]; k=P[m,rs,192+o:192+o+HD]; v=P[m,rs,384+o:384+o+HD]
            g=gatt[rs,h*HD:(h+1)*HD]
            p=probs[r,h]
            gv=tn(p,g)
            gp=nt(g,v)
            pf=p.astype(F32)
            ds=(pf*(gp-jnp.sum(pf*gp,axis=1,keepdims=True))).astype(BF)
            P[m,rs,o:o+HD]=(nn(ds,k)*scale).astype(BF)
            P[m,rs,192+o:192+o+HD]=(tn(ds,q)*scale).astype(BF)
            P[m,rs,384+o:384+o+HD]=gv.astype(BF)
    acc[...]=jnp.zeros_like(acc)
    @pl.loop(0,4)
    def _(m):
        slot=lax.rem(m,2)
        @pl.when(m==0)
        def _(): gcopy(2,3,0).wait()
        @pl.when(m==1)
        def _(): gcopy(1,3,1).wait()
        @pl.when(m>1)
        def _(): gcopy(0,m-2,slot).wait()
        gst[slot,:,0:576]=nn(nT[...],P[m,:,0:576]).astype(BF)
        gst[slot,:,576:768]=gob[m]
        gcopy(0,m,slot).start()
        acc[...]+=nt(P[m,:,0:576],W_ref[0,m,:,0:576])
    x=sel_ref[:,0:D].astype(F32)
    gin,gain0g=back(acc[...],gain0,x*inv,inv)
    rg=jnp.sum(glog*x,axis=0,keepdims=True)
    rows_ref[:,D:]=(sel_ref[:,D:].astype(F32)+mid[...]+gin+glog*router).astype(BF)
    gcopy(0,2,0).wait()
    gcopy(0,3,1).wait()
    small_ref[...]=jnp.concatenate([rg,gain0g,gain1g,jnp.zeros((5,D),F32)],axis=0)
def block_call(sel,W,vec,seg,picks):
    T=sel.shape[0]; D=768; R=T//picks
    V=pltpu.VMEM
    vm=pl.BlockSpec(memory_space=V); an=pl.BlockSpec(memory_space=pl.ANY)
    return pl.pallas_call(functools.partial(block_kernel,picks),
        out_shape=(jax.ShapeDtypeStruct((3,4,D,D),BF),jax.ShapeDtypeStruct((T,2*D),BF),jax.ShapeDtypeStruct((8,D),F32)),
        in_specs=[vm,an,vm,vm,vm],out_specs=(an,vm,vm),
        scratch_shapes=[V((T,D),BF),V((4,T,D),BF),V((R,12,picks,picks),BF),V((T,D),BF),V((T,D),F32),V((T,D),F32),V((T,D),BF),
            V((4,T,D),BF),V((4,T,D),BF),V((T,D),BF),V((4,T,D),BF),V((T,D),F32),V((D,T),BF),V((D,T),BF),V((D,T),BF),V((D,T),BF),V((T,D),BF),
            V((3,4,D,D),BF),V((2,D,D),BF),V((4,D,192),BF),pltpu.SemaphoreType.DMA((3,4)),pltpu.SemaphoreType.DMA((2,))],
        compiler_params=pltpu.CompilerParams(vmem_limit_bytes=60<<20),
        name="block")(sel,W,vec,seg[:,None,:],seg[:,:,None])


D=768; ZF=0
EPS_SQUARE=1e-30; CLIP=0.3
def summed_kernel(nz, rp, nb, G_ref, rows_ref, small_ref, w_ref, rold_ref, cold_ref, vold_ref, vmom_ref,
                  Gs_ref, all_ref, R_ref, C_ref, S_ref, V_ref, vdir_ref,
                  P, RC, RY, RX, RLy, RRy, RLz, RRz, Fy, Fx, vin, vmp, cin, rin, sin, smp, rloc, cloc, sloc, vsend,
                  loc, csem, crec, yS, yR, xS, xR, zS, zR, ls, lr, fS, fR, rS, rR, eS, eR):
    p=Plane()
    bar=pltpu.get_barrier_semaphore()
    bpeers=[(lax.rem(p.b+k,nb),p.m) for k in range(1,nb)]
    mpeers=[(p.b,lax.rem(p.m+k,4)) for k in range(1,4)]
    for d in bpeers+mpeers: pl.semaphore_signal(bar,inc=1,device_id=d,device_id_type=MESH)
    pl.semaphore_wait(bar,nb-1+3)
    xm=lambda xr: (p.x if xr==0 else 1-p.x)
    ym=lambda yr: (p.y if yr==0 else 1-p.y)
    YF=[i for i in range(3) if i!=ZF]
    pend=[]
    def remote(src,dst,s,r,dev):
        return pltpu.make_async_remote_copy(src_ref=src,dst_ref=dst,send_sem=s,recv_sem=r,device_id=dev,device_id_type=MESH)
    def start(cp,cond=None):
        if cond is None: cp.start()
        else:
            @pl.when(cond)
            def _(): cp.start()
        pend.append((cp,cond))
    def when(cond,f):
        if cond is None: f()
        else:
            @pl.when(cond)
            def _(): f()
    def shard(i,x,b): return P.at[i,x,pl.ds(pl.multiple_of(b*rp,rp),rp)]
    def core_desc(i,x,b):
        return remote(G_ref.at[i,x*2+1-p.c,pl.ds(pl.multiple_of(b*rp,rp),rp)],RC.at[i,x,pl.ds(pl.multiple_of(b*rp,rp),rp)],
                      csem.at[i,x,b],crec.at[i,x,b],p.core)
    def add(dst,src):
        @pl.loop(0,rp,step=32)
        def _(k):
            ks=pl.ds(pl.multiple_of(k,32),32)
            dst[ks]=(dst[ks].astype(F32)+src[ks].astype(F32)).astype(BF)
    loaded=set()
    def own(i,x,b):
        core_desc(i,x,b).wait_recv()
        add(shard(i,x,b),RC.at[i,x,pl.ds(pl.multiple_of(b*rp,rp),rp)])
    for i in (ZF,*YF):
        for x in range(2):
            pltpu.make_async_copy(G_ref.at[i,x*2+p.c],P.at[i,x],loc.at[i,x]).start()
    order=[]
    for z in range(nz):
        for xr in (1,0):
            for i in YF: order.append((i,xm(xr),z*2+ym(1)))
        zz=nz-1-z if z%2==0 else z-1
        for xr in (0,1):
            for yr in (0,1): order.append((ZF,xm(xr),z*2+ym(yr)))
    for z in range(nz):
        for i in YF:
            for xr in (1,0): order.append((i,xm(xr),z*2+ym(0)))
    for (i,x,b) in order: start(core_desc(i,x,b))
    nch=8; T=rows_ref.shape[0]; ch=T//nch
    def rowx(k): return remote(rows_ref.at[pl.ds(k*ch,ch)],all_ref.at[p.m,pl.ds(k*ch,ch)],rS.at[0,k],rR.at[0,k],(p.b,(1-p.x)*2+p.c))
    lc=pltpu.make_async_copy(rows_ref,all_ref.at[p.m],loc.at[0,2])
    lc.start()
    rowc=remote(rows_ref,all_ref.at[p.m],rS.at[1,0],rR.at[1,0],p.core)
    xmm=(1-p.x)*2+p.c
    rowf=remote(all_ref.at[xmm],all_ref.at[xmm],rS.at[1,1],rR.at[1,1],p.core)
    start(rowc)
    rk=[0]
    def rows_more(n):
        for _ in range(n):
            if rk[0]<nch: start(rowx(rk[0])); rk[0]+=1
    rows_more(3)
    for k in range(nb):
        vsend[k]=jnp.concatenate([small_ref[:,k*96:(k+1)*96],jnp.zeros((8,32),F32)],axis=1)
    vcs=[]
    for k,d in enumerate(bpeers):
        cp=remote(vsend.at[d[0]],vin.at[k],eS.at[0,k],eR.at[0,k],d); start(cp); vcs.append(cp)
    for i in (ZF,*YF):
        for x in range(2):
            pltpu.make_async_copy(G_ref.at[i,x*2+p.c],P.at[i,x],loc.at[i,x]).wait()
    def zright(i,x,y,t,ci,RL,cond=None,needown=False):
        b=t*2+y
        cp=remote(shard(i,x,b),RL.at[ci,t],zS.at[ci,0,t],zR.at[ci,0,t],p.right)
        @pl.when(p.z<t)
        def _():
            if needown: own(i,x,b)
            @pl.when(p.z>0)
            def _():
                cp.wait_recv(); add(shard(i,x,b),RL.at[ci,t])
            cp.start()
        pend.append((cp,p.z<t))
    def zleft(i,x,y,t,ci,RR,needown=False):
        b=t*2+y
        cp=remote(shard(i,x,b),RR.at[ci,t],zS.at[ci,1,t],zR.at[ci,1,t],p.left)
        @pl.when(p.z>t)
        def _():
            if needown: own(i,x,b)
            @pl.when(p.z<nz-1)
            def _():
                cp.wait_recv(); add(shard(i,x,b),RR.at[ci,t])
            cp.start()
        pend.append((cp,p.z>t))
    def zfinal(i,x,y,ci,RL,RR):
        rl=remote(shard(i,x,p.b),RL.at[ci,p.z],zS.at[ci,0,0],zR.at[ci,0,p.z],p.right)
        rr=remote(shard(i,x,p.b),RR.at[ci,p.z],zS.at[ci,1,0],zR.at[ci,1,p.z],p.left)
        @pl.when(p.z>0)
        def _(): rl.wait_recv()
        @pl.when(p.z<nz-1)
        def _(): rr.wait_recv()
        @pl.when(p.z==0)
        def _(): RL[ci,0]=jnp.zeros((rp,D),BF)
        @pl.when(p.z==nz-1)
        def _(): RR[ci,nz-1]=jnp.zeros((rp,D),BF)
    combos=[(xr,yr) for yr in (1,0) for xr in (1,0)]
    cz=lambda xr,yr: xr*2+yr
    def ysend(k,xr,z):
        i=YF[k]; b=z*2+ym(1)
        own(i,xm(xr),b)
        cp=remote(shard(i,xm(xr),b),RY.at[k,xm(xr),z],yS.at[k,xr,z],yR.at[k,xm(xr),z],p.ypeer)
        start(cp)
    def yrecv(k,xr,z):
        i=YF[k]; b=z*2+p.y
        own(i,xm(xr),b)
        remote(shard(i,xm(xr),b),RY.at[k,xm(xr),z],yS.at[k,xr,z],yR.at[k,xm(xr),z],p.ypeer).wait_recv()
        add(shard(i,xm(xr),b),RY.at[k,xm(xr),z])
    def xdesc(k,z):
        i=YF[k]
        return remote(shard(i,1-p.x,z*2+p.y),RX.at[k,z],xS.at[k,z],xR.at[k,z],p.xpeer)
    for z in range(nz):
        for (xr,yr) in combos:
            tr=nz-1-z
            if tr>0: zright(ZF,xm(xr),ym(yr),tr,cz(xr,yr),RLz,needown=True)
            if z<nz-1: zleft(ZF,xm(xr),ym(yr),z,cz(xr,yr),RRz,needown=True)
        for xr in (1,0):
            ysend(0,xr,z)
    for z in range(nz):
        for xr in (1,0): ysend(1,xr,z)
    rows_more(1)
    for z in range(nz):
        yrecv(0,1,z); start(xdesc(0,z))
    rows_more(1)
    for (xr,yr) in combos:
        own(ZF,xm(xr),p.z*2+ym(yr))
        ci=cz(xr,yr)
        zfinal(ZF,xm(xr),ym(yr),ci,RLz,RRz)
        sh=shard(ZF,xm(xr),p.z*2+ym(yr))
        add(sh,RLz.at[ci,p.z]); add(sh,RRz.at[ci,p.z])
        if yr==1:
            start(remote(sh,Fy.at[xm(xr)],fS.at[0,xr],fR.at[0,xm(xr)],p.ypeer))
    for xr in (1,0):
        sh=shard(ZF,xm(xr),p.b)
        remote(sh,Fy.at[xm(xr)],fS.at[0,xr],fR.at[0,xm(xr)],p.ypeer).wait_recv()
        add(sh,Fy.at[xm(xr)])
        if xr==1: start(remote(sh,Fx,fS.at[1,0],fR.at[1,0],p.xpeer))
    for z in range(nz): yrecv(0,0,z)
    rows_more(1)
    def line(k):
        i=YF[k]
        for t in range(nz):
            xdesc(k,t).wait_recv(); add(shard(i,p.x,t*2+p.y),RX.at[k,t])
        for z in range(nz):
            tr=nz-1-z
            if tr>0: zright(i,p.x,p.y,tr,4+k,RLy)
            if z<nz-1: zleft(i,p.x,p.y,z,4+k,RRy)
    line(0)
    rows_more(1)
    for z in range(nz):
        yrecv(1,1,z); start(xdesc(1,z))
    rows_more(8)
    for z in range(nz): yrecv(1,0,z)
    def fin(i,parts):
        Gs_ref[i]=sum([q[...].astype(F32) for q in parts[1:]],parts[0][...].astype(F32))
    remote(shard(ZF,p.x,p.b),Fx,fS.at[1,0],fR.at[1,0],p.xpeer).wait_recv()
    fin(ZF,[shard(ZF,p.x,p.b),Fx])
    zfinal(YF[0],p.x,p.y,4,RLy,RRy)
    fin(YF[0],[shard(YF[0],p.x,p.b),RLy.at[4,p.z],RRy.at[4,p.z]])
    line(1)
    for k in range(nch): rowx(k).wait_recv()
    start(rowf)
    for cp in vcs: cp.wait_recv()
    vs=vsend[p.b]
    for k in range(nb-1): vs=vs+vin[k]
    vloc=vs
    vsend[p.b]=vs
    vms=[]
    for k,d in enumerate(mpeers):
        cp=remote(vsend.at[p.b],vmp.at[k],eS.at[1,k],eR.at[1,k],d); start(cp); vms.append(cp)
    lanes=lax.broadcasted_iota(jnp.int32,(8,128),1); sub=lax.broadcasted_iota(jnp.int32,(8,128),0)
    tile=jnp.zeros((8,128),F32)
    def put(tile,lane,val): return tile+jnp.where((lanes==lane)&(sub==0),val,0.0)
    def tot(v): return jnp.sum(jnp.sum(v,axis=1,keepdims=True),axis=0,keepdims=True)
    def blocks(i): return [(j,slice(j*192,(j+1)*192)) for j in range(4)] if i==0 else [(3+i,slice(0,D))]
    for i in range(3):
        for (j,s) in blocks(i):
            wv=w_ref[i,:,s].astype(F32); tile=put(tile,12+j,tot(wv*wv))
    for j in range(3):
        wv=vold_ref[j:j+1,:]; tile=put(tile,18+j,tot(wv*wv)*0.25)
    for cp in vms: cp.wait_recv()
    for k in range(3): vs=vs+vmp[k]
    V_ref[0:8,:]=vs
    mom=0.5*vmom_ref[...]+0.5*(vs*vs+EPS_SQUARE)
    V_ref[8:16,:]=mom
    vd=jnp.where(lanes<96,vs*lax.rsqrt(mom),0.0)
    vdir_ref[...]=vd
    for j in range(3): tile=put(tile,21+j,tot(vd[j:j+1]*vd[j:j+1])*0.25)
    zfinal(YF[1],p.x,p.y,5,RLy,RRy)
    fin(YF[1],[shard(YF[1],p.x,p.b),RLy.at[5,p.z],RRy.at[5,p.z]])
    rl=jnp.zeros((rp,128),F32); rlane=lax.broadcasted_iota(jnp.int32,(rp,128),1)
    for i in range(3):
        sq=Gs_ref[i]; sq=sq*sq+EPS_SQUARE
        for (j,s) in blocks(i): rl=rl+jnp.where(rlane==j,jnp.sum(sq[:,s],axis=1,keepdims=True),0.0)
        cloc[i:i+1,:]=jnp.sum(sq,axis=0,keepdims=True)
    cloc[3:8,:]=jnp.zeros((5,D),F32)
    rloc[...]=rl
    ccs=[];rcs=[]
    for k,d in enumerate(bpeers):
        cp=remote(cloc,cin.at[k],eS.at[2,k],eR.at[2,k],d); start(cp); ccs.append(cp)
    for k,d in enumerate(mpeers):
        cp=remote(rloc,rin.at[k],eS.at[3,k],eR.at[3,k],d); start(cp); rcs.append(cp)
    for cp in rcs: cp.wait_recv()
    rs=rloc[...]+rin[0]+rin[1]+rin[2]
    ncol=jnp.where(rlane>=4,1.0/3072.0,1.0/768.0)
    rnew=0.5*rold_ref[...]+0.5*rs*ncol
    R_ref[...]=rnew
    for cp in ccs: cp.wait_recv()
    cs=cloc[...]
    for k in range(nb-1): cs=cs+cin[k]
    cnew=0.5*cold_ref[...]+0.5*cs*(1.0/768.0)
    C_ref[...]=cnew
    for i in range(3):
        g=Gs_ref[i]; g2=g*g/cnew[i:i+1,:]
        for (j,s) in blocks(i):
            tile=put(tile,6+j,tot(jnp.sum(g2[:,s],axis=1,keepdims=True)/rnew[:,j:j+1]))
    for j in (0,1,2,4): tile=put(tile,j,tot(rnew[:,j:j+1])*(1.0/(768*4)))
    tile=put(tile,3,tot(cnew[0:1,576:768])*(1.0/(768*nb)))
    tile=put(tile,5,tot(cnew[2:3,:])*(1.0/(3072*nb)))
    sloc[0]=tile
    scs=[]
    for k,d in enumerate(bpeers):
        cp=remote(sloc.at[0],sin.at[k],eS.at[4,k],eR.at[4,k],d); start(cp); scs.append(cp)
    for cp in scs: cp.wait_recv()
    for k in range(nb-1): tile=tile+sin[k]
    sloc[1]=tile
    scs=[]
    for k,d in enumerate(mpeers):
        cp=remote(sloc.at[1],smp.at[k],eS.at[5,k],eR.at[5,k],d); start(cp); scs.append(cp)
    for cp in scs: cp.wait_recv()
    for k in range(3): tile=tile+smp[k]
    out=jnp.zeros((8,128),F32)
    for j in range(9):
        n=768.0*768.0 if j<4 else (768.0*3072.0 if j<6 else 768.0)
        if j<6:
            mean=tile[0:1,j:j+1]; us=mean*tile[0:1,6+j:7+j]/n; ws=tile[0:1,12+j:13+j]/n
        else:
            mean=jnp.ones((1,1),F32); us=tile[0:1,15+j:16+j]/n; ws=tile[0:1,12+j:13+j]/n
        urms=jnp.sqrt(us)
        coef=jnp.sqrt(ws)/jnp.maximum(1.0,urms/CLIP)*jnp.sqrt(mean)
        out=out+jnp.where((lanes==j)&(sub==0),urms,0.0)+jnp.where((lanes==j)&(sub==1),coef,0.0)
    S_ref[...]=out
    rowc.wait_recv(); rowf.wait_recv(); lc.wait()
    for cp,cond in pend:
        when(cond,cp.wait_send)

def summed_call(G,rows,small,w,rold,cold,vold,vmom,nb):
    nz=nb//2; rp=w.shape[1]; T=rows.shape[0]
    V=pltpu.VMEM; S=pltpu.SemaphoreType.DMA
    vm=pl.BlockSpec(memory_space=V); an=pl.BlockSpec(memory_space=pl.ANY)
    sd=jax.ShapeDtypeStruct
    return pl.pallas_call(functools.partial(summed_kernel,nz,rp,nb),
        out_shape=(sd((3,rp,D),F32),sd((4,T,2*D),BF),sd((rp,128),F32),sd((8,D),F32),sd((8,128),F32),sd((16,128),F32),sd((8,128),F32)),
        in_specs=[an,an]+[vm]*6,out_specs=(vm,an)+(vm,)*5,
        scratch_shapes=[V((3,2,nb*rp,D),BF),V((3,2,nb*rp,D),BF),V((2,2,nz,rp,D),BF),V((2,nz,rp,D),BF),V((6,nz,rp,D),BF),V((6,nz,rp,D),BF),
            V((4,nz,rp,D),BF),V((4,nz,rp,D),BF),V((2,rp,D),BF),V((rp,D),BF),V((nb,8,128),F32),V((3,8,128),F32),V((nb,8,D),F32),V((3,rp,128),F32),
            V((nb,8,128),F32),V((3,8,128),F32),V((rp,128),F32),V((8,D),F32),V((2,8,128),F32),V((nb,8,128),F32),
            S((3,3)),S((3,2,nb)),S((3,2,nb)),S((2,2,nz)),S((2,2,nz)),S((2,nz)),S((2,nz)),S((6,2,nz)),S((6,2,nz)),S((1,)),S((1,)),S((2,2)),S((2,2)),S((2,8)),S((2,8)),S((6,nb)),S((6,nb))],
        compiler_params=pltpu.CompilerParams(collective_id=1,has_side_effects=True,vmem_limit_bytes=60<<20),
        name="summed")(G,rows,small,w,rold,cold,vold,vmom)


BF=jnp.bfloat16; F32=jnp.float32; D=768
def place_kernel(tok_ref, cot_ref, rows_ref, sel_ref, G_ref, w_ref, vold_ref, R_ref, C_ref, S_ref, V_ref, vdir_ref,
                 bo_ref, ig_ref, qg, qr, qc, qn, og, orr, oc, on, ug, ur, uc, un, dgr, dr, dc, dn, rg, rm, rn, gg, gmo, gn):
    length=tok_ref.shape[1]; picks=rows_ref.shape[1]
    pos=lax.broadcasted_iota(jnp.int32,(length,picks),0)
    hot=(pos==sel_ref[0]).astype(F32)
    cover=jnp.sum(hot,axis=1,keepdims=True)>0.5
    hot=hot.astype(BF)
    vals=jnp.dot(hot,rows_ref[0],preferred_element_type=F32)
    bo_ref[0]=jnp.where(cover,vals[:,0:D],tok_ref[0].astype(F32)).astype(BF)
    ig_ref[0]=jnp.where(cover,vals[:,D:],cot_ref[0].astype(F32))
    @pl.when(pl.program_id(0)==0)
    def _():
        def new(i,s,j):
            g=G_ref[i,:,s]
            return g,w_ref[i,:,s].astype(F32)-S_ref[1:2,j:j+1]*(g*lax.rsqrt(R_ref[:,j:j+1]*C_ref[i:i+1,s]))
        for j in range(3):
            qg[j],qn[j]=new(0,slice(j*192,(j+1)*192),j)
            qc[j:j+1,:]=C_ref[0:1,j*192:(j+1)*192]
        g,n=new(0,slice(576,768),3); og[...]=g.T; on[...]=n.T
        g,n=new(1,slice(0,D),4); ug[...]=g; un[...]=n
        g,n=new(2,slice(0,D),5); dgr[...]=g.T; dn[...]=n.T
        Rt=R_ref[...].T
        qr[...]=Rt[0:3]; oc[...]=Rt[3:4]; ur[...]=Rt[4:5]; dc[...]=Rt[5:6]
        orr[...]=C_ref[0:1,576:768]; uc[...]=C_ref[1:2,:]; dr[...]=C_ref[2:3,:]
        rg[...]=V_ref[0:1,0:96]; gg[...]=V_ref[1:3,0:96]
        rm[...]=V_ref[8:9,0:96]; gmo[...]=V_ref[9:11,0:96]
        rn[...]=vold_ref[0:1,0:96]-S_ref[1:2,6:7]*vdir_ref[0:1,0:96]
        gn[0:1,:]=vold_ref[1:2,0:96]-S_ref[1:2,7:8]*vdir_ref[1:2,0:96]
        gn[1:2,:]=vold_ref[2:3,0:96]-S_ref[1:2,8:9]*vdir_ref[2:3,0:96]
def place_call(tokens,cot,allrows,selrel,G,w,vold,R,C,S,V,vdir):
    rows,length,_=tokens.shape; picks=selrel.shape[2]
    allrows=allrows.reshape(rows,picks,2*D)
    sd=lambda *s: jax.ShapeDtypeStruct(s,F32)
    rp=w.shape[1]
    row=lambda *s: pl.BlockSpec((1,)+s,lambda i:(i,0,0))
    def whole(s):
        n=len(s); return pl.BlockSpec(s,lambda i:(0,)*n)
    small=[(3,rp,192),(3,rp),(3,192),(3,rp,192),(192,rp),(1,192),(1,rp),(192,rp),(rp,D),(1,rp),(1,D),(rp,D),(D,rp),(1,D),(1,rp),(D,rp),(1,rp),(1,rp),(1,rp),(2,rp),(2,rp),(2,rp)]
    return pl.pallas_call(place_kernel,grid=(rows,),
        out_shape=(jax.ShapeDtypeStruct(tokens.shape,BF),jax.ShapeDtypeStruct(cot.shape,F32))+tuple(sd(*s) for s in small),
        in_specs=[row(length,D),row(length,D),row(picks,2*D),row(1,picks)]+[whole(a.shape) for a in (G,w,vold,R,C,S,V,vdir)],
        out_specs=(row(length,D),row(length,D))+tuple(whole(s) for s in small),
        compiler_params=pltpu.CompilerParams(vmem_limit_bytes=48<<20),
        name="place")(tokens,cot,allrows,selrel,G,w,vold,R,C,S,V,vdir)


def tile_of(rows,height,width):
    padded=[jnp.pad(r.astype(F32),((0,0),(0,width-r.shape[1]))) for r in rows]
    v=jnp.concatenate(padded,axis=0)
    return jnp.pad(v,((0,height-v.shape[0]),(0,0)))

def local_fast(tokens,segments,selection,cotangent,qkv_weight,out_weight,up_weight,down_weight,router_weight,norm_gains,
               qkv_rows,qkv_cols,out_rows,out_cols,up_rows,up_cols,down_rows,down_cols,router_moment,gains_moment):
    nb=lax.axis_size("batch"); m=lax.axis_index("mp")
    length=tokens.shape[1]; picks=selection.shape[1]; rows=tokens.shape[0]; per=rows//4
    w=jnp.stack([jnp.concatenate([qkv_weight[0],qkv_weight[1],qkv_weight[2],out_weight.T],axis=1),up_weight,down_weight.T])
    vold=tile_of([router_weight[None],norm_gains],8,128)
    vmom=tile_of([router_moment[None],gains_moment],8,128)
    rold=tile_of([qkv_rows,out_cols[None],up_rows[None],down_cols[None]],128,qkv_rows.shape[1]).T
    cold=tile_of([qkv_cols.reshape(1,-1),],1,768)
    cold=tile_of([jnp.concatenate([qkv_cols.reshape(1,-1),out_rows[None]],axis=1),up_cols[None],down_rows[None]],8,768)
    mine=lax.dynamic_slice_in_dim(selection,m*per,per,0)
    segs=lax.dynamic_slice_in_dim(segments,m*per,per,0)
    begin=jnp.sum(segs[:,:,None]<jnp.arange(1,8)[None,None,:],axis=1)
    seg=jnp.sum(mine[:,:,None]>=begin[:,None,:],axis=2).astype(jnp.int32)
    W,sel,vall=gather_call(w,vold,tokens,cotangent,selection[:,:,None],nb,picks)
    G,out_rows_low,small=block_call(sel,W,vall,seg,picks)
    Gs,allrows,R,C,S,V,vdir=summed_call(G,out_rows_low,small,w,rold,cold,vold,vmom,nb)
    (bo,ig,qg,qr,qc,qn,og,orr,oc,on,ug,ur,uc,un,dgr,dr,dc,dn,rg,rm,rn,gg,gmo,gn)=place_call(
        tokens,cotangent,allrows,(selection-m*length)[:,None,:],Gs,w,vold,R,C,S,V,vdir)
    return (bo,ig,qg,qr,qc,qn,og,orr[0],oc[0],on,ug,ur[0],uc[0],un,dgr,dr[0],dc[0],dn,rg[0],rm[0],rn[0],gg,gmo,gn,S[0,:9])

def chosen_local(mesh):
    return local_fast if (mesh.shape["batch"],mesh.shape["mp"])==(8,4) else local_any


def solution(mesh):
    in_specs = (
        P("batch", "mp", None),
        P("batch", None),
        P("batch", None),
        P("batch", "mp", None),
        P(None, "batch", "mp"),
        P("mp", "batch"),
        P("batch", "mp"),
        P("mp", "batch"),
        P("batch"),
        P(None, "batch"),
        P(None, "batch"),
        P(None, "mp"),
        P("mp"),
        P("batch"),
        P("batch"),
        P("mp"),
        P("mp"),
        P("batch"),
        P("batch"),
        P(None, "batch"),
    )
    out_specs = (
        P("batch", "mp", None),
        P("batch", "mp", None),
        P(None, "batch", "mp"),
        P(None, "batch"),
        P(None, "mp"),
        P(None, "batch", "mp"),
        P("mp", "batch"),
        P("mp"),
        P("batch"),
        P("mp", "batch"),
        P("batch", "mp"),
        P("batch"),
        P("mp"),
        P("batch", "mp"),
        P("mp", "batch"),
        P("mp"),
        P("batch"),
        P("mp", "batch"),
        P("batch"),
        P("batch"),
        P("batch"),
        P(None, "batch"),
        P(None, "batch"),
        P(None, "batch"),
        P(),
    )
    return jax.shard_map(chosen_local(mesh), mesh=mesh, in_specs=in_specs, out_specs=out_specs, check_vma=False)
```

```python
import functools

import jax
import jax.numpy as jnp
from jax import lax
from jax.experimental import pallas as pl
from jax.experimental.pallas import tpu as pltpu
from jax.sharding import PartitionSpec as P


D = 768
HEAD_DIM = 64
FF = 3072
MICRO = 2


EPS_NORM = 1e-06
EPS_SQUARE = 1e-30
DECAY = 0.5
CLIP_RMS = 0.3
RATE = 1.0
MASKED = -1e30


def rms_parts(values):
    inverse = lax.rsqrt(jnp.mean(values * values, axis=1, keepdims=True) + EPS_NORM)
    return (values * inverse, inverse)


def norm_back(grad_norm, gain_vec, scaled, inverse):
    grad_scaled = grad_norm * gain_vec
    grad_input = inverse * (
        grad_scaled - scaled * jnp.mean(grad_scaled * scaled, axis=1, keepdims=True)
    )
    return (grad_input, jnp.sum(grad_norm * scaled, axis=0))


def spread_into(values, index, pieces):
    size_piece = values.shape[-1]
    shape_full = values.shape[:-1] + (size_piece * pieces,)
    return lax.dynamic_update_slice_in_dim(
        jnp.zeros(shape_full, jnp.float32), values, index * size_piece, values.ndim - 1
    )


def own_piece(values, index, size_piece):
    return lax.dynamic_slice_in_dim(values, index * size_piece, size_piece, values.ndim - 1)


def factor_terms(gradient, row_old, col_old, row_index, row_count, col_index, col_count):
    square = gradient * gradient + EPS_SQUARE
    rows_here, cols_here = gradient.shape[-2:]
    row_term = (1.0 - DECAY) * jnp.sum(square, axis=-1) / (
        cols_here * col_count
    ) + DECAY * row_old * (col_index == 0)
    col_term = (1.0 - DECAY) * jnp.sum(square, axis=-2) / (
        rows_here * row_count
    ) + DECAY * col_old * (row_index == 0)
    return (
        spread_into(row_term, row_index, row_count),
        spread_into(col_term, col_index, col_count),
    )


def factor_direction(gradient, row_full, col_full, row_index, col_index):
    rows_here, cols_here = gradient.shape[-2:]
    row_mine = own_piece(row_full, row_index, rows_here)
    col_mine = own_piece(col_full, col_index, cols_here)
    mean_row = jnp.mean(row_full, axis=-1)[..., None, None]
    second = row_mine[..., :, None] * col_mine[..., None, :] / mean_row
    return (gradient * lax.rsqrt(second), row_mine, col_mine)


def local_any(
    tokens,
    segments,
    selection,
    cotangent,
    qkv_weight,
    out_weight,
    up_weight,
    down_weight,
    router_weight,
    norm_gains,
    qkv_rows,
    qkv_cols,
    out_rows,
    out_cols,
    up_rows,
    up_cols,
    down_rows,
    down_cols,
    router_moment,
    gains_moment,
):
    qkv_all, out_all, up_all, down_all, router_all, gains_all = (
        lax.all_gather(qkv_weight, "batch", axis=1, tiled=True),
        lax.all_gather(out_weight, "batch", axis=1, tiled=True),
        lax.all_gather(up_weight, "batch", axis=0, tiled=True),
        lax.all_gather(down_weight, "batch", axis=1, tiled=True),
        lax.all_gather(router_weight, "batch", axis=0, tiled=True),
        lax.all_gather(norm_gains, "batch", axis=1, tiled=True),
    )
    mp_index = lax.axis_index("mp")
    mp_count = lax.axis_size("mp")
    batch_index = lax.axis_index("batch")
    batch_count = lax.axis_size("batch")
    rows_dev, length_here, width_full = tokens.shape
    width_local = width_full // mp_count
    heads_local = qkv_all.shape[2] // HEAD_DIM
    per_micro = rows_dev // MICRO
    score_scale = HEAD_DIM ** (-0.5)
    gain_attn = gains_all[0].astype(jnp.float32)
    gain_mlp = gains_all[1].astype(jnp.float32)
    router_float = router_all.astype(jnp.float32)
    first_position = mp_index * length_here
    totals = None
    shards = None
    output_list = []
    grad_list = []
    for micro_index in range(MICRO):
        row_start = micro_index * per_micro
        row_stop = row_start + per_micro
        token_rows = tokens[row_start:row_stop]
        chosen = selection[row_start:row_stop]
        cot_rows = cotangent[row_start:row_stop]
        row_count, pick_count = chosen.shape
        token_count = row_count * pick_count
        local_position = chosen - first_position
        inside = (local_position >= 0) & (local_position < length_here)
        clipped = jnp.clip(local_position, 0, length_here - 1)
        zero_low = jnp.zeros((), jnp.bfloat16)
        token_term = jnp.where(
            inside[:, :, None],
            jnp.take_along_axis(token_rows, clipped[:, :, None], axis=1),
            zero_low,
        ).reshape(token_count, width_full)
        cot_term = jnp.where(
            inside[:, :, None], jnp.take_along_axis(cot_rows, clipped[:, :, None], axis=1), zero_low
        ).reshape(token_count, width_full)
        picked_float = lax.psum(token_term, "mp").astype(jnp.float32)
        cot_float = lax.psum(cot_term, "mp").astype(jnp.float32)
        picked_full = picked_float.astype(jnp.bfloat16)
        picked_local = lax.dynamic_slice_in_dim(picked_full, mp_index * width_local, width_local, 1)
        cot_local = lax.dynamic_slice_in_dim(cot_float, mp_index * width_local, width_local, 1)
        picked_segments = jnp.take_along_axis(segments[row_start:row_stop], chosen, axis=1)
        allowed = (chosen[:, None, None, :] <= chosen[:, None, :, None]) & (
            picked_segments[:, None, None, :] == picked_segments[:, None, :, None]
        )
        router_gate = jax.nn.sigmoid(
            jnp.dot(picked_full, router_all, preferred_element_type=jnp.float32)
        )
        scaled_attn, inverse_attn = rms_parts(picked_float)
        normed = (scaled_attn * gain_attn).astype(jnp.bfloat16)
        projected = jnp.einsum(
            "td,cde->cte", normed, qkv_all, preferred_element_type=jnp.float32
        ).astype(jnp.bfloat16)
        shaped = projected.reshape(3, row_count, pick_count, heads_local, HEAD_DIM)
        queries = shaped[0]
        key_rows = shaped[1]
        value_rows = shaped[2]
        scores = (
            jnp.einsum("rqhe,rkhe->rhqk", queries, key_rows, preferred_element_type=jnp.float32)
            * score_scale
        )
        masked = jnp.where(allowed, scores, MASKED)
        highest_score = jnp.max(masked, axis=-1, keepdims=True)
        exponent = jnp.exp(masked - highest_score)
        exp_total = jnp.sum(exponent, axis=-1, keepdims=True)
        log_total = highest_score + jnp.log(exp_total)
        attention_low = (exponent / exp_total).astype(jnp.bfloat16)
        attended = jnp.einsum(
            "rhqk,rkhe->rqhe", attention_low, value_rows, preferred_element_type=jnp.float32
        )
        attended = attended.reshape(token_count, heads_local * HEAD_DIM).astype(jnp.bfloat16)
        attn_local = lax.psum_scatter(
            jnp.dot(attended, out_all, preferred_element_type=jnp.float32),
            "mp",
            scatter_dimension=1,
            tiled=True,
        )
        middle_local = picked_local.astype(jnp.float32) + attn_local
        middle = lax.all_gather(middle_local, "mp", axis=1, tiled=True)
        scaled_mlp, inverse_mlp = rms_parts(middle)
        normed_mid = (scaled_mlp * gain_mlp).astype(jnp.bfloat16)
        hidden = jnp.dot(normed_mid, up_all, preferred_element_type=jnp.float32)
        active = jax.nn.gelu(hidden).astype(jnp.bfloat16)
        mlp_local = lax.psum_scatter(
            jnp.dot(active, down_all, preferred_element_type=jnp.float32).astype(jnp.bfloat16),
            "mp",
            scatter_dimension=1,
            tiled=True,
        ).astype(jnp.float32)
        branch_local = attn_local + mlp_local
        output_local = (
            picked_local.astype(jnp.float32) + router_gate[:, None] * branch_local
        ).astype(jnp.bfloat16)
        output_full = lax.all_gather(output_local, "mp", axis=1, tiled=True)
        grad_gate = lax.psum(jnp.sum(cot_local * branch_local, axis=1), "mp")
        direct = router_gate[:, None] * cot_float
        grad_mlp = direct.astype(jnp.bfloat16)
        down_part = jnp.einsum("tf,td->fd", active, grad_mlp, preferred_element_type=jnp.float32)
        grad_active = jnp.einsum(
            "td,fd->tf", grad_mlp, down_all, preferred_element_type=jnp.float32
        )
        gelu_values, gelu_pull = jax.vjp(jax.nn.gelu, hidden)
        grad_hidden = gelu_pull(grad_active)[0].astype(jnp.bfloat16)
        up_part = jnp.einsum(
            "td,tf->df", normed_mid, grad_hidden, preferred_element_type=jnp.float32
        )
        grad_normed_mid = lax.psum(
            jnp.einsum("tf,df->td", grad_hidden, up_all, preferred_element_type=jnp.float32), "mp"
        )
        grad_middle, gain_mlp_part = norm_back(grad_normed_mid, gain_mlp, scaled_mlp, inverse_mlp)
        grad_attn = (grad_middle + direct).astype(jnp.bfloat16)
        out_part = jnp.einsum("te,td->ed", attended, grad_attn, preferred_element_type=jnp.float32)
        grad_attended = jnp.einsum(
            "td,ed->te", grad_attn, out_all, preferred_element_type=jnp.float32
        ).astype(jnp.bfloat16)
        grad_attended = grad_attended.reshape(row_count, pick_count, heads_local, HEAD_DIM)
        scores_again = (
            jnp.einsum("rqhe,rkhe->rhqk", queries, key_rows, preferred_element_type=jnp.float32)
            * score_scale
        )
        attention = jnp.exp(jnp.where(allowed, scores_again, MASKED) - log_total)
        grad_values = jnp.einsum(
            "rhqk,rqhe->rkhe",
            attention.astype(jnp.bfloat16),
            grad_attended,
            preferred_element_type=jnp.float32,
        )
        grad_weights = jnp.einsum(
            "rqhe,rkhe->rhqk", grad_attended, value_rows, preferred_element_type=jnp.float32
        )
        grad_scores = (
            attention * (grad_weights - jnp.sum(attention * grad_weights, axis=-1, keepdims=True))
        ).astype(jnp.bfloat16)
        grad_queries = (
            jnp.einsum("rhqk,rkhe->rqhe", grad_scores, key_rows, preferred_element_type=jnp.float32)
            * score_scale
        )
        grad_keys = (
            jnp.einsum("rhqk,rqhe->rkhe", grad_scores, queries, preferred_element_type=jnp.float32)
            * score_scale
        )
        grad_projected = (
            jnp.stack([grad_queries, grad_keys, grad_values])
            .reshape(3, token_count, heads_local * HEAD_DIM)
            .astype(jnp.bfloat16)
        )
        qkv_part = jnp.einsum(
            "td,cte->cde", normed, grad_projected, preferred_element_type=jnp.float32
        )
        grad_normed = lax.psum(
            jnp.einsum(
                "cte,cde->td", grad_projected, qkv_all, preferred_element_type=jnp.float32
            ).astype(jnp.bfloat16),
            "mp",
        ).astype(jnp.float32)
        grad_norm_in, gain_attn_part = norm_back(grad_normed, gain_attn, scaled_attn, inverse_attn)
        grad_logit = grad_gate * router_gate * (1.0 - router_gate)
        router_part = jnp.dot(grad_logit, picked_float, precision=lax.Precision.HIGHEST)
        grad_full = cot_float + grad_middle + grad_norm_in + grad_logit[:, None] * router_float
        row_positions = jnp.arange(row_count)[:, None]
        write_index = jnp.where(inside, local_position, length_here)
        output_rows = token_rows.at[row_positions, write_index].set(
            output_full.reshape(row_count, pick_count, width_full), mode="drop"
        )
        grad_rows = (
            cot_rows.astype(jnp.float32)
            .at[row_positions, write_index]
            .set(grad_full.reshape(row_count, pick_count, width_full), mode="drop")
        )
        gradients = (
            qkv_part,
            out_part,
            up_part,
            down_part,
            router_part,
            jnp.stack([gain_attn_part, gain_mlp_part]),
        )
        gradients, output_rows, grad_rows = (gradients, output_rows, grad_rows)
        output_list.append(output_rows)
        grad_list.append(grad_rows)
        totals = gradients if totals is None else jax.tree.map(jnp.add, totals, gradients)
    shards = (
        lax.psum_scatter(totals[0], "batch", scatter_dimension=1, tiled=True),
        lax.psum_scatter(totals[1], "batch", scatter_dimension=1, tiled=True),
        lax.psum_scatter(totals[2], "batch", scatter_dimension=0, tiled=True),
        lax.psum_scatter(totals[3], "batch", scatter_dimension=1, tiled=True),
        lax.psum_scatter(totals[4], "batch", scatter_dimension=0, tiled=True),
        lax.psum_scatter(totals[5], "batch", scatter_dimension=1, tiled=True),
    )
    block_output = jnp.concatenate(output_list, axis=0)
    input_grad = jnp.concatenate(grad_list, axis=0)
    qkv_grad, out_grad, up_grad, down_grad, router_grad, gains_grad = shards
    first_mp = (mp_index == 0).astype(jnp.float32)
    qkv_old = qkv_weight.astype(jnp.float32)
    out_old = out_weight.astype(jnp.float32)
    up_old = up_weight.astype(jnp.float32)
    down_old = down_weight.astype(jnp.float32)
    router_old = router_weight.astype(jnp.float32)
    gains_old = norm_gains.astype(jnp.float32)
    qkv_row_term, qkv_col_term = factor_terms(
        qkv_grad, qkv_rows, qkv_cols, batch_index, batch_count, mp_index, mp_count
    )
    out_row_term, out_col_term = factor_terms(
        out_grad, out_rows, out_cols, mp_index, mp_count, batch_index, batch_count
    )
    up_row_term, up_col_term = factor_terms(
        up_grad, up_rows, up_cols, batch_index, batch_count, mp_index, mp_count
    )
    down_row_term, down_col_term = factor_terms(
        down_grad, down_rows, down_cols, mp_index, mp_count, batch_index, batch_count
    )
    weight_squares = jnp.concatenate(
        [
            jnp.sum(qkv_old * qkv_old, axis=(1, 2)),
            jnp.stack(
                [
                    jnp.sum(out_old * out_old),
                    jnp.sum(up_old * up_old),
                    jnp.sum(down_old * down_old),
                    first_mp * jnp.sum(router_old * router_old),
                ]
            ),
            first_mp * jnp.sum(gains_old * gains_old, axis=1),
        ]
    )
    (
        qkv_row_full,
        qkv_col_full,
        out_row_full,
        out_col_full,
        up_row_full,
        up_col_full,
        down_row_full,
        down_col_full,
        weight_sums,
    ) = lax.psum(
        (
            qkv_row_term,
            qkv_col_term,
            out_row_term,
            out_col_term,
            up_row_term,
            up_col_term,
            down_row_term,
            down_col_term,
            weight_squares,
        ),
        ("batch", "mp"),
    )
    qkv_dir, qkv_rows_new, qkv_cols_new = factor_direction(
        qkv_grad, qkv_row_full, qkv_col_full, batch_index, mp_index
    )
    out_dir, out_rows_new, out_cols_new = factor_direction(
        out_grad, out_row_full, out_col_full, mp_index, batch_index
    )
    up_dir, up_rows_new, up_cols_new = factor_direction(
        up_grad, up_row_full, up_col_full, batch_index, mp_index
    )
    down_dir, down_rows_new, down_cols_new = factor_direction(
        down_grad, down_row_full, down_col_full, mp_index, batch_index
    )
    router_moment_new = DECAY * router_moment + (1.0 - DECAY) * (
        router_grad * router_grad + EPS_SQUARE
    )
    router_dir = router_grad * lax.rsqrt(router_moment_new)
    gains_moment_new = DECAY * gains_moment + (1.0 - DECAY) * (gains_grad * gains_grad + EPS_SQUARE)
    gains_dir = gains_grad * lax.rsqrt(gains_moment_new)
    update_squares = jnp.concatenate(
        [
            jnp.sum(qkv_dir * qkv_dir, axis=(1, 2)),
            jnp.stack(
                [
                    jnp.sum(out_dir * out_dir),
                    jnp.sum(up_dir * up_dir),
                    jnp.sum(down_dir * down_dir),
                    first_mp * jnp.sum(router_dir * router_dir),
                ]
            ),
            first_mp * jnp.sum(gains_dir * gains_dir, axis=1),
        ]
    )
    update_sums = lax.psum(update_squares, ("batch", "mp"))
    entries = jnp.array([D * D, D * D, D * D, D * D, D * FF, FF * D, D, D, D], jnp.float32)
    update_rms = jnp.sqrt(update_sums / entries)
    weight_rms = jnp.sqrt(weight_sums / entries)
    factors = RATE * weight_rms / jnp.maximum(1.0, update_rms / CLIP_RMS)
    qkv_new = qkv_old - factors[0:3, None, None] * qkv_dir
    out_new = out_old - factors[3] * out_dir
    up_new = up_old - factors[4] * up_dir
    down_new = down_old - factors[5] * down_dir
    router_new = router_old - factors[6] * router_dir
    gains_new = gains_old - factors[7:9, None] * gains_dir
    return (
        block_output,
        input_grad,
        qkv_grad,
        qkv_rows_new,
        qkv_cols_new,
        qkv_new,
        out_grad,
        out_rows_new,
        out_cols_new,
        out_new,
        up_grad,
        up_rows_new,
        up_cols_new,
        up_new,
        down_grad,
        down_rows_new,
        down_cols_new,
        down_new,
        router_grad,
        router_moment_new,
        router_new,
        gains_grad,
        gains_moment_new,
        gains_new,
        update_rms,
    )


MESH=pl.DeviceIdType.MESH
BF=jnp.bfloat16; F32=jnp.float32

class Plane:
    def __init__(s):
        s.b=lax.axis_index("batch"); s.m=lax.axis_index("mp")
        s.z=s.b//2; s.y=lax.rem(s.b,2); s.x=s.m//2; s.c=lax.rem(s.m,2)
        s.left=(s.b-2,s.m); s.right=(s.b+2,s.m)
        s.ypeer=(s.z*2+1-s.y,s.m); s.xpeer=(s.b,(1-s.x)*2+s.c); s.core=(s.b,s.x*2+1-s.c)

def greet(peers):
    bar=pltpu.get_barrier_semaphore()
    for d in peers: pl.semaphore_signal(bar,inc=1,device_id=d,device_id_type=MESH)
    pl.semaphore_wait(bar,len(peers))

def gather_kernel(nz, rp, length_here, picks, w_ref, v_ref, tok_ref, cot_ref, sel_ref, W_ref, out_ref, vall_ref,
                  tokb, cotb, zbuf, ra, rb, rx, locsem, tsem, csem, rsem, ssem, xs, xr, vs, vr):
    p=Plane()
    nb=2*nz
    bpeers=[(lax.rem(p.b+k,nb),p.m) for k in range(1,nb)]
    greet(bpeers+[p.xpeer,p.core])
    def at(i,m,b): return W_ref.at[i,m,pl.ds(pl.multiple_of(b*rp,rp),rp)]
    groups=[((1-p.x)*2+1-p.c),((1-p.x)*2+p.c),(p.x*2+1-p.c),p.m]
    cps=[]
    own=[pltpu.make_async_copy(w_ref.at[i],at(i,p.m,p.b),locsem.at[i]) for i in range(3)]
    sends=[]
    def send(i,m,b,d,slot,src=None):
        cp=pltpu.make_async_remote_copy(src_ref=at(i,m,b) if src is None else src,dst_ref=at(i,m,b),
            send_sem=ssem.at[i,slot],recv_sem=rsem.at[i,m,b],device_id=d,device_id_type=MESH)
        cp.start()
        return cp
    def arrived(i,m,b):
        pltpu.make_async_remote_copy(src_ref=at(i,m,b),dst_ref=at(i,m,b),send_sem=ssem.at[i,0],recv_sem=rsem.at[i,m,b],
            device_id=p.core,device_id_type=MESH).wait_recv()
    class Ctr:
        def __init__(s): s.n={}
    ctr=[0,0,0]
    pend=[]
    def fwd(i,m,b,d,cond=None,src=None):
        slot=ctr[i]; ctr[i]+=1
        if cond is None:
            pend.append((None,send(i,m,b,d,slot,src)))
        else:
            @pl.when(cond)
            def _(): send(i,m,b,d,slot,src)
            pend.append((cond,(i,m,b,d,slot,src)))
    def done():
        for cond,x in pend:
            if cond is None: x.wait_send()
            else:
                i,m,b,d,slot,src=x
                @pl.when(cond)
                def _():
                    pltpu.make_async_remote_copy(src_ref=at(i,m,b) if src is None else src,dst_ref=at(i,m,b),
                        send_sem=ssem.at[i,slot],recv_sem=rsem.at[i,m,b],device_id=d,device_id_type=MESH).wait_send()
    mx=(1-p.x)*2+p.c
    mc=p.x*2+1-p.c
    yb=p.z*2+1-p.y
    def zpass(i,shards,t,extra):
        for (m,y) in shards:
            zl=p.z-1-t
            @pl.when(zl>=0)
            def _(): arrived(i,m,zl*2+y)
            fwd(i,m,zl*2+y,p.right,(zl>=0)&(p.z<nz-1))
            for d in extra: fwd(i,m,zl*2+y,d,zl>=0)
            zr=p.z+1+t
            @pl.when(zr<nz)
            def _(): arrived(i,m,zr*2+y)
            fwd(i,m,zr*2+y,p.left,(zr<nz)&(p.z>0))
            for d in extra: fwd(i,m,zr*2+y,d,zr<nz)
    for i in range(3): own[i].start()
    vall_ref[p.b]=v_ref[...]
    vcs=[pltpu.make_async_remote_copy(src_ref=v_ref,dst_ref=vall_ref.at[p.b],send_sem=vs.at[k],recv_sem=vr.at[k],device_id=d,device_id_type=MESH) for k,d in enumerate(bpeers)]
    for cp in vcs: cp.start()
    for i in (0,2,1):
        src=w_ref.at[i]
        if i!=LAST:
            fwd(i,p.m,p.b,p.right,p.z<nz-1,src); fwd(i,p.m,p.b,p.left,p.z>0,src)
            fwd(i,p.m,p.b,p.xpeer,None,src); fwd(i,p.m,p.b,p.ypeer,None,src)
        else:
            fwd(i,p.m,p.b,p.xpeer,None,src); fwd(i,p.m,p.b,p.ypeer,None,src)
            fwd(i,p.m,p.b,p.right,p.z<nz-1,src); fwd(i,p.m,p.b,p.left,p.z>0,src)
        fwd(i,p.m,p.b,p.core,None,src)
    for g in groups:
        for k in range(2):
            r=g*2+k
            a=pltpu.make_async_copy(tok_ref.at[r],tokb.at[r],tsem.at[r]); a.start()
            a=pltpu.make_async_copy(cot_ref.at[r],cotb.at[r],csem.at[r]); a.start()
    def pick(g,slot):
        for k in range(2):
            r=g*2+k
            pltpu.make_async_copy(tok_ref.at[r],tokb.at[r],tsem.at[r]).wait()
            pltpu.make_async_copy(cot_ref.at[r],cotb.at[r],csem.at[r]).wait()
            col=sel_ref[r]-p.m*length_here
            hot=(col==lax.broadcasted_iota(jnp.int32,(picks,length_here),1)).astype(F32).astype(BF)
            zbuf[slot,k*picks:(k+1)*picks,0:768]=jnp.dot(hot,tokb[r],preferred_element_type=F32).astype(BF)
            zbuf[slot,k*picks:(k+1)*picks,768:1536]=jnp.dot(hot,cotb[r],preferred_element_type=F32).astype(BF)
    def ship(slot,dst,n,d):
        return pltpu.make_async_remote_copy(src_ref=zbuf.at[slot],dst_ref=dst,send_sem=xs.at[n],recv_sem=xr.at[n],device_id=d,device_id_type=MESH)
    pick(groups[0],0)
    cb=ship(0,rb,0,p.core); cb.start()
    zx=[i for i in range(3) if i!=LAST]
    i=LAST
    arrived(i,mx,p.b); fwd(i,mx,p.b,p.ypeer); fwd(i,mx,p.b,p.right,p.z<nz-1); fwd(i,mx,p.b,p.left,p.z>0); fwd(i,mx,p.b,p.core)
    for i in zx: zpass(i,[(p.m,p.y)],0,[p.xpeer,p.ypeer,p.core])
    pick(groups[1],1)
    cb.wait_recv()
    zbuf[1]=zbuf[1]+rb[...]
    cx=ship(1,rx,1,p.xpeer); cx.start()
    i=LAST
    arrived(i,p.m,yb); fwd(i,p.m,yb,p.right,p.z<nz-1); fwd(i,p.m,yb,p.left,p.z>0); fwd(i,p.m,yb,p.core)
    arrived(i,mx,yb); fwd(i,mx,yb,p.right,p.z<nz-1); fwd(i,mx,yb,p.left,p.z>0); fwd(i,mx,yb,p.core)
    pick(groups[2],2)
    ca=ship(2,ra,2,p.core); ca.start()
    for i in zx: zpass(i,[(p.m,p.y)],1,[p.xpeer,p.ypeer,p.core])
    pick(groups[3],3)
    zpass(LAST,[(p.m,p.y),(mx,p.y)],0,[p.core])
    for i in zx:
        arrived(i,mx,p.b); fwd(i,mx,p.b,p.ypeer); fwd(i,mx,p.b,p.core)
    zpass(LAST,[(p.m,1-p.y),(mx,1-p.y)],0,[p.core])
    for i in zx: zpass(i,[(p.m,p.y)],2,[p.xpeer,p.ypeer,p.core])
    allsh=[(p.m,p.y),(mx,p.y),(p.m,1-p.y),(mx,1-p.y)]
    def xarr(i,t):
        zl=p.z-1-t
        @pl.when(zl>=0)
        def _(): arrived(i,mx,zl*2+p.y)
        fwd(i,mx,zl*2+p.y,p.ypeer,zl>=0); fwd(i,mx,zl*2+p.y,p.core,zl>=0)
        zr=p.z+1+t
        @pl.when(zr<nz)
        def _(): arrived(i,mx,zr*2+p.y)
        fwd(i,mx,zr*2+p.y,p.ypeer,zr<nz); fwd(i,mx,zr*2+p.y,p.core,zr<nz)
    zpass(LAST,allsh,1,[p.core])
    for i in zx:
        arrived(i,p.m,yb); fwd(i,p.m,yb,p.core)
        xarr(i,0)
    for i in zx: xarr(i,1)
    zpass(LAST,allsh,2,[p.core])
    for i in zx: xarr(i,2)
    for z in range(nz):
        for i in zx:
            for m in (p.m,mx):
                if m is p.m:
                    cond=p.z!=z
                    @pl.when(cond)
                    def _(): arrived(i,m,z*2+1-p.y)
                    fwd(i,m,z*2+1-p.y,p.core,cond)
                else:
                    arrived(i,m,z*2+1-p.y); fwd(i,m,z*2+1-p.y,p.core)
    ca.wait_recv(); cx.wait_recv()
    zbuf[3]=zbuf[3]+ra[...]+rx[...]
    fin=pltpu.make_async_copy(zbuf.at[3],out_ref,locsem.at[3]); fin.start()
    for i in range(3):
        for m in (mc,(1-p.x)*2+1-p.c):
            for b in range(2*nz): arrived(i,m,b)
    fin.wait()
    for cp in vcs: cp.wait()
    for o in own: o.wait()
    cb.wait_send(); cx.wait_send(); ca.wait_send()
    done()
LAST=0
def gather_call(wsh,vold,tokens,cot,selcol,B,picks):
    nz=B//2; rp=wsh.shape[1]
    rows,length_here,width=tokens.shape
    per=rows//4*picks
    D=pltpu.SemaphoreType.DMA
    return pl.pallas_call(functools.partial(gather_kernel,nz,rp,length_here,picks),
        out_shape=(jax.ShapeDtypeStruct((3,4,B*rp,768),BF),jax.ShapeDtypeStruct((per,2*width),BF),jax.ShapeDtypeStruct((B,8,128),F32)),
        in_specs=[pl.BlockSpec(memory_space=m) for m in (pl.ANY,pltpu.VMEM,pl.ANY,pl.ANY,pltpu.VMEM)],
        out_specs=(pl.BlockSpec(memory_space=pl.ANY),)*2+(pl.BlockSpec(memory_space=pltpu.VMEM),),
        scratch_shapes=[pltpu.VMEM((rows,length_here,width),BF),pltpu.VMEM((rows,length_here,width),BF),
            pltpu.VMEM((4,per,2*width),BF),pltpu.VMEM((per,2*width),BF),pltpu.VMEM((per,2*width),BF),pltpu.VMEM((per,2*width),BF),
            D((4,)),D((rows,)),D((rows,)),D((3,4,B)),D((3,120)),D((3,)),D((3,)),D((B,)),D((B,))],
        compiler_params=pltpu.CompilerParams(collective_id=0,has_side_effects=True,vmem_limit_bytes=56<<20),
        name="gather_all")(wsh,vold,tokens,cot,selcol)


BF=jnp.bfloat16; F32=jnp.float32
EPS_NORM=1e-6; MASKED=-1e30; HD=64
GC=0.7978845608028654; GA=0.044715
def nn(a,b): return jnp.dot(a,b,preferred_element_type=F32)
def nt(a,b): return lax.dot_general(a,b,(((1,),(1,)),((),())),preferred_element_type=F32)
def tn(a,b): return lax.dot_general(a,b,(((0,),(0,)),((),())),preferred_element_type=F32)
def vectors(vec_ref):
    nb=vec_ref.shape[0]
    vec=jnp.concatenate([vec_ref[b,:,0:768//nb] for b in range(nb)],axis=1)
    return vec[0:1,:],vec[1:2,:],vec[2:3,:]
def root(v): return lax.rsqrt(jnp.mean(v*v,axis=1,keepdims=True)+EPS_NORM)
def front_kernel(picks, sel_ref, Wh_ref, vec_ref, seg_ref, segc_ref,
                 Gh_ref, P, probs, att, mid, accb, rows_ref, gg_ref,
                 normed, ba, nm, gm, act, gh, acc, nmT, gmT, W_ref, gst, wsem, gsem):
    router,gain0,gain1=vectors(vec_ref)
    T=sel_ref.shape[0]; D=768; R=T//picks
    def wcopy(i,m): return pltpu.make_async_copy(Wh_ref.at[i,m],W_ref.at[i,m],wsem.at[i,m])
    def gcopy(i,m,slot): return pltpu.make_async_copy(gst.at[slot],Gh_ref.at[i,m],gsem.at[slot])
    for i in range(3):
        for m in range(4): wcopy(i,m).start()
    x=sel_ref[:,0:D].astype(F32)
    gate=jax.nn.sigmoid(jnp.sum(x*router,axis=1,keepdims=True))
    normed[...]=(x*root(x)*gain0).astype(BF)
    gmv=(gate*sel_ref[:,D:].astype(F32)).astype(BF)
    gm[...]=gmv
    gmT[...]=gmv.T
    @pl.loop(0,4)
    def _(m):
        wcopy(0,m).wait()
        P[m]=nn(normed[...],W_ref[0,m]).astype(BF)
    scale=HD**-0.5
    qi=lax.broadcasted_iota(jnp.int32,(picks,picks),0); ki=lax.broadcasted_iota(jnp.int32,(picks,picks),1)
    @pl.loop(0,R)
    def _(r):
        rs=pl.ds(pl.multiple_of(r*picks,picks),picks)
        ok=(ki<=qi)&(seg_ref[r]==segc_ref[r])
        for m in range(4):
            outs=[]
            for j in range(3):
                o=j*HD
                q=P[m,rs,o:o+HD]; k=P[m,rs,192+o:192+o+HD]; v=P[m,rs,384+o:384+o+HD]
                s=jnp.where(ok,nt(q,k)*scale,MASKED)
                e=jnp.exp(s-jnp.max(s,axis=1,keepdims=True))
                p=(e/jnp.sum(e,axis=1,keepdims=True)).astype(BF)
                probs[r,m,j]=p
                outs.append(nn(p,v))
            att[m,rs,:]=jnp.concatenate(outs,axis=1).astype(BF)
    a=jnp.zeros((T,D),F32)
    for m in range(4):
        a=a+nt(att[m],W_ref[0,m,:,576:768])
    ba[...]=a
    mv=sel_ref[:,0:D].astype(F32)+a
    mid[...]=mv
    nmv=(mv*root(mv)*gain1).astype(BF)
    nm[...]=nmv
    nmT[...]=nmv.T
    acc[...]=jnp.zeros_like(acc)
    accb[...]=jnp.zeros_like(accb)
    @pl.loop(0,4)
    def _(m):
        wcopy(1,m).wait()
        wcopy(2,m).wait()
        for t in range(3):
            cs=slice(t*256,(t+1)*256)
            h=nn(nm[...],W_ref[1,m,:,cs])
            th=jnp.tanh(GC*(h+GA*h*h*h))
            act[:,cs]=(0.5*h*(1.0+th)).astype(BF)
            dg=0.5*(1.0+th)+0.5*h*(1.0-th*th)*(GC*(1.0+3.0*GA*h*h))
            gh[:,cs]=(nn(gm[...],W_ref[2,m,:,cs])*dg).astype(BF)
        acc[...]+=nt(act[...],W_ref[2,m])
        @pl.when(m>0)
        def _(): gcopy(1,m-1,0).wait()
        gst[0]=nn(gmT[...],act[...]).astype(BF)
        gcopy(1,m,0).start()
        @pl.when(m>0)
        def _(): gcopy(0,m-1,1).wait()
        gst[1]=nn(nmT[...],gh[...]).astype(BF)
        gcopy(0,m,1).start()
        accb[...]+=nt(gh[...],W_ref[1,m])
    br=ba[...]+acc[...]
    rows_ref[...]=(sel_ref[:,0:D].astype(F32)+gate*br).astype(BF)
    gg_ref[...]=jnp.sum(sel_ref[:,D:].astype(F32)*br,axis=1,keepdims=True)
    gcopy(1,3,0).wait()
    gcopy(0,3,1).wait()
def front_call(sel,W,vec,seg,picks):
    T=sel.shape[0]; D=768; R=T//picks
    V=pltpu.VMEM; S=pltpu.SemaphoreType.DMA
    vm=pl.BlockSpec(memory_space=V); an=pl.BlockSpec(memory_space=pl.ANY)
    sd=jax.ShapeDtypeStruct
    return pl.pallas_call(functools.partial(front_kernel,picks),
        out_shape=(sd((2,4,D,D),BF),sd((4,T,D),BF),sd((R,4,3,picks,picks),BF),sd((4,T,192),BF),sd((T,D),F32),sd((T,D),F32),sd((T,D),BF),sd((T,1),F32)),
        in_specs=[vm,an,vm,vm,vm],out_specs=(an,)+(vm,)*7,
        scratch_shapes=[V((T,D),BF),V((T,D),F32),V((T,D),BF),V((T,D),BF),V((T,D),BF),V((T,D),BF),V((T,D),F32),V((D,T),BF),V((D,T),BF),
            V((3,4,D,D),BF),V((2,D,D),BF),S((3,4)),S((2,))],
        compiler_params=pltpu.CompilerParams(vmem_limit_bytes=58<<20),
        name="front")(sel,W,vec,seg[:,None,:],seg[:,:,None])


ORDER=(('RO',3,),('YS',1,1,3,),('C',0,),('C',1,),('YS',1,1,0,),('YS',1,1,1,),('ZL',0,),('ZR',1,),('YS',1,0,2,),('RO',1,),('C',2,),('C',3,),('C',4,),('ZR',0,),('ZL',9,),('C',5,),('C',6,),('YS',1,1,2,),('ZL',11,),('YR',1,1,0,),('YS',1,0,1,),('C',7,),('ZR',2,),('C',8,),('C',9,),('ZR',4,),('YR',1,1,1,),('C',10,),('YR',1,0,2,),('ZL',8,),('YS',0,1,1,),('RO',0,),('YS',1,0,3,),('YS',0,1,3,),('YR',1,1,2,),('C',11,),('YS',0,1,2,),('YR',1,1,3,),('ZR',10,),('ZL',1,),('ZR',8,),('C',12,),('RO',2,),('C',13,),('C',14,),('YS',1,0,0,),('ZL',2,),('ZL',10,),('YR',0,1,1,),('C',15,),('C',16,),('ZL',3,),('ZR',11,),('ZL',5,),('C',17,),('YR',0,1,2,),('C',18,),('YS',0,1,0,),('C',19,),('ZL',7,),('YR',1,0,1,),('ZL',6,),('ZL',4,),('ZR',3,),('C',20,),('YS',0,0,0,),('C',21,),('ZR',6,),('YR',1,0,3,),('YS',0,0,2,),('YR',0,1,3,),('XR',1,3,),('YR',0,1,0,),('C',22,),('C',23,),('YS',0,0,1,),('ZR',9,),('LR',1,3,),('C',24,),('C',25,),('RG',1,),('ZR',7,),('RG',3,),('YR',1,0,0,),('XR',1,2,),('ZR',5,),('XR',1,1,),('VS',),('YS',0,0,3,),('XR',1,0,),('LR',1,2,),('YR',0,0,2,),('RG',0,),('LL',1,0,),('YR',0,0,0,),('YR',0,0,1,),('VM',),('XR',0,2,),('LR',0,2,),('XR',0,1,),('LL',0,2,),('RG',2,),('F2',1,0,),('LR',0,1,),('XR',0,0,),('F2',0,1,),('YR',0,0,3,),('LL',0,0,),('LL',0,1,),('XR',0,3,),('LL',1,1,),('F2',1,1,),('LL',1,2,),('F2',0,0,),('LR',1,1,),('LR',0,3,),('FY',1,),('FY',0,),('FIN',1,),('ST',1,),('FIN',0,),('ST',0,),('RF',),('FX',),('ST',2,))


EPS_SQUARE=1e-30; CLIP=0.3
ROW_CHUNKS=4
def back_kernel(order, nz, rp, nb, picks, G_ref, W_hbm, sel_hbm, P_hbm, probs_hbm, att_hbm, mid_hbm, accb_hbm, rows_hbm, gg_ref, vec_ref,
                w_ref, rold_ref, cold_ref, vold_ref, vmom_ref,
                Gs_ref, out_ref, grad_ref, R_ref, C_ref, S_ref, V_ref, vdir_ref,
                Pl, RC, RY, RX, RLy, RRy, RLz, RRz, Fy, Fx, gst,
                W0, sel, P, probs, att, mid, accb, acc, ga, gaT, nT, gatt, gob, rows,
                vin, vmp, cin, rin, sin, smp, rloc, cloc, sloc, vsend, small,
                loc, cS, cR, yS, yR, xS, xR, zS, zR, lS, lR, fS, fR, rS, rR, eS, eR):
    D=768; T=sel.shape[0]
    p=Plane()
    bpeers=[(lax.rem(p.b+k,nb),p.m) for k in range(1,nb)]
    mpeers=[(p.b,lax.rem(p.m+k,4)) for k in range(1,4)]
    bar=pltpu.get_barrier_semaphore()
    for d in bpeers+mpeers: pl.semaphore_signal(bar,inc=1,device_id=d,device_id_type=MESH)
    xo=1-p.x; yo=1-p.y; co=1-p.c
    loads={}
    def load(n,src,dst,k):
        loads[n]=pltpu.make_async_copy(src,dst,loc.at[k]); loads[n].start()
    own_blocks=[(i,x) for x in (0,1) for i in (2,1)]
    for k,(i,x) in enumerate(own_blocks): load((i,x),G_ref.at[i-1,x*2+p.c],Pl.at[i,x],k)
    for k,(n,src,dst) in enumerate([(0,accb_hbm,accb),(1,mid_hbm,mid),(2,sel_hbm,sel),(3,W_hbm.at[0],W0),(4,att_hbm,att),(5,P_hbm,P),(6,probs_hbm,probs)]):
        load(n,src,dst,4+k)
    pl.semaphore_wait(bar,nb-1+3)
    pend=[]
    def remote(src,dst,s,r,dev):
        return pltpu.make_async_remote_copy(src_ref=src,dst_ref=dst,send_sem=s,recv_sem=r,device_id=dev,device_id_type=MESH)
    def start(cp): cp.start(); pend.append((None,cp))
    def part(ref,b): return ref.at[pl.ds(pl.multiple_of(b*rp,rp),rp)]
    def shard(i,x,b): return Pl.at[i,x,pl.ds(pl.multiple_of(b*rp,rp),rp)]
    def add(dst,*src):
        @pl.loop(0,rp,step=32)
        def _(k):
            ks=pl.ds(pl.multiple_of(k,32),32)
            v=dst[ks].astype(F32)
            for q in src: v=v+q[ks].astype(F32)
            dst[ks]=v.astype(BF)
    def core_copy(i,x,src): return remote(src,RC.at[i,x],cS.at[i,x],cR.at[i,x],p.core)
    for (i,x) in own_blocks: start(core_copy(i,x,G_ref.at[i-1,x*2+co]))
    for (i,x) in own_blocks:
        loads[(i,x)].wait(); core_copy(i,x,gst.at[0]).wait_recv()
        dst=Pl.at[i,x]; src=RC.at[i,x]
        @pl.loop(0,D,step=32)
        def _(k):
            ks=pl.ds(pl.multiple_of(k,32),32)
            dst[ks]=(dst[ks].astype(F32)+src[ks].astype(F32)).astype(BF)
    ax=lambda xr: p.x if xr==0 else xo
    ay=lambda yr: p.y if yr==0 else yo
    def ys_copy(g,xr,z): return remote(shard(g,ax(xr),z*2+yo),RY.at[g,ax(xr),z],yS.at[g,xr,z],yR.at[g,ax(xr),z],p.ypeer)
    def xs_copy(g,z): return remote(shard(g,xo,z*2+p.y),RX.at[g,z],xS.at[g,z],xR.at[g,z],p.xpeer)
    def t_YS(g,xr,z): start(ys_copy(g,xr,z))
    def t_YR(g,xr,z):
        ys_copy(g,xr,z).wait_recv()
        add(shard(g,ax(xr),z*2+p.y),RY.at[g,ax(xr),z])
        if xr==1: start(xs_copy(g,z))
    def t_XR(g,z):
        xs_copy(g,z).wait_recv(); add(shard(g,p.x,z*2+p.y),RX.at[g,z])
    def guarded(cond,cp,more,recv,dst):
        @pl.when(cond)
        def _():
            @pl.when(more)
            def _(): cp.wait_recv(); add(dst,recv)
            cp.start()
        pend.append((cond,cp))
    def t_LR(g,t):
        cp=remote(shard(g,p.x,t*2+p.y),RLy.at[g,t],lS.at[g,0,t],lR.at[g,0,t],p.right)
        guarded(p.z<t,cp,p.z>0,RLy.at[g,t],shard(g,p.x,t*2+p.y))
    def t_LL(g,t):
        cp=remote(shard(g,p.x,t*2+p.y),RRy.at[g,t],lS.at[g,1,t],lR.at[g,1,t],p.left)
        guarded(p.z>t,cp,p.z<nz-1,RRy.at[g,t],shard(g,p.x,t*2+p.y))
    def t_ZR(k):
        t=nz-1-k//4; c=k%4; sh=shard(2,c//2,t*2+c%2)
        cp=remote(sh,RLz.at[c,t],zS.at[c,0,t],zR.at[c,0,t],p.right)
        guarded(p.z<t,cp,p.z>0,RLz.at[c,t],sh)
    def t_ZL(k):
        t=k//4; c=k%4; sh=shard(2,c//2,t*2+c%2)
        cp=remote(sh,RRz.at[c,t],zS.at[c,1,t],zR.at[c,1,t],p.left)
        guarded(p.z>t,cp,p.z<nz-1,RRz.at[c,t],sh)
    def last(RL,RR,rl,rr,dst):
        @pl.when(p.z>0)
        def _(): rl.wait_recv(); add(dst,RL)
        @pl.when(p.z<nz-1)
        def _(): rr.wait_recv(); add(dst,RR)
    def fy_copy(xr): return remote(shard(2,ax(xr),p.z*2+yo),Fy.at[ax(xr)],fS.at[0,xr],fR.at[0,ax(xr)],p.ypeer)
    def fx_copy(): return remote(shard(2,xo,p.b),Fx,fS.at[1,0],fR.at[1,0],p.xpeer)
    def t_F2(xr,yr):
        c=ax(xr)*2+ay(yr); sh=shard(2,ax(xr),p.z*2+ay(yr))
        rl=remote(sh,RLz.at[c,p.z],zS.at[0,0,0],zR.at[c,0,p.z],p.right)
        rr=remote(sh,RRz.at[c,p.z],zS.at[0,1,0],zR.at[c,1,p.z],p.left)
        last(RLz.at[c,p.z],RRz.at[c,p.z],rl,rr,sh)
        if yr==1: start(fy_copy(xr))
    def t_FY(xr):
        fy_copy(xr).wait_recv(); add(shard(2,ax(xr),p.b),Fy.at[ax(xr)])
        if xr==1: start(fx_copy())
    def t_FX():
        fx_copy().wait_recv()
        Gs_ref[2]=shard(2,p.x,p.b)[...].astype(F32)+Fx[...].astype(F32)
    def t_FIN(g):
        sh=shard(g,p.x,p.b)
        Gs_ref[g]=sh[...].astype(F32)
        @pl.when(p.z>0)
        def _():
            remote(sh,RLy.at[g,p.z],lS.at[g,0,0],lR.at[g,0,p.z],p.right).wait_recv()
            Gs_ref[g]+=RLy[g,p.z].astype(F32)
        @pl.when(p.z<nz-1)
        def _():
            remote(sh,RRy.at[g,p.z],lS.at[g,1,0],lR.at[g,1,p.z],p.left).wait_recv()
            Gs_ref[g]+=RRy[g,p.z].astype(F32)
    ch=T//ROW_CHUNKS
    def row_copy(k,q):
        src,dst=((rows_hbm,out_ref),(rows,grad_ref))[k]
        return remote(src.at[pl.ds(q*ch,ch)],dst.at[p.m,pl.ds(q*ch,ch)],rS.at[k,q],rR.at[k,q],p.xpeer)
    xm=xo*2+p.c
    def core_rows(k):
        src,dst=((rows_hbm,out_ref),(rows,grad_ref))[k]
        return remote(src,dst.at[p.m],rS.at[k,4],rR.at[k,4],p.core),pltpu.make_async_copy(src,dst.at[p.m],loc.at[11+k])
    def fwd_rows(k):
        dst=(out_ref,grad_ref)[k]
        return remote(dst.at[xm],dst.at[xm],rS.at[k,5],rR.at[k,5],p.core)
    def t_RO(q):
        start(row_copy(0,q))
        if q==0:
            cp,lc=core_rows(0); start(cp); lc.start()
    def t_RG(q):
        start(row_copy(1,q))
        if q==0:
            cp,lc=core_rows(1); start(cp); lc.start()
    def t_RF():
        for k in range(2):
            for q in range(ROW_CHUNKS): row_copy(k,q).wait_recv()
            start(fwd_rows(k))
    router,gain0,gain1=vectors(vec_ref)
    scale=HD**-0.5
    ms=[xo*2+co,xo*2+p.c,p.x*2+co,p.x*2+p.c]
    keep={}
    def gate_of(): return jax.nn.sigmoid(jnp.sum(sel[:,0:D].astype(F32)*router,axis=1,keepdims=True))
    def back(e,gain,scaled,iv):
        eg=e*gain
        return iv*(eg-scaled*jnp.mean(eg*scaled,axis=1,keepdims=True)),jnp.sum(e*scaled,axis=0,keepdims=True)
    def c_first():
        for n in (0,1,2): loads[n].wait()
        iv=root(mid[...])
        gmid,g1=back(accb[...],gain1,mid[...]*iv,iv)
        small[2:3,:]=g1
        mid[...]=gmid
        gv=(gmid+gate_of()*sel[:,D:].astype(F32)).astype(BF)
        ga[...]=gv
        gaT[...]=gv.T
        xv=sel[:,0:D].astype(F32)
        nT[...]=(xv*root(xv)*gain0).astype(BF).T
        acc[...]=jnp.zeros_like(acc)
        for n in (3,4,5,6): loads[n].wait()
    def c_out(mi):
        m=ms[mi]
        gatt[...]=nn(ga[...],W0[m,:,576:768]).astype(BF)
        gob[...]=nn(gaT[...],att[m])
    def c_head(mi,j):
        m=ms[mi]; o=j*HD
        @pl.loop(0,T//picks)
        def _(r):
            rs=pl.ds(pl.multiple_of(r*picks,picks),picks)
            q=P[m,rs,o:o+HD]; k=P[m,rs,192+o:192+o+HD]; v=P[m,rs,384+o:384+o+HD]
            g=gatt[rs,o:o+HD]
            pr=probs[r,m,j]
            gp=nt(g,v)
            pf=pr.astype(F32)
            ds=(pf*(gp-jnp.sum(pf*gp,axis=1,keepdims=True))).astype(BF)
            P[m,rs,o:o+HD]=(nn(ds,k)*scale).astype(BF)
            P[m,rs,192+o:192+o+HD]=(tn(ds,q)*scale).astype(BF)
            P[m,rs,384+o:384+o+HD]=tn(pr,g).astype(BF)
    def c_block(mi):
        m=ms[mi]; x=(xo,xo,p.x,p.x)[mi]
        g=nn(nT[...],P[m,:,0:576])
        if mi%2==0:
            s=mi//2
            gst[s,:,0:576]=g.astype(BF); gst[s,:,576:768]=gob[...].astype(BF)
            start(core_copy(0,x,gst.at[s]))
        else:
            core_copy(0,x,gst.at[0]).wait_recv()
            Pl[0,x,:,0:576]=(g+RC[0,x,:,0:576].astype(F32)).astype(BF)
            Pl[0,x,:,576:768]=(gob[...]+RC[0,x,:,576:768].astype(F32)).astype(BF)
    def c_norm(mi):
        m=ms[mi]
        acc[...]+=nt(P[m,:,0:576],W0[m,:,0:576])
    vcs=[]
    def c_last():
        xv=sel[:,0:D].astype(F32); gate=gate_of()
        glog=gg_ref[...]*gate*(1.0-gate)
        iv=root(xv)
        gin,g0=back(acc[...],gain0,xv*iv,iv)
        small[0:1,:]=jnp.sum(glog*xv,axis=0,keepdims=True)
        small[1:2,:]=g0
        small[3:8,:]=jnp.zeros((5,D),F32)
        rows[...]=(sel[:,D:].astype(F32)+mid[...]+gin+glog*router).astype(BF)
        n=D//nb
        for k in range(nb):
            vsend[k]=jnp.concatenate([small[:,k*n:(k+1)*n],jnp.zeros((8,128-n),F32)],axis=1)
        for k,d in enumerate(bpeers):
            cp=remote(vsend.at[d[0]],vin.at[k],eS.at[0,k],eR.at[0,k],d); start(cp); vcs.append(cp)
    def t_C(i):
        if i==0: c_first()
        elif i<=20:
            mi,k=divmod(i-1,5)
            if k==0: c_out(mi)
            elif k<4: c_head(mi,k-1)
            else: c_block(mi)
        elif i<=24: c_norm(i-21)
        else: c_last()
    table=dict(YS=t_YS,YR=t_YR,XR=t_XR,LR=t_LR,LL=t_LL,ZR=t_ZR,ZL=t_ZL,F2=t_F2,FY=t_FY,FX=t_FX,FIN=t_FIN,RO=t_RO,RG=t_RG,RF=t_RF,C=t_C)
    lanes=lax.broadcasted_iota(jnp.int32,(8,128),1); sub=lax.broadcasted_iota(jnp.int32,(8,128),0)
    keep["tile"]=jnp.zeros((8,128),F32)
    def put(lane,val): keep["tile"]=keep["tile"]+jnp.where((lanes==lane)&(sub==0),val,0.0)
    def tot(v): return jnp.sum(jnp.sum(v,axis=1,keepdims=True),axis=0,keepdims=True)
    def blocks(i): return [(j,slice(j*192,(j+1)*192)) for j in range(4)] if i==0 else [(3+i,slice(0,D))]
    rlane=lax.broadcasted_iota(jnp.int32,(rp,128),1)
    def t_VS():
        for cp in vcs: cp.wait_recv()
        vs=vsend[p.b]
        for k in range(nb-1): vs=vs+vin[k]
        vsend[p.b]=vs
        keep["vms"]=[]
        for k,d in enumerate(mpeers):
            cp=remote(vsend.at[p.b],vmp.at[k],eS.at[1,k],eR.at[1,k],d); start(cp); keep["vms"].append(cp)
        for i in range(3):
            for (j,s) in blocks(i):
                wv=w_ref[i,:,s].astype(F32); put(12+j,tot(wv*wv))
        for j in range(3):
            wv=vold_ref[j:j+1,:]; put(18+j,tot(wv*wv)*0.25)
    def t_VM():
        for cp in keep["vms"]: cp.wait_recv()
        vs=vsend[p.b]
        for k in range(3): vs=vs+vmp[k]
        V_ref[0:8,:]=vs
        mom=0.5*vmom_ref[...]+0.5*(vs*vs+EPS_SQUARE)
        V_ref[8:16,:]=mom
        vd=jnp.where(lanes<D//nb,vs*lax.rsqrt(mom),0.0)
        vdir_ref[...]=vd
        for j in range(3): put(21+j,tot(vd[j:j+1]*vd[j:j+1])*0.25)
        cloc[3:8,:]=jnp.zeros((5,D),F32)
        rloc[...]=jnp.zeros_like(rloc)
    def t_ST(i):
        sq=Gs_ref[i]; sq=sq*sq+EPS_SQUARE
        for (j,s) in blocks(i): rloc[...]+=jnp.where(rlane==j,jnp.sum(sq[:,s],axis=1,keepdims=True),0.0)
        cloc[i:i+1,:]=jnp.sum(sq,axis=0,keepdims=True)
    table.update(VS=t_VS,VM=t_VM,ST=t_ST)
    for n in order: table[n[0]](*n[1:])
    ccs=[];rcs=[]
    for k,d in enumerate(bpeers):
        cp=remote(cloc,cin.at[k],eS.at[2,k],eR.at[2,k],d); start(cp); ccs.append(cp)
    for k,d in enumerate(mpeers):
        cp=remote(rloc,rin.at[k],eS.at[3,k],eR.at[3,k],d); start(cp); rcs.append(cp)
    for cp in rcs: cp.wait_recv()
    rs=rloc[...]+rin[0]+rin[1]+rin[2]
    ncol=jnp.where(rlane>=4,1.0/3072.0,1.0/768.0)
    rnew=0.5*rold_ref[...]+0.5*rs*ncol
    R_ref[...]=rnew
    for cp in ccs: cp.wait_recv()
    cs=cloc[...]
    for k in range(nb-1): cs=cs+cin[k]
    cnew=0.5*cold_ref[...]+0.5*cs*(1.0/768.0)
    C_ref[...]=cnew
    for i in range(3):
        g=Gs_ref[i]; g2=g*g/cnew[i:i+1,:]
        for (j,s) in blocks(i):
            put(6+j,tot(jnp.sum(g2[:,s],axis=1,keepdims=True)/rnew[:,j:j+1]))
    for j in (0,1,2,4): put(j,tot(rnew[:,j:j+1])*(1.0/(768*4)))
    put(3,tot(cnew[0:1,576:768])*(1.0/(768*nb)))
    put(5,tot(cnew[2:3,:])*(1.0/(3072*nb)))
    tile=keep["tile"]
    sloc[0]=tile
    scs=[]
    for k,d in enumerate(bpeers):
        cp=remote(sloc.at[0],sin.at[k],eS.at[4,k],eR.at[4,k],d); start(cp); scs.append(cp)
    for cp in scs: cp.wait_recv()
    for k in range(nb-1): tile=tile+sin[k]
    sloc[1]=tile
    scs=[]
    for k,d in enumerate(mpeers):
        cp=remote(sloc.at[1],smp.at[k],eS.at[5,k],eR.at[5,k],d); start(cp); scs.append(cp)
    for cp in scs: cp.wait_recv()
    for k in range(3): tile=tile+smp[k]
    out=jnp.zeros((8,128),F32)
    for j in range(9):
        n=768.0*768.0 if j<4 else (768.0*3072.0 if j<6 else 768.0)
        if j<6:
            mean=tile[0:1,j:j+1]; us=mean*tile[0:1,6+j:7+j]/n; ws=tile[0:1,12+j:13+j]/n
        else:
            mean=jnp.ones((1,1),F32); us=tile[0:1,15+j:16+j]/n; ws=tile[0:1,12+j:13+j]/n
        urms=jnp.sqrt(us)
        coef=jnp.sqrt(ws)/jnp.maximum(1.0,urms/CLIP)*jnp.sqrt(mean)
        out=out+jnp.where((lanes==j)&(sub==0),urms,0.0)+jnp.where((lanes==j)&(sub==1),coef,0.0)
    S_ref[...]=out
    for k in range(2):
        cp,lc=core_rows(k); cp.wait_recv(); lc.wait(); fwd_rows(k).wait_recv()
    for cond,cp in pend:
        if cond is None: cp.wait_send()
        else:
            @pl.when(cond)
            def _(): cp.wait_send()
def back_call(G,W,sel,P,probs,att,mid,accb,rows,gg,vec,w,rold,cold,vold,vmom,nb,picks):
    D=768; nz=nb//2; rp=w.shape[1]; T=rows.shape[0]; R=T//picks
    V=pltpu.VMEM; S=pltpu.SemaphoreType.DMA
    vm=pl.BlockSpec(memory_space=V); an=pl.BlockSpec(memory_space=pl.ANY)
    sd=jax.ShapeDtypeStruct
    order=[n for n in ORDER]
    return pl.pallas_call(functools.partial(back_kernel,order,nz,rp,nb,picks),
        out_shape=(sd((3,rp,D),F32),sd((4,T,D),BF),sd((4,T,D),BF),sd((rp,128),F32),sd((8,D),F32),sd((8,128),F32),sd((16,128),F32),sd((8,128),F32)),
        in_specs=[an]*9+[vm]*7,out_specs=(vm,an,an)+(vm,)*5,
        scratch_shapes=[V((3,2,D,D),BF),V((3,2,D,D),BF),V((2,2,nz,rp,D),BF),V((2,nz,rp,D),BF),V((2,nz,rp,D),BF),V((2,nz,rp,D),BF),
            V((4,nz,rp,D),BF),V((4,nz,rp,D),BF),V((2,rp,D),BF),V((rp,D),BF),V((2,D,D),BF),
            V((4,D,D),BF),V((T,2*D),BF),V((4,T,D),BF),V((R,4,3,picks,picks),BF),V((4,T,192),BF),V((T,D),F32),V((T,D),F32),V((T,D),F32),
            V((T,D),BF),V((D,T),BF),V((D,T),BF),V((T,192),BF),V((D,192),F32),V((T,D),BF),
            V((nb,8,128),F32),V((3,8,128),F32),V((nb,8,D),F32),V((3,rp,128),F32),
            V((nb,8,128),F32),V((3,8,128),F32),V((rp,128),F32),V((8,D),F32),V((2,8,128),F32),V((nb,8,128),F32),V((8,D),F32),
            S((13,)),S((3,2)),S((3,2)),S((2,2,nz)),S((2,2,nz)),S((2,nz)),S((2,nz)),S((4,2,nz)),S((4,2,nz)),S((2,2,nz)),S((2,2,nz)),
            S((2,2)),S((2,2)),S((2,6)),S((2,6)),S((6,nb)),S((6,nb))],
        compiler_params=pltpu.CompilerParams(collective_id=1,has_side_effects=True,vmem_limit_bytes=58<<20),
        name="back")(G,W,sel,P,probs,att,mid,accb,rows,gg,vec,w,rold,cold,vold,vmom)


BF=jnp.bfloat16; F32=jnp.float32; D=768
def place_kernel(tok_ref, cot_ref, rows_ref, grads_ref, sel_ref, G_ref, w_ref, vold_ref, R_ref, C_ref, S_ref, V_ref, vdir_ref,
                 bo_ref, ig_ref, qg, qr, qc, qn, og, orr, oc, on, ug, ur, uc, un, dgr, dr, dc, dn, rg, rm, rn, gg, gmo, gn):
    length=tok_ref.shape[1]; picks=rows_ref.shape[1]
    pos=lax.broadcasted_iota(jnp.int32,(length,picks),0)
    hot=(pos==sel_ref[0]).astype(F32)
    cover=jnp.sum(hot,axis=1,keepdims=True)>0.5
    hot=hot.astype(BF)
    bo_ref[0]=jnp.where(cover,jnp.dot(hot,rows_ref[0],preferred_element_type=F32),tok_ref[0].astype(F32)).astype(BF)
    ig_ref[0]=jnp.where(cover,jnp.dot(hot,grads_ref[0],preferred_element_type=F32),cot_ref[0].astype(F32))
    @pl.when(pl.program_id(0)==0)
    def _():
        def new(i,s,j):
            g=G_ref[i,:,s]
            return g,w_ref[i,:,s].astype(F32)-S_ref[1:2,j:j+1]*(g*lax.rsqrt(R_ref[:,j:j+1]*C_ref[i:i+1,s]))
        for j in range(3):
            qg[j],qn[j]=new(0,slice(j*192,(j+1)*192),j)
            qc[j:j+1,:]=C_ref[0:1,j*192:(j+1)*192]
        g,n=new(0,slice(576,768),3); og[...]=g.T; on[...]=n.T
        g,n=new(1,slice(0,D),4); ug[...]=g; un[...]=n
        g,n=new(2,slice(0,D),5); dgr[...]=g.T; dn[...]=n.T
        Rt=R_ref[...].T
        qr[...]=Rt[0:3]; oc[...]=Rt[3:4]; ur[...]=Rt[4:5]; dc[...]=Rt[5:6]
        orr[...]=C_ref[0:1,576:768]; uc[...]=C_ref[1:2,:]; dr[...]=C_ref[2:3,:]
        rg[...]=V_ref[0:1,0:96]; gg[...]=V_ref[1:3,0:96]
        rm[...]=V_ref[8:9,0:96]; gmo[...]=V_ref[9:11,0:96]
        rn[...]=vold_ref[0:1,0:96]-S_ref[1:2,6:7]*vdir_ref[0:1,0:96]
        gn[0:1,:]=vold_ref[1:2,0:96]-S_ref[1:2,7:8]*vdir_ref[1:2,0:96]
        gn[1:2,:]=vold_ref[2:3,0:96]-S_ref[1:2,8:9]*vdir_ref[2:3,0:96]
def place_call(tokens,cot,allrows,allgrads,selrel,G,w,vold,R,C,S,V,vdir):
    rows,length,_=tokens.shape; picks=selrel.shape[2]
    allrows=allrows.reshape(rows,picks,D); allgrads=allgrads.reshape(rows,picks,D)
    sd=lambda *s: jax.ShapeDtypeStruct(s,F32)
    rp=w.shape[1]
    row=lambda *s: pl.BlockSpec((1,)+s,lambda i:(i,0,0))
    def whole(s):
        n=len(s); return pl.BlockSpec(s,lambda i:(0,)*n)
    small=[(3,rp,192),(3,rp),(3,192),(3,rp,192),(192,rp),(1,192),(1,rp),(192,rp),(rp,D),(1,rp),(1,D),(rp,D),(D,rp),(1,D),(1,rp),(D,rp),(1,rp),(1,rp),(1,rp),(2,rp),(2,rp),(2,rp)]
    return pl.pallas_call(place_kernel,grid=(rows,),
        out_shape=(jax.ShapeDtypeStruct(tokens.shape,BF),jax.ShapeDtypeStruct(cot.shape,F32))+tuple(sd(*s) for s in small),
        in_specs=[row(length,D),row(length,D),row(picks,D),row(picks,D),row(1,picks)]+[whole(a.shape) for a in (G,w,vold,R,C,S,V,vdir)],
        out_specs=(row(length,D),row(length,D))+tuple(whole(s) for s in small),
        compiler_params=pltpu.CompilerParams(vmem_limit_bytes=48<<20),
        name="place")(tokens,cot,allrows,allgrads,selrel,G,w,vold,R,C,S,V,vdir)


def tile_of(rows,height,width):
    padded=[jnp.pad(r.astype(F32),((0,0),(0,width-r.shape[1]))) for r in rows]
    v=jnp.concatenate(padded,axis=0)
    return jnp.pad(v,((0,height-v.shape[0]),(0,0)))

def local_fast(tokens,segments,selection,cotangent,qkv_weight,out_weight,up_weight,down_weight,router_weight,norm_gains,
               qkv_rows,qkv_cols,out_rows,out_cols,up_rows,up_cols,down_rows,down_cols,router_moment,gains_moment):
    nb=lax.axis_size("batch"); m=lax.axis_index("mp")
    length=tokens.shape[1]; picks=selection.shape[1]; rows=tokens.shape[0]; per=rows//4
    w=jnp.stack([jnp.concatenate([qkv_weight[0],qkv_weight[1],qkv_weight[2],out_weight.T],axis=1),up_weight,down_weight.T])
    vold=tile_of([router_weight[None],norm_gains],8,128)
    vmom=tile_of([router_moment[None],gains_moment],8,128)
    rold=tile_of([qkv_rows,out_cols[None],up_rows[None],down_cols[None]],128,qkv_rows.shape[1]).T
    cold=tile_of([qkv_cols.reshape(1,-1),],1,768)
    cold=tile_of([jnp.concatenate([qkv_cols.reshape(1,-1),out_rows[None]],axis=1),up_cols[None],down_rows[None]],8,768)
    mine=lax.dynamic_slice_in_dim(selection,m*per,per,0)
    segs=lax.dynamic_slice_in_dim(segments,m*per,per,0)
    begin=jnp.sum(segs[:,:,None]<jnp.arange(1,8)[None,None,:],axis=1)
    seg=jnp.sum(mine[:,:,None]>=begin[:,None,:],axis=2).astype(jnp.int32)
    W,sel,vall=gather_call(w,vold,tokens,cotangent,selection[:,:,None],nb,picks)
    G,projected,probs,attended,middle,grad_mid,rows_low,grad_gate=front_call(sel,W,vall,seg,picks)
    Gs,allrows,allgrads,R,C,S,V,vdir=back_call(G,W,sel,projected,probs,attended,middle,grad_mid,rows_low,grad_gate,vall,w,rold,cold,vold,vmom,nb,picks)
    (bo,ig,qg,qr,qc,qn,og,orr,oc,on,ug,ur,uc,un,dgr,dr,dc,dn,rg,rm,rn,gg,gmo,gn)=place_call(
        tokens,cotangent,allrows,allgrads,(selection-m*length)[:,None,:],Gs,w,vold,R,C,S,V,vdir)
    return (bo,ig,qg,qr,qc,qn,og,orr[0],oc[0],on,ug,ur[0],uc[0],un,dgr,dr[0],dc[0],dn,rg[0],rm[0],rn[0],gg,gmo,gn,S[0,:9])

def chosen_local(mesh):
    return local_fast if (mesh.shape["batch"],mesh.shape["mp"])==(8,4) else local_any


def solution(mesh):
    in_specs = (
        P("batch", "mp", None),
        P("batch", None),
        P("batch", None),
        P("batch", "mp", None),
        P(None, "batch", "mp"),
        P("mp", "batch"),
        P("batch", "mp"),
        P("mp", "batch"),
        P("batch"),
        P(None, "batch"),
        P(None, "batch"),
        P(None, "mp"),
        P("mp"),
        P("batch"),
        P("batch"),
        P("mp"),
        P("mp"),
        P("batch"),
        P("batch"),
        P(None, "batch"),
    )
    out_specs = (
        P("batch", "mp", None),
        P("batch", "mp", None),
        P(None, "batch", "mp"),
        P(None, "batch"),
        P(None, "mp"),
        P(None, "batch", "mp"),
        P("mp", "batch"),
        P("mp"),
        P("batch"),
        P("mp", "batch"),
        P("batch", "mp"),
        P("batch"),
        P("mp"),
        P("batch", "mp"),
        P("mp", "batch"),
        P("mp"),
        P("batch"),
        P("mp", "batch"),
        P("batch"),
        P("batch"),
        P("batch"),
        P(None, "batch"),
        P(None, "batch"),
        P(None, "batch"),
        P(),
    )
    return jax.shard_map(chosen_local(mesh), mesh=mesh, in_specs=in_specs, out_specs=out_specs, check_vma=False)
```

```python
import functools

import jax
import jax.numpy as jnp
from jax import lax
from jax.experimental import pallas as pl
from jax.experimental.pallas import tpu as pltpu
from jax.sharding import PartitionSpec as P


D = 768
HEAD_DIM = 64
FF = 3072
MICRO = 2


EPS_NORM = 1e-06
EPS_SQUARE = 1e-30
DECAY = 0.5
CLIP_RMS = 0.3
RATE = 1.0
MASKED = -1e30


def rms_parts(values):
    inverse = lax.rsqrt(jnp.mean(values * values, axis=1, keepdims=True) + EPS_NORM)
    return (values * inverse, inverse)


def norm_back(grad_norm, gain_vec, scaled, inverse):
    grad_scaled = grad_norm * gain_vec
    grad_input = inverse * (
        grad_scaled - scaled * jnp.mean(grad_scaled * scaled, axis=1, keepdims=True)
    )
    return (grad_input, jnp.sum(grad_norm * scaled, axis=0))


def spread_into(values, index, pieces):
    size_piece = values.shape[-1]
    shape_full = values.shape[:-1] + (size_piece * pieces,)
    return lax.dynamic_update_slice_in_dim(
        jnp.zeros(shape_full, jnp.float32), values, index * size_piece, values.ndim - 1
    )


def own_piece(values, index, size_piece):
    return lax.dynamic_slice_in_dim(values, index * size_piece, size_piece, values.ndim - 1)


def factor_terms(gradient, row_old, col_old, row_index, row_count, col_index, col_count):
    square = gradient * gradient + EPS_SQUARE
    rows_here, cols_here = gradient.shape[-2:]
    row_term = (1.0 - DECAY) * jnp.sum(square, axis=-1) / (
        cols_here * col_count
    ) + DECAY * row_old * (col_index == 0)
    col_term = (1.0 - DECAY) * jnp.sum(square, axis=-2) / (
        rows_here * row_count
    ) + DECAY * col_old * (row_index == 0)
    return (
        spread_into(row_term, row_index, row_count),
        spread_into(col_term, col_index, col_count),
    )


def factor_direction(gradient, row_full, col_full, row_index, col_index):
    rows_here, cols_here = gradient.shape[-2:]
    row_mine = own_piece(row_full, row_index, rows_here)
    col_mine = own_piece(col_full, col_index, cols_here)
    mean_row = jnp.mean(row_full, axis=-1)[..., None, None]
    second = row_mine[..., :, None] * col_mine[..., None, :] / mean_row
    return (gradient * lax.rsqrt(second), row_mine, col_mine)


def local_any(
    tokens,
    segments,
    selection,
    cotangent,
    qkv_weight,
    out_weight,
    up_weight,
    down_weight,
    router_weight,
    norm_gains,
    qkv_rows,
    qkv_cols,
    out_rows,
    out_cols,
    up_rows,
    up_cols,
    down_rows,
    down_cols,
    router_moment,
    gains_moment,
):
    qkv_all, out_all, up_all, down_all, router_all, gains_all = (
        lax.all_gather(qkv_weight, "batch", axis=1, tiled=True),
        lax.all_gather(out_weight, "batch", axis=1, tiled=True),
        lax.all_gather(up_weight, "batch", axis=0, tiled=True),
        lax.all_gather(down_weight, "batch", axis=1, tiled=True),
        lax.all_gather(router_weight, "batch", axis=0, tiled=True),
        lax.all_gather(norm_gains, "batch", axis=1, tiled=True),
    )
    mp_index = lax.axis_index("mp")
    mp_count = lax.axis_size("mp")
    batch_index = lax.axis_index("batch")
    batch_count = lax.axis_size("batch")
    rows_dev, length_here, width_full = tokens.shape
    width_local = width_full // mp_count
    heads_local = qkv_all.shape[2] // HEAD_DIM
    per_micro = rows_dev // MICRO
    score_scale = HEAD_DIM ** (-0.5)
    gain_attn = gains_all[0].astype(jnp.float32)
    gain_mlp = gains_all[1].astype(jnp.float32)
    router_float = router_all.astype(jnp.float32)
    first_position = mp_index * length_here
    totals = None
    shards = None
    output_list = []
    grad_list = []
    for micro_index in range(MICRO):
        row_start = micro_index * per_micro
        row_stop = row_start + per_micro
        token_rows = tokens[row_start:row_stop]
        chosen = selection[row_start:row_stop]
        cot_rows = cotangent[row_start:row_stop]
        row_count, pick_count = chosen.shape
        token_count = row_count * pick_count
        local_position = chosen - first_position
        inside = (local_position >= 0) & (local_position < length_here)
        clipped = jnp.clip(local_position, 0, length_here - 1)
        zero_low = jnp.zeros((), jnp.bfloat16)
        token_term = jnp.where(
            inside[:, :, None],
            jnp.take_along_axis(token_rows, clipped[:, :, None], axis=1),
            zero_low,
        ).reshape(token_count, width_full)
        cot_term = jnp.where(
            inside[:, :, None], jnp.take_along_axis(cot_rows, clipped[:, :, None], axis=1), zero_low
        ).reshape(token_count, width_full)
        picked_float = lax.psum(token_term, "mp").astype(jnp.float32)
        cot_float = lax.psum(cot_term, "mp").astype(jnp.float32)
        picked_full = picked_float.astype(jnp.bfloat16)
        picked_local = lax.dynamic_slice_in_dim(picked_full, mp_index * width_local, width_local, 1)
        cot_local = lax.dynamic_slice_in_dim(cot_float, mp_index * width_local, width_local, 1)
        picked_segments = jnp.take_along_axis(segments[row_start:row_stop], chosen, axis=1)
        allowed = (chosen[:, None, None, :] <= chosen[:, None, :, None]) & (
            picked_segments[:, None, None, :] == picked_segments[:, None, :, None]
        )
        router_gate = jax.nn.sigmoid(
            jnp.dot(picked_full, router_all, preferred_element_type=jnp.float32)
        )
        scaled_attn, inverse_attn = rms_parts(picked_float)
        normed = (scaled_attn * gain_attn).astype(jnp.bfloat16)
        projected = jnp.einsum(
            "td,cde->cte", normed, qkv_all, preferred_element_type=jnp.float32
        ).astype(jnp.bfloat16)
        shaped = projected.reshape(3, row_count, pick_count, heads_local, HEAD_DIM)
        queries = shaped[0]
        key_rows = shaped[1]
        value_rows = shaped[2]
        scores = (
            jnp.einsum("rqhe,rkhe->rhqk", queries, key_rows, preferred_element_type=jnp.float32)
            * score_scale
        )
        masked = jnp.where(allowed, scores, MASKED)
        highest_score = jnp.max(masked, axis=-1, keepdims=True)
        exponent = jnp.exp(masked - highest_score)
        exp_total = jnp.sum(exponent, axis=-1, keepdims=True)
        log_total = highest_score + jnp.log(exp_total)
        attention_low = (exponent / exp_total).astype(jnp.bfloat16)
        attended = jnp.einsum(
            "rhqk,rkhe->rqhe", attention_low, value_rows, preferred_element_type=jnp.float32
        )
        attended = attended.reshape(token_count, heads_local * HEAD_DIM).astype(jnp.bfloat16)
        attn_local = lax.psum_scatter(
            jnp.dot(attended, out_all, preferred_element_type=jnp.float32),
            "mp",
            scatter_dimension=1,
            tiled=True,
        )
        middle_local = picked_local.astype(jnp.float32) + attn_local
        middle = lax.all_gather(middle_local, "mp", axis=1, tiled=True)
        scaled_mlp, inverse_mlp = rms_parts(middle)
        normed_mid = (scaled_mlp * gain_mlp).astype(jnp.bfloat16)
        hidden = jnp.dot(normed_mid, up_all, preferred_element_type=jnp.float32)
        active = jax.nn.gelu(hidden).astype(jnp.bfloat16)
        mlp_local = lax.psum_scatter(
            jnp.dot(active, down_all, preferred_element_type=jnp.float32).astype(jnp.bfloat16),
            "mp",
            scatter_dimension=1,
            tiled=True,
        ).astype(jnp.float32)
        branch_local = attn_local + mlp_local
        output_local = (
            picked_local.astype(jnp.float32) + router_gate[:, None] * branch_local
        ).astype(jnp.bfloat16)
        output_full = lax.all_gather(output_local, "mp", axis=1, tiled=True)
        grad_gate = lax.psum(jnp.sum(cot_local * branch_local, axis=1), "mp")
        direct = router_gate[:, None] * cot_float
        grad_mlp = direct.astype(jnp.bfloat16)
        down_part = jnp.einsum("tf,td->fd", active, grad_mlp, preferred_element_type=jnp.float32)
        grad_active = jnp.einsum(
            "td,fd->tf", grad_mlp, down_all, preferred_element_type=jnp.float32
        )
        gelu_values, gelu_pull = jax.vjp(jax.nn.gelu, hidden)
        grad_hidden = gelu_pull(grad_active)[0].astype(jnp.bfloat16)
        up_part = jnp.einsum(
            "td,tf->df", normed_mid, grad_hidden, preferred_element_type=jnp.float32
        )
        grad_normed_mid = lax.psum(
            jnp.einsum("tf,df->td", grad_hidden, up_all, preferred_element_type=jnp.float32), "mp"
        )
        grad_middle, gain_mlp_part = norm_back(grad_normed_mid, gain_mlp, scaled_mlp, inverse_mlp)
        grad_attn = (grad_middle + direct).astype(jnp.bfloat16)
        out_part = jnp.einsum("te,td->ed", attended, grad_attn, preferred_element_type=jnp.float32)
        grad_attended = jnp.einsum(
            "td,ed->te", grad_attn, out_all, preferred_element_type=jnp.float32
        ).astype(jnp.bfloat16)
        grad_attended = grad_attended.reshape(row_count, pick_count, heads_local, HEAD_DIM)
        scores_again = (
            jnp.einsum("rqhe,rkhe->rhqk", queries, key_rows, preferred_element_type=jnp.float32)
            * score_scale
        )
        attention = jnp.exp(jnp.where(allowed, scores_again, MASKED) - log_total)
        grad_values = jnp.einsum(
            "rhqk,rqhe->rkhe",
            attention.astype(jnp.bfloat16),
            grad_attended,
            preferred_element_type=jnp.float32,
        )
        grad_weights = jnp.einsum(
            "rqhe,rkhe->rhqk", grad_attended, value_rows, preferred_element_type=jnp.float32
        )
        grad_scores = (
            attention * (grad_weights - jnp.sum(attention * grad_weights, axis=-1, keepdims=True))
        ).astype(jnp.bfloat16)
        grad_queries = (
            jnp.einsum("rhqk,rkhe->rqhe", grad_scores, key_rows, preferred_element_type=jnp.float32)
            * score_scale
        )
        grad_keys = (
            jnp.einsum("rhqk,rqhe->rkhe", grad_scores, queries, preferred_element_type=jnp.float32)
            * score_scale
        )
        grad_projected = (
            jnp.stack([grad_queries, grad_keys, grad_values])
            .reshape(3, token_count, heads_local * HEAD_DIM)
            .astype(jnp.bfloat16)
        )
        qkv_part = jnp.einsum(
            "td,cte->cde", normed, grad_projected, preferred_element_type=jnp.float32
        )
        grad_normed = lax.psum(
            jnp.einsum(
                "cte,cde->td", grad_projected, qkv_all, preferred_element_type=jnp.float32
            ).astype(jnp.bfloat16),
            "mp",
        ).astype(jnp.float32)
        grad_norm_in, gain_attn_part = norm_back(grad_normed, gain_attn, scaled_attn, inverse_attn)
        grad_logit = grad_gate * router_gate * (1.0 - router_gate)
        router_part = jnp.dot(grad_logit, picked_float, precision=lax.Precision.HIGHEST)
        grad_full = cot_float + grad_middle + grad_norm_in + grad_logit[:, None] * router_float
        row_positions = jnp.arange(row_count)[:, None]
        write_index = jnp.where(inside, local_position, length_here)
        output_rows = token_rows.at[row_positions, write_index].set(
            output_full.reshape(row_count, pick_count, width_full), mode="drop"
        )
        grad_rows = (
            cot_rows.astype(jnp.float32)
            .at[row_positions, write_index]
            .set(grad_full.reshape(row_count, pick_count, width_full), mode="drop")
        )
        gradients = (
            qkv_part,
            out_part,
            up_part,
            down_part,
            router_part,
            jnp.stack([gain_attn_part, gain_mlp_part]),
        )
        gradients, output_rows, grad_rows = (gradients, output_rows, grad_rows)
        output_list.append(output_rows)
        grad_list.append(grad_rows)
        totals = gradients if totals is None else jax.tree.map(jnp.add, totals, gradients)
    shards = (
        lax.psum_scatter(totals[0], "batch", scatter_dimension=1, tiled=True),
        lax.psum_scatter(totals[1], "batch", scatter_dimension=1, tiled=True),
        lax.psum_scatter(totals[2], "batch", scatter_dimension=0, tiled=True),
        lax.psum_scatter(totals[3], "batch", scatter_dimension=1, tiled=True),
        lax.psum_scatter(totals[4], "batch", scatter_dimension=0, tiled=True),
        lax.psum_scatter(totals[5], "batch", scatter_dimension=1, tiled=True),
    )
    block_output = jnp.concatenate(output_list, axis=0)
    input_grad = jnp.concatenate(grad_list, axis=0)
    qkv_grad, out_grad, up_grad, down_grad, router_grad, gains_grad = shards
    first_mp = (mp_index == 0).astype(jnp.float32)
    qkv_old = qkv_weight.astype(jnp.float32)
    out_old = out_weight.astype(jnp.float32)
    up_old = up_weight.astype(jnp.float32)
    down_old = down_weight.astype(jnp.float32)
    router_old = router_weight.astype(jnp.float32)
    gains_old = norm_gains.astype(jnp.float32)
    qkv_row_term, qkv_col_term = factor_terms(
        qkv_grad, qkv_rows, qkv_cols, batch_index, batch_count, mp_index, mp_count
    )
    out_row_term, out_col_term = factor_terms(
        out_grad, out_rows, out_cols, mp_index, mp_count, batch_index, batch_count
    )
    up_row_term, up_col_term = factor_terms(
        up_grad, up_rows, up_cols, batch_index, batch_count, mp_index, mp_count
    )
    down_row_term, down_col_term = factor_terms(
        down_grad, down_rows, down_cols, mp_index, mp_count, batch_index, batch_count
    )
    weight_squares = jnp.concatenate(
        [
            jnp.sum(qkv_old * qkv_old, axis=(1, 2)),
            jnp.stack(
                [
                    jnp.sum(out_old * out_old),
                    jnp.sum(up_old * up_old),
                    jnp.sum(down_old * down_old),
                    first_mp * jnp.sum(router_old * router_old),
                ]
            ),
            first_mp * jnp.sum(gains_old * gains_old, axis=1),
        ]
    )
    (
        qkv_row_full,
        qkv_col_full,
        out_row_full,
        out_col_full,
        up_row_full,
        up_col_full,
        down_row_full,
        down_col_full,
        weight_sums,
    ) = lax.psum(
        (
            qkv_row_term,
            qkv_col_term,
            out_row_term,
            out_col_term,
            up_row_term,
            up_col_term,
            down_row_term,
            down_col_term,
            weight_squares,
        ),
        ("batch", "mp"),
    )
    qkv_dir, qkv_rows_new, qkv_cols_new = factor_direction(
        qkv_grad, qkv_row_full, qkv_col_full, batch_index, mp_index
    )
    out_dir, out_rows_new, out_cols_new = factor_direction(
        out_grad, out_row_full, out_col_full, mp_index, batch_index
    )
    up_dir, up_rows_new, up_cols_new = factor_direction(
        up_grad, up_row_full, up_col_full, batch_index, mp_index
    )
    down_dir, down_rows_new, down_cols_new = factor_direction(
        down_grad, down_row_full, down_col_full, mp_index, batch_index
    )
    router_moment_new = DECAY * router_moment + (1.0 - DECAY) * (
        router_grad * router_grad + EPS_SQUARE
    )
    router_dir = router_grad * lax.rsqrt(router_moment_new)
    gains_moment_new = DECAY * gains_moment + (1.0 - DECAY) * (gains_grad * gains_grad + EPS_SQUARE)
    gains_dir = gains_grad * lax.rsqrt(gains_moment_new)
    update_squares = jnp.concatenate(
        [
            jnp.sum(qkv_dir * qkv_dir, axis=(1, 2)),
            jnp.stack(
                [
                    jnp.sum(out_dir * out_dir),
                    jnp.sum(up_dir * up_dir),
                    jnp.sum(down_dir * down_dir),
                    first_mp * jnp.sum(router_dir * router_dir),
                ]
            ),
            first_mp * jnp.sum(gains_dir * gains_dir, axis=1),
        ]
    )
    update_sums = lax.psum(update_squares, ("batch", "mp"))
    entries = jnp.array([D * D, D * D, D * D, D * D, D * FF, FF * D, D, D, D], jnp.float32)
    update_rms = jnp.sqrt(update_sums / entries)
    weight_rms = jnp.sqrt(weight_sums / entries)
    factors = RATE * weight_rms / jnp.maximum(1.0, update_rms / CLIP_RMS)
    qkv_new = qkv_old - factors[0:3, None, None] * qkv_dir
    out_new = out_old - factors[3] * out_dir
    up_new = up_old - factors[4] * up_dir
    down_new = down_old - factors[5] * down_dir
    router_new = router_old - factors[6] * router_dir
    gains_new = gains_old - factors[7:9, None] * gains_dir
    return (
        block_output,
        input_grad,
        qkv_grad,
        qkv_rows_new,
        qkv_cols_new,
        qkv_new,
        out_grad,
        out_rows_new,
        out_cols_new,
        out_new,
        up_grad,
        up_rows_new,
        up_cols_new,
        up_new,
        down_grad,
        down_rows_new,
        down_cols_new,
        down_new,
        router_grad,
        router_moment_new,
        router_new,
        gains_grad,
        gains_moment_new,
        gains_new,
        update_rms,
    )


BF=jnp.bfloat16; F32=jnp.float32
EPS_NORM=1e-6; MASKED=-1e30; HD=64
GC=0.7978845608028654; GA=0.044715
def nn(a,b): return jnp.dot(a,b,preferred_element_type=F32)
def nt(a,b): return lax.dot_general(a,b,(((1,),(1,)),((),())),preferred_element_type=F32)
def tn(a,b): return lax.dot_general(a,b,(((0,),(0,)),((),())),preferred_element_type=F32)
def vectors(vec_ref):
    nb=vec_ref.shape[0]
    vec=jnp.concatenate([vec_ref[b,:,0:768//nb] for b in range(nb)],axis=1)
    return vec[0:1,:],vec[1:2,:],vec[2:3,:]
def root(v): return lax.rsqrt(jnp.mean(v*v,axis=1,keepdims=True)+EPS_NORM)


MESH=pl.DeviceIdType.MESH
class Plane:
    def __init__(s):
        s.b=lax.axis_index("batch"); s.m=lax.axis_index("mp")
        s.z=s.b//2; s.y=lax.rem(s.b,2); s.x=s.m//2; s.c=lax.rem(s.m,2)
        s.left=(s.b-2,s.m); s.right=(s.b+2,s.m)
        s.ypeer=(s.z*2+1-s.y,s.m); s.xpeer=(s.b,(1-s.x)*2+s.c); s.core=(s.b,s.x*2+1-s.c)


FORE_ORDER=(('S',2,'X',),('S',0,'L',),('FY',0,0,2,0,),('FY',1,0,2,0,),('S',0,'R',),('S',2,'Z',),('PK',1,0,),('FX',0,2,0,),('PK',0,0,),('ZA',0,0,0,),('S',2,'Y',),('ZA',0,1,0,),('S',1,'L',),('S',1,'R',),('FX',0,0,0,),('FX',0,1,0,),('PK',1,1,),('YA',0,0,2,0,),('PK',0,1,),('PK',2,0,),('CMB',0,),('TX',0,1,),('FY',0,0,0,0,),('TX',0,0,),('ZA',0,0,1,),('YA',1,0,2,0,),('FY',0,0,1,0,),('FY',0,0,0,1,),('PK',2,1,),('ZA',1,0,0,),('ZA',0,1,1,),('XA2',2,),('FY',0,1,2,0,),('ZA',0,0,2,),('FY',0,0,1,1,),('FY',0,0,0,2,),('PK',3,1,),('ZA',1,1,0,),('FY',0,1,0,0,),('FX',0,0,2,),('ZA',1,0,1,),('FX',0,0,1,),('YA2',2,0,),('ZA',0,1,2,),('PK',3,0,),('FX',0,1,2,),('FY',0,1,1,0,),('CMB',1,),('YA',0,0,1,0,),('YA',0,0,0,1,),('YA',0,0,0,0,),('ZA2',2,1,0,0,0,),('ZA',1,0,2,),('FY',1,0,0,2,),('FX',0,1,1,),('FY',0,0,1,2,),('ZA',1,1,1,),('FX',1,0,2,),('TX',1,1,),('ZA2',2,0,0,0,0,),('FY',0,1,0,2,),('ZA2',2,1,0,1,0,),('YA2',2,1,),('YA',0,0,0,2,),('ZA2',2,0,1,0,0,),('TX',1,0,),('ZA2',2,0,0,1,0,),('SEL',0,),('ZA2',2,0,1,1,0,),('YA',0,0,1,2,),('YA',0,0,1,1,),('YA',0,1,2,0,),('FY',0,1,1,2,),('YA',0,1,0,0,),('NRM',),('QKV',0,),('FY',0,1,1,1,),('ZA',1,1,2,),('FY',0,1,0,1,),('FX',1,0,1,),('YA',1,0,0,2,),('FX',1,1,2,),('FX',1,1,1,),('FX',1,2,0,),('ZA2',2,1,0,0,1,),('FY',1,0,1,2,),('QKV',1,),('FY',1,0,0,0,),('FY',1,1,0,2,),('YA',0,1,1,2,),('FY',1,0,0,1,),('YA',0,1,1,0,),('ZA2',2,1,0,1,1,),('FY',1,0,1,1,),('HD',1,),('ZA2',2,1,1,0,0,),('ZA2',2,1,1,1,0,),('YA',0,1,0,1,),('FX',1,0,0,),('YA',0,1,1,1,),('ZA2',2,0,0,0,1,),('FX',1,1,0,),('FY',1,0,1,0,),('YA',0,1,0,2,),('HD',0,),('ZA2',2,0,0,1,1,),('QKV',3,),('QKV',2,),('ZA2',2,0,1,1,1,),('HD',3,),('HD',2,),('OUT',),('YA',1,0,0,1,),('ZA2',2,0,1,0,1,),('YA',1,1,0,2,),('YA',1,0,0,0,),('FY',1,1,1,2,),('SEL',1,),('YA',1,0,1,2,),('YA',1,0,1,0,),('ZA2',2,0,0,1,2,),('ZA2',2,1,1,1,1,),('ZA2',2,0,1,0,2,),('ZA2',2,0,0,0,2,),('FY',1,1,1,1,),('ZA2',2,1,1,0,1,),('YA',1,0,1,1,),('ZA2',2,0,1,1,2,),('GM',),('FY',1,1,0,1,),('ML',0,0,),('FY',1,1,2,0,),('ML',0,1,),('YA',1,1,0,1,),('ZA2',2,1,0,0,2,),('ZA2',2,1,0,1,2,),('YA',1,1,1,2,),('ZA2',2,1,1,0,2,),('FY',1,1,0,0,),('YA',1,1,1,1,),('ZA2',2,1,1,1,2,),('FY',1,1,1,0,),('ML',1,0,),('ML',1,1,),('YA',1,1,0,0,),('YA',1,1,1,0,),('YA',1,1,2,0,),('ML',2,0,),('ML',2,1,),('ML',3,0,),('ML',3,1,),('END',))


def fore_kernel(order, nz, rp, picks, w_ref, v_ref, tok_ref, cot_ref, selc_ref, seg_ref, segc_ref,
                W0_out, Gown, Gpart, sel_out, P_out, probs_out, att_out, mid_out, accb_out, rows_out, gg_ref, vall_ref,
                W, tokb, cotb, zbuf, ra, rb, rx, normed, P, probs, att, mid, ba, nm, gm, act, gh, acc, accb, nmT, gmT, gst,
                tsem, csem, rsem, ssem, shS, shR, txS, txR, vs, vr, gS, gR, gL, osem):
    D=768; nb=2*nz; T=nm.shape[0]; length=tok_ref.shape[1]; R=T//picks
    p=Plane()
    bpeers=[(lax.rem(p.b+k,nb),p.m) for k in range(1,nb)]
    peers=bpeers+[p.xpeer,p.core]
    bar=pltpu.get_barrier_semaphore()
    for d in peers: pl.semaphore_signal(bar,inc=1,device_id=d,device_id_type=MESH)
    xo=1-p.x; yo=1-p.y; co=1-p.c
    groups=[xo*2+co,xo*2+p.c,p.x*2+co,p.m]
    def row_load(h,g,k):
        r=groups[g]*R+k; s=g*R+k
        src,dst,sem=((tok_ref,tokb,tsem),(cot_ref,cotb,csem))[h]
        return pltpu.make_async_copy(src.at[r],dst.at[s%(2*R)],sem.at[s])
    own=[pltpu.make_async_copy(w_ref.at[i],W.at[i,p.m,pl.ds(pl.multiple_of(p.b*rp,rp),rp)],osem.at[i]) for i in range(3)]
    for h in (0,1):
        for g in (0,1):
            for k in range(R): row_load(h,g,k).start()
    for i in range(3): own[i].start()
    vall_ref[p.b]=v_ref[...]
    for i in range(3): own[i].wait()
    pl.semaphore_wait(bar,len(peers))
    pend=[]
    def remote(src,dst,s,r,dev):
        return pltpu.make_async_remote_copy(src_ref=src,dst_ref=dst,send_sem=s,recv_sem=r,device_id=dev,device_id_type=MESH)
    def start(cp,cond=None):
        if cond is None: cp.start()
        else:
            @pl.when(cond)
            def _(): cp.start()
        pend.append((cond,cp))
    def when(cond,f):
        if cond is None: f()
        else:
            @pl.when(cond)
            def _(): f()
    vcs=[remote(v_ref,vall_ref.at[p.b],vs.at[k],vr.at[k],d) for k,d in enumerate(bpeers)]
    for cp in vcs: start(cp)
    count=[0]*3
    def at(i,m,b): return W.at[i,m,pl.ds(pl.multiple_of(b*rp,rp),rp)]
    def fwd(i,m,b,dev,cond=None):
        s=count[i]; count[i]+=1
        start(remote(at(i,m,b),at(i,m,b),ssem.at[i,s],rsem.at[i,m,b],dev),cond)
    def arrived(i,m,b): remote(at(i,m,b),at(i,m,b),ssem.at[i,0],rsem.at[i,m,b],p.core).wait_recv()
    def mm(xr): return p.m if xr==0 else xo*2+p.c
    def zc(dr,k):
        if dr==2: return p.z,None
        return (p.z-1-k,p.z>k) if dr==0 else (p.z+1+k,p.z<nz-1-k)
    def both(a,b): return b if a is None else (a if b is None else a&b)
    def t_S(i,d):
        if d=="R": fwd(i,p.m,p.b,p.right,p.z<nz-1)
        elif d=="L": fwd(i,p.m,p.b,p.left,p.z>0)
        elif d=="X": fwd(i,p.m,p.b,p.xpeer)
        elif d=="Y": fwd(i,p.m,p.b,p.ypeer)
        else:
            fwd(i,p.m,p.b,p.right,p.z<nz-1); fwd(i,p.m,p.b,p.left,p.z>0)
    for i in range(3): fwd(i,p.m,p.b,p.core)
    def along(i,m,b,dr,cond):
        if dr==0: fwd(i,m,b,p.right,both(cond,p.z<nz-1))
        else: fwd(i,m,b,p.left,both(cond,p.z>0))
    def t_ZA(i,dr,k):
        z,c=zc(dr,k); b=z*2+p.y
        when(c,lambda: arrived(i,p.m,b))
        along(i,p.m,b,dr,c); fwd(i,p.m,b,p.core,c)
    def t_FX(i,dr,k):
        z,c=zc(dr,k); fwd(i,p.m,z*2+p.y,p.xpeer,c)
    def t_FY(i,xr,dr,k):
        z,c=zc(dr,k); b=z*2+p.y; m=mm(xr)
        if xr==1:
            when(c,lambda: arrived(i,m,b)); fwd(i,m,b,p.core,c)
        fwd(i,m,b,p.ypeer,c)
    def t_YA(i,xr,dr,k):
        z,c=zc(dr,k); b=z*2+yo; m=mm(xr)
        when(c,lambda: arrived(i,m,b)); fwd(i,m,b,p.core,c)
    def t_XA2(i):
        m=mm(1); arrived(i,m,p.b)
        fwd(i,m,p.b,p.ypeer); fwd(i,m,p.b,p.right,p.z<nz-1); fwd(i,m,p.b,p.left,p.z>0); fwd(i,m,p.b,p.core)
    def t_YA2(i,xr):
        m=mm(xr); b=p.z*2+yo; arrived(i,m,b)
        fwd(i,m,b,p.right,p.z<nz-1); fwd(i,m,b,p.left,p.z>0); fwd(i,m,b,p.core)
    def t_ZA2(i,xr,yr,dr,k):
        z,c=zc(dr,k); m=mm(xr); b=z*2+(p.y if yr==0 else yo)
        when(c,lambda: arrived(i,m,b))
        along(i,m,b,dr,c); fwd(i,m,b,p.core,c)
    hot={}
    def t_PK(g,h):
        for k in range(R):
            row_load(h,g,k).wait()
            col=selc_ref[groups[g]*R+k]-p.m*length
            one=(col==lax.broadcasted_iota(jnp.int32,(picks,length),1)).astype(F32).astype(BF)
            buf=(tokb,cotb)[h]
            zbuf[g,k*picks:(k+1)*picks,h*D:(h+1)*D]=nn(one,buf[(g*R+k)%(2*R)]).astype(BF)
        if g<2:
            for k in range(R): row_load(h,g+2,k).start()
        if g==0: start(ship(0,h))
        if g==2: start(ship(1,h))
    cols=[slice(0,D),slice(D,2*D)]
    def ship(a,h):
        src=zbuf.at[2*a]; dst=(rb,ra)[a]
        return remote(src.at[:,cols[h]],dst.at[:,cols[h]],shS.at[a,h],shR.at[a,h],p.core)
    ch=T//2
    def tx(h,q):
        rs=pl.ds(q*ch,ch)
        return remote(zbuf.at[1,rs,cols[h]],rx.at[rs,cols[h]],txS.at[h,q],txR.at[h,q],p.xpeer)
    def t_CMB(h):
        ship(0,h).wait_recv()
        zbuf[1,:,cols[h]]=zbuf[1,:,cols[h]]+rb[:,cols[h]]
    def t_TX(h,q): start(tx(h,q))
    def t_SEL(h):
        ship(1,h).wait_recv()
        for q in (0,1): tx(h,q).wait_recv()
        zbuf[3,:,cols[h]]=zbuf[3,:,cols[h]]+ra[:,cols[h]]+rx[:,cols[h]]
    sel=zbuf.at[3]
    keep={}
    outs=[]
    def write(src,dst):
        cp=pltpu.make_async_copy(src,dst,osem.at[3+len(outs)]); cp.start(); outs.append(cp)
    def t_NRM():
        for cp in vcs: cp.wait_recv()
        router,gain0,gain1=vectors(vall_ref)
        keep["gain1"]=gain1
        x=sel[:,0:D].astype(F32)
        keep["gate"]=jax.nn.sigmoid(jnp.sum(x*router,axis=1,keepdims=True))
        normed[...]=(x*root(x)*gain0).astype(BF)
    def t_GM():
        gmv=(keep["gate"]*sel[:,D:].astype(F32)).astype(BF)
        gm[...]=gmv
        gmT[...]=gmv.T
        write(sel,sel_out)
    mis=[p.m,p.x*2+co,xo*2+p.c,xo*2+co]
    def ready(i,mi):
        if mi%2==1:
            for b in range(nb): arrived(i,mis[mi],b)
    scale=HD**-0.5
    def t_QKV(mi):
        m=mis[mi]; ready(0,mi)
        P[m]=nn(normed[...],W[0,m]).astype(BF)
    def t_HD(mi):
        m=mis[mi]
        @pl.loop(0,R)
        def _(r):
            qi=lax.broadcasted_iota(jnp.int32,(picks,picks),0); ki=lax.broadcasted_iota(jnp.int32,(picks,picks),1)
            ok=(ki<=qi)&(seg_ref[r]==segc_ref[r])
            rs=pl.ds(pl.multiple_of(r*picks,picks),picks)
            res=[]
            for j in range(3):
                o=j*HD
                q=P[m,rs,o:o+HD]; k=P[m,rs,192+o:192+o+HD]; v=P[m,rs,384+o:384+o+HD]
                s=jnp.where(ok,nt(q,k)*scale,MASKED)
                e=jnp.exp(s-jnp.max(s,axis=1,keepdims=True))
                pr=(e/jnp.sum(e,axis=1,keepdims=True)).astype(BF)
                probs[r,m,j]=pr
                res.append(nn(pr,v))
            att[m,rs,:]=jnp.concatenate(res,axis=1).astype(BF)
    def t_OUT():
        write(W.at[0],W0_out); write(P,P_out); write(probs,probs_out); write(att,att_out)
        a=nt(att[0],W[0,0,:,576:768])
        for m in range(1,4): a=a+nt(att[m],W[0,m,:,576:768])
        ba[...]=a
        mv=sel[:,0:D].astype(F32)+a
        mid[...]=mv
        write(mid,mid_out)
        nmv=(mv*root(mv)*keep["gain1"]).astype(BF)
        nm[...]=nmv
        nmT[...]=nmv.T
        acc[...]=jnp.zeros_like(acc)
        accb[...]=jnp.zeros_like(accb)
    def g_copy(i,mi):
        x=(p.x,p.x,xo,xo)[mi]
        if mi%2==0: return pltpu.make_async_copy(gst.at[i],Gown.at[i,x],gL.at[i,x])
        return remote(gst.at[i],Gpart.at[i,x],gS.at[i,x],gR.at[i,x],p.core)
    def g_out(i,mi,val):
        if mi>0:
            cp=g_copy(i,mi-1)
            if mi%2==1: cp.wait()
            else: cp.wait_send()
        gst[i]=val.astype(BF)
        g_copy(i,mi).start()
    def t_ML(mi,part):
        m=mis[mi]
        if part==0:
            ready(1,mi); ready(2,mi)
            for t in range(3):
                cs=slice(t*256,(t+1)*256)
                h=nn(nm[...],W[1,m,:,cs])
                th=jnp.tanh(GC*(h+GA*h*h*h))
                act[:,cs]=(0.5*h*(1.0+th)).astype(BF)
                dg=0.5*(1.0+th)+0.5*h*(1.0-th*th)*(GC*(1.0+3.0*GA*h*h))
                gh[:,cs]=(nn(gm[...],W[2,m,:,cs])*dg).astype(BF)
        else:
            g_out(1,mi,nn(gmT[...],act[...]))
            g_out(0,mi,nn(nmT[...],gh[...]))
            acc[...]+=nt(act[...],W[2,m])
            accb[...]+=nt(gh[...],W[1,m])
    def t_END():
        write(accb,accb_out)
        br=ba[...]+acc[...]
        normed[...]=(sel[:,0:D].astype(F32)+keep["gate"]*br).astype(BF)
        write(normed,rows_out)
        gg_ref[...]=jnp.sum(sel[:,D:].astype(F32)*br,axis=1,keepdims=True)
    table=dict(S=t_S,ZA=t_ZA,FX=t_FX,FY=t_FY,YA=t_YA,XA2=t_XA2,YA2=t_YA2,ZA2=t_ZA2,PK=t_PK,CMB=t_CMB,TX=t_TX,SEL=t_SEL,NRM=t_NRM,GM=t_GM,QKV=t_QKV,HD=t_HD,OUT=t_OUT,ML=t_ML,END=t_END)
    for n in order: table[n[0]](*n[1:])
    for i in (0,1):
        g_copy(i,3).wait_send()
        for mi in (1,3): g_copy(i,mi).wait_recv()
    for cp in outs: cp.wait()
    for cond,cp in pend: when(cond,cp.wait_send)
def fore_call(w,vold,tokens,cot,selcol,seg,nb,picks):
    nz=nb//2; rp=w.shape[1]; rows,length,D=tokens.shape; R=rows//4; T=R*picks
    V=pltpu.VMEM; S=pltpu.SemaphoreType.DMA
    vm=pl.BlockSpec(memory_space=V); an=pl.BlockSpec(memory_space=pl.ANY)
    sd=jax.ShapeDtypeStruct
    return pl.pallas_call(functools.partial(fore_kernel,FORE_ORDER,nz,rp,picks),
        out_shape=(sd((4,D,D),BF),sd((2,2,D,D),BF),sd((2,2,D,D),BF),sd((T,2*D),BF),sd((4,T,D),BF),sd((R,4,3,picks,picks),BF),sd((4,T,192),BF),
            sd((T,D),F32),sd((T,D),F32),sd((T,D),BF),sd((T,1),F32),sd((nb,8,128),F32)),
        in_specs=[an,vm,an,an,vm,vm,vm],out_specs=(an,)*10+(vm,vm),
        scratch_shapes=[V((3,4,D,D),BF),V((2*R,length,D),BF),V((2*R,length,D),BF),V((4,T,2*D),BF),V((T,2*D),BF),V((T,2*D),BF),V((T,2*D),BF),
            V((T,D),BF),V((4,T,D),BF),V((R,4,3,picks,picks),BF),V((4,T,192),BF),V((T,D),F32),V((T,D),F32),V((T,D),BF),V((T,D),BF),V((T,D),BF),V((T,D),BF),
            V((T,D),F32),V((T,D),F32),V((D,T),BF),V((D,T),BF),V((2,D,D),BF),
            S((rows,)),S((rows,)),S((3,4,nb)),S((3,80)),S((2,2)),S((2,2)),S((2,2)),S((2,2)),S((nb,)),S((nb,)),S((2,2)),S((2,2)),S((2,2)),S((12,))],
        compiler_params=pltpu.CompilerParams(collective_id=0,has_side_effects=True,vmem_limit_bytes=60<<20),
        name="fore")(w,vold,tokens,cot,selcol,seg[:,None,:],seg[:,:,None])


BACK_ORDER=(('RO',2,),('AD',1,0,),('AD',1,1,),('YS',1,1,1,),('RO',1,),('YS',1,1,2,),('RO',0,),('YS',1,1,3,),('AD',2,0,),('ZR',5,),('RO',3,),('YS',1,1,0,),('C',0,),('YR',1,1,1,),('YS',1,0,0,),('AD',2,1,),('ZR',6,),('C',1,),('YS',1,0,1,),('C',2,),('C',3,),('ZR',4,),('YR',1,1,2,),('C',4,),('ZR',7,),('ZL',0,),('C',5,),('YR',1,1,3,),('C',6,),('ZL',1,),('C',7,),('C',8,),('C',9,),('ZL',3,),('ZR',10,),('C',10,),('YS',0,1,3,),('YS',0,1,0,),('YR',1,1,0,),('ZR',8,),('C',11,),('ZL',2,),('YS',0,1,2,),('C',12,),('C',13,),('YS',0,1,1,),('YS',1,0,2,),('C',14,),('ZL',7,),('C',15,),('YS',1,0,3,),('ZL',6,),('C',16,),('C',17,),('ZL',4,),('YR',0,1,3,),('C',18,),('YR',0,1,0,),('ZL',5,),('ZR',9,),('ZL',10,),('ZR',3,),('C',19,),('C',20,),('YS',0,0,3,),('C',21,),('YR',0,1,2,),('ZR',1,),('C',22,),('YR',0,1,1,),('C',23,),('ZL',11,),('ZR',0,),('C',24,),('C',25,),('RG',2,),('YS',0,0,0,),('ZR',2,),('RG',1,),('YR',1,0,1,),('RG',3,),('XR',1,1,),('VS',),('YR',1,0,0,),('YR',1,0,2,),('ZL',9,),('YS',0,0,1,),('YS',0,0,2,),('YR',1,0,3,),('RG',0,),('XR',1,0,),('VM',),('LL',1,1,),('XR',1,3,),('XR',1,2,),('YR',0,0,3,),('ZL',8,),('LR',1,3,),('XR',0,3,),('YR',0,0,0,),('XR',0,0,),('LR',0,3,),('ZR',11,),('LR',1,2,),('LL',0,0,),('YR',0,0,1,),('LL',1,2,),('F2',1,1,),('XR',0,1,),('LR',0,1,),('F2',0,1,),('YR',0,0,2,),('XR',0,2,),('LR',0,2,),('LL',1,0,),('F2',1,0,),('LL',0,1,),('FY',1,),('LR',1,1,),('F2',0,0,),('FY',0,),('RF',),('FIN',1,),('ST',1,),('FIN',0,),('ST',0,),('LL',0,2,),('FX',),('ST',2,))


EPS_SQUARE=1e-30; CLIP=0.3
ROW_CHUNKS=4
def back_kernel(order, nz, rp, nb, picks, Gown, Gpart, W_hbm, sel_hbm, P_hbm, probs_hbm, att_hbm, mid_hbm, accb_hbm, rows_hbm, gg_ref, vec_ref,
                w_ref, rold_ref, cold_ref, vold_ref, vmom_ref,
                Gs_ref, out_ref, grad_ref, R_ref, C_ref, S_ref, V_ref, vdir_ref,
                Pl, RC, RY, RX, RLy, RRy, RLz, RRz, Fy, Fx, gst,
                W0, sel, P, probs, att, mid, accb, acc, ga, gaT, nT, gatt, gob, rows,
                vin, vmp, cin, rin, sin, smp, rloc, cloc, sloc, vsend, small,
                loc, cS, cR, yS, yR, xS, xR, zS, zR, lS, lR, fS, fR, rS, rR, eS, eR):
    D=768; T=sel.shape[0]
    p=Plane()
    bpeers=[(lax.rem(p.b+k,nb),p.m) for k in range(1,nb)]
    mpeers=[(p.b,lax.rem(p.m+k,4)) for k in range(1,4)]
    bar=pltpu.get_barrier_semaphore()
    for d in bpeers+mpeers: pl.semaphore_signal(bar,inc=1,device_id=d,device_id_type=MESH)
    xo=1-p.x; yo=1-p.y; co=1-p.c
    loads={}
    def load(n,src,dst,k):
        loads[n]=pltpu.make_async_copy(src,dst,loc.at[k]); loads[n].start()
    own_blocks=[(i,x) for x in (0,1) for i in (2,1)]
    for k,(i,x) in enumerate(own_blocks):
        load((i,x),Gown.at[i-1,x],Pl.at[i,x],k)
        load((i,x,1),Gpart.at[i-1,x],RC.at[i,x],13+k)
    for k,(n,src,dst) in enumerate([(0,accb_hbm,accb),(1,mid_hbm,mid),(2,sel_hbm,sel),(3,W_hbm,W0),(4,att_hbm,att),(5,P_hbm,P),(6,probs_hbm,probs)]):
        load(n,src,dst,4+k)
    pl.semaphore_wait(bar,nb-1+3)
    pend=[]
    def remote(src,dst,s,r,dev):
        return pltpu.make_async_remote_copy(src_ref=src,dst_ref=dst,send_sem=s,recv_sem=r,device_id=dev,device_id_type=MESH)
    def start(cp): cp.start(); pend.append((None,cp))
    def part(ref,b): return ref.at[pl.ds(pl.multiple_of(b*rp,rp),rp)]
    def shard(i,x,b): return Pl.at[i,x,pl.ds(pl.multiple_of(b*rp,rp),rp)]
    def add(dst,*src):
        @pl.loop(0,rp,step=32)
        def _(k):
            ks=pl.ds(pl.multiple_of(k,32),32)
            v=dst[ks].astype(F32)
            for q in src: v=v+q[ks].astype(F32)
            dst[ks]=v.astype(BF)
    def core_copy(i,x,src): return remote(src,RC.at[i,x],cS.at[i,x],cR.at[i,x],p.core)
    def t_AD(i,x):
        loads[(i,x)].wait(); loads[(i,x,1)].wait()
        dst=Pl.at[i,x]; src=RC.at[i,x]
        @pl.loop(0,D,step=64)
        def _(k):
            ks=pl.ds(pl.multiple_of(k,64),64)
            dst[ks]=(dst[ks].astype(F32)+src[ks].astype(F32)).astype(BF)
    ax=lambda xr: p.x if xr==0 else xo
    ay=lambda yr: p.y if yr==0 else yo
    def ys_copy(g,xr,z): return remote(shard(g,ax(xr),z*2+yo),RY.at[g,ax(xr),z],yS.at[g,xr,z],yR.at[g,ax(xr),z],p.ypeer)
    def xs_copy(g,z): return remote(shard(g,xo,z*2+p.y),RX.at[g,z],xS.at[g,z],xR.at[g,z],p.xpeer)
    def t_YS(g,xr,z): start(ys_copy(g,xr,z))
    def t_YR(g,xr,z):
        ys_copy(g,xr,z).wait_recv()
        add(shard(g,ax(xr),z*2+p.y),RY.at[g,ax(xr),z])
        if xr==1: start(xs_copy(g,z))
    def t_XR(g,z):
        xs_copy(g,z).wait_recv(); add(shard(g,p.x,z*2+p.y),RX.at[g,z])
    def guarded(cond,cp,more,recv,dst):
        @pl.when(cond)
        def _():
            @pl.when(more)
            def _(): cp.wait_recv(); add(dst,recv)
            cp.start()
        pend.append((cond,cp))
    def t_LR(g,t):
        cp=remote(shard(g,p.x,t*2+p.y),RLy.at[g,t],lS.at[g,0,t],lR.at[g,0,t],p.right)
        guarded(p.z<t,cp,p.z>0,RLy.at[g,t],shard(g,p.x,t*2+p.y))
    def t_LL(g,t):
        cp=remote(shard(g,p.x,t*2+p.y),RRy.at[g,t],lS.at[g,1,t],lR.at[g,1,t],p.left)
        guarded(p.z>t,cp,p.z<nz-1,RRy.at[g,t],shard(g,p.x,t*2+p.y))
    def t_ZR(k):
        t=nz-1-k//4; c=k%4; sh=shard(2,c//2,t*2+c%2)
        cp=remote(sh,RLz.at[c,t],zS.at[c,0,t],zR.at[c,0,t],p.right)
        guarded(p.z<t,cp,p.z>0,RLz.at[c,t],sh)
    def t_ZL(k):
        t=k//4; c=k%4; sh=shard(2,c//2,t*2+c%2)
        cp=remote(sh,RRz.at[c,t],zS.at[c,1,t],zR.at[c,1,t],p.left)
        guarded(p.z>t,cp,p.z<nz-1,RRz.at[c,t],sh)
    def last(RL,RR,rl,rr,dst):
        @pl.when(p.z>0)
        def _(): rl.wait_recv(); add(dst,RL)
        @pl.when(p.z<nz-1)
        def _(): rr.wait_recv(); add(dst,RR)
    def fy_copy(xr): return remote(shard(2,ax(xr),p.z*2+yo),Fy.at[ax(xr)],fS.at[0,xr],fR.at[0,ax(xr)],p.ypeer)
    def fx_copy(): return remote(shard(2,xo,p.b),Fx,fS.at[1,0],fR.at[1,0],p.xpeer)
    def t_F2(xr,yr):
        c=ax(xr)*2+ay(yr); sh=shard(2,ax(xr),p.z*2+ay(yr))
        rl=remote(sh,RLz.at[c,p.z],zS.at[0,0,0],zR.at[c,0,p.z],p.right)
        rr=remote(sh,RRz.at[c,p.z],zS.at[0,1,0],zR.at[c,1,p.z],p.left)
        last(RLz.at[c,p.z],RRz.at[c,p.z],rl,rr,sh)
        if yr==1: start(fy_copy(xr))
    def t_FY(xr):
        fy_copy(xr).wait_recv(); add(shard(2,ax(xr),p.b),Fy.at[ax(xr)])
        if xr==1: start(fx_copy())
    def t_FX():
        fx_copy().wait_recv()
        Gs_ref[2]=shard(2,p.x,p.b)[...].astype(F32)+Fx[...].astype(F32)
    def t_FIN(g):
        sh=shard(g,p.x,p.b)
        Gs_ref[g]=sh[...].astype(F32)
        @pl.when(p.z>0)
        def _():
            remote(sh,RLy.at[g,p.z],lS.at[g,0,0],lR.at[g,0,p.z],p.right).wait_recv()
            Gs_ref[g]+=RLy[g,p.z].astype(F32)
        @pl.when(p.z<nz-1)
        def _():
            remote(sh,RRy.at[g,p.z],lS.at[g,1,0],lR.at[g,1,p.z],p.left).wait_recv()
            Gs_ref[g]+=RRy[g,p.z].astype(F32)
    ch=T//ROW_CHUNKS
    def row_copy(k,q):
        src,dst=((rows_hbm,out_ref),(rows,grad_ref))[k]
        return remote(src.at[pl.ds(q*ch,ch)],dst.at[p.m,pl.ds(q*ch,ch)],rS.at[k,q],rR.at[k,q],p.xpeer)
    xm=xo*2+p.c
    def core_rows(k):
        src,dst=((rows_hbm,out_ref),(rows,grad_ref))[k]
        return remote(src,dst.at[p.m],rS.at[k,4],rR.at[k,4],p.core),pltpu.make_async_copy(src,dst.at[p.m],loc.at[11+k])
    def fwd_rows(k):
        dst=(out_ref,grad_ref)[k]
        return remote(dst.at[xm],dst.at[xm],rS.at[k,5],rR.at[k,5],p.core)
    def t_RO(q):
        start(row_copy(0,q))
        if q==0:
            cp,lc=core_rows(0); start(cp); lc.start()
    def t_RG(q):
        start(row_copy(1,q))
        if q==0:
            cp,lc=core_rows(1); start(cp); lc.start()
    def t_RF():
        for k in range(2):
            for q in range(ROW_CHUNKS): row_copy(k,q).wait_recv()
            start(fwd_rows(k))
    router,gain0,gain1=vectors(vec_ref)
    scale=HD**-0.5
    ms=[xo*2+co,xo*2+p.c,p.x*2+co,p.x*2+p.c]
    keep={}
    def gate_of(): return jax.nn.sigmoid(jnp.sum(sel[:,0:D].astype(F32)*router,axis=1,keepdims=True))
    def back(e,gain,scaled,iv):
        eg=e*gain
        return iv*(eg-scaled*jnp.mean(eg*scaled,axis=1,keepdims=True)),jnp.sum(e*scaled,axis=0,keepdims=True)
    def c_first():
        for n in (0,1,2): loads[n].wait()
        iv=root(mid[...])
        gmid,g1=back(accb[...],gain1,mid[...]*iv,iv)
        small[2:3,:]=g1
        mid[...]=gmid
        gv=(gmid+gate_of()*sel[:,D:].astype(F32)).astype(BF)
        ga[...]=gv
        gaT[...]=gv.T
        xv=sel[:,0:D].astype(F32)
        nT[...]=(xv*root(xv)*gain0).astype(BF).T
        acc[...]=jnp.zeros_like(acc)
        for n in (3,4,5,6): loads[n].wait()
    def c_out(mi):
        m=ms[mi]
        gatt[...]=nn(ga[...],W0[m,:,576:768]).astype(BF)
        gob[...]=nn(gaT[...],att[m])
    def c_head(mi,j):
        m=ms[mi]; o=j*HD
        @pl.loop(0,T//picks)
        def _(r):
            rs=pl.ds(pl.multiple_of(r*picks,picks),picks)
            q=P[m,rs,o:o+HD]; k=P[m,rs,192+o:192+o+HD]; v=P[m,rs,384+o:384+o+HD]
            g=gatt[rs,o:o+HD]
            pr=probs[r,m,j]
            gp=nt(g,v)
            pf=pr.astype(F32)
            ds=(pf*(gp-jnp.sum(pf*gp,axis=1,keepdims=True))).astype(BF)
            P[m,rs,o:o+HD]=(nn(ds,k)*scale).astype(BF)
            P[m,rs,192+o:192+o+HD]=(tn(ds,q)*scale).astype(BF)
            P[m,rs,384+o:384+o+HD]=tn(pr,g).astype(BF)
    def c_block(mi):
        m=ms[mi]; x=(xo,xo,p.x,p.x)[mi]
        g=nn(nT[...],P[m,:,0:576])
        if mi%2==0:
            s=mi//2
            gst[s,:,0:576]=g.astype(BF); gst[s,:,576:768]=gob[...].astype(BF)
            start(core_copy(0,x,gst.at[s]))
        else:
            core_copy(0,x,gst.at[0]).wait_recv()
            Pl[0,x,:,0:576]=(g+RC[0,x,:,0:576].astype(F32)).astype(BF)
            Pl[0,x,:,576:768]=(gob[...]+RC[0,x,:,576:768].astype(F32)).astype(BF)
    def c_norm(mi):
        m=ms[mi]
        acc[...]+=nt(P[m,:,0:576],W0[m,:,0:576])
    vcs=[]
    def c_last():
        xv=sel[:,0:D].astype(F32); gate=gate_of()
        glog=gg_ref[...]*gate*(1.0-gate)
        iv=root(xv)
        gin,g0=back(acc[...],gain0,xv*iv,iv)
        small[0:1,:]=jnp.sum(glog*xv,axis=0,keepdims=True)
        small[1:2,:]=g0
        small[3:8,:]=jnp.zeros((5,D),F32)
        rows[...]=(sel[:,D:].astype(F32)+mid[...]+gin+glog*router).astype(BF)
        n=D//nb
        for k in range(nb):
            vsend[k]=jnp.concatenate([small[:,k*n:(k+1)*n],jnp.zeros((8,128-n),F32)],axis=1)
        for k,d in enumerate(bpeers):
            cp=remote(vsend.at[d[0]],vin.at[k],eS.at[0,k],eR.at[0,k],d); start(cp); vcs.append(cp)
    def t_C(i):
        if i==0: c_first()
        elif i<=20:
            mi,k=divmod(i-1,5)
            if k==0: c_out(mi)
            elif k<4: c_head(mi,k-1)
            else: c_block(mi)
        elif i<=24: c_norm(i-21)
        else: c_last()
    table=dict(YS=t_YS,YR=t_YR,XR=t_XR,LR=t_LR,LL=t_LL,ZR=t_ZR,ZL=t_ZL,F2=t_F2,FY=t_FY,FX=t_FX,FIN=t_FIN,RO=t_RO,RG=t_RG,RF=t_RF,C=t_C,AD=t_AD)
    lanes=lax.broadcasted_iota(jnp.int32,(8,128),1); sub=lax.broadcasted_iota(jnp.int32,(8,128),0)
    keep["tile"]=jnp.zeros((8,128),F32)
    def put(lane,val): keep["tile"]=keep["tile"]+jnp.where((lanes==lane)&(sub==0),val,0.0)
    def tot(v): return jnp.sum(jnp.sum(v,axis=1,keepdims=True),axis=0,keepdims=True)
    def blocks(i): return [(j,slice(j*192,(j+1)*192)) for j in range(4)] if i==0 else [(3+i,slice(0,D))]
    rlane=lax.broadcasted_iota(jnp.int32,(rp,128),1)
    def t_VS():
        for cp in vcs: cp.wait_recv()
        vs=vsend[p.b]
        for k in range(nb-1): vs=vs+vin[k]
        vsend[p.b]=vs
        keep["vms"]=[]
        for k,d in enumerate(mpeers):
            cp=remote(vsend.at[p.b],vmp.at[k],eS.at[1,k],eR.at[1,k],d); start(cp); keep["vms"].append(cp)
        for i in range(3):
            for (j,s) in blocks(i):
                wv=w_ref[i,:,s].astype(F32); put(12+j,tot(wv*wv))
        for j in range(3):
            wv=vold_ref[j:j+1,:]; put(18+j,tot(wv*wv)*0.25)
    def t_VM():
        for cp in keep["vms"]: cp.wait_recv()
        vs=vsend[p.b]
        for k in range(3): vs=vs+vmp[k]
        V_ref[0:8,:]=vs
        mom=0.5*vmom_ref[...]+0.5*(vs*vs+EPS_SQUARE)
        V_ref[8:16,:]=mom
        vd=jnp.where(lanes<D//nb,vs*lax.rsqrt(mom),0.0)
        vdir_ref[...]=vd
        for j in range(3): put(21+j,tot(vd[j:j+1]*vd[j:j+1])*0.25)
        cloc[3:8,:]=jnp.zeros((5,D),F32)
        rloc[...]=jnp.zeros_like(rloc)
    def t_ST(i):
        sq=Gs_ref[i]; sq=sq*sq+EPS_SQUARE
        for (j,s) in blocks(i): rloc[...]+=jnp.where(rlane==j,jnp.sum(sq[:,s],axis=1,keepdims=True),0.0)
        cloc[i:i+1,:]=jnp.sum(sq,axis=0,keepdims=True)
    table.update(VS=t_VS,VM=t_VM,ST=t_ST)
    for n in order: table[n[0]](*n[1:])
    ccs=[];rcs=[]
    for k,d in enumerate(bpeers):
        cp=remote(cloc,cin.at[k],eS.at[2,k],eR.at[2,k],d); start(cp); ccs.append(cp)
    for k,d in enumerate(mpeers):
        cp=remote(rloc,rin.at[k],eS.at[3,k],eR.at[3,k],d); start(cp); rcs.append(cp)
    for cp in rcs: cp.wait_recv()
    rs=rloc[...]+rin[0]+rin[1]+rin[2]
    ncol=jnp.where(rlane>=4,1.0/3072.0,1.0/768.0)
    rnew=0.5*rold_ref[...]+0.5*rs*ncol
    R_ref[...]=rnew
    for cp in ccs: cp.wait_recv()
    cs=cloc[...]
    for k in range(nb-1): cs=cs+cin[k]
    cnew=0.5*cold_ref[...]+0.5*cs*(1.0/768.0)
    C_ref[...]=cnew
    for i in range(3):
        g=Gs_ref[i]; g2=g*g/cnew[i:i+1,:]
        for (j,s) in blocks(i):
            put(6+j,tot(jnp.sum(g2[:,s],axis=1,keepdims=True)/rnew[:,j:j+1]))
    for j in (0,1,2,4): put(j,tot(rnew[:,j:j+1])*(1.0/(768*4)))
    put(3,tot(cnew[0:1,576:768])*(1.0/(768*nb)))
    put(5,tot(cnew[2:3,:])*(1.0/(3072*nb)))
    tile=keep["tile"]
    sloc[0]=tile
    scs=[]
    for k,d in enumerate(bpeers):
        cp=remote(sloc.at[0],sin.at[k],eS.at[4,k],eR.at[4,k],d); start(cp); scs.append(cp)
    for cp in scs: cp.wait_recv()
    for k in range(nb-1): tile=tile+sin[k]
    sloc[1]=tile
    scs=[]
    for k,d in enumerate(mpeers):
        cp=remote(sloc.at[1],smp.at[k],eS.at[5,k],eR.at[5,k],d); start(cp); scs.append(cp)
    for cp in scs: cp.wait_recv()
    for k in range(3): tile=tile+smp[k]
    out=jnp.zeros((8,128),F32)
    for j in range(9):
        n=768.0*768.0 if j<4 else (768.0*3072.0 if j<6 else 768.0)
        if j<6:
            mean=tile[0:1,j:j+1]; us=mean*tile[0:1,6+j:7+j]/n; ws=tile[0:1,12+j:13+j]/n
        else:
            mean=jnp.ones((1,1),F32); us=tile[0:1,15+j:16+j]/n; ws=tile[0:1,12+j:13+j]/n
        urms=jnp.sqrt(us)
        coef=jnp.sqrt(ws)/jnp.maximum(1.0,urms/CLIP)*jnp.sqrt(mean)
        out=out+jnp.where((lanes==j)&(sub==0),urms,0.0)+jnp.where((lanes==j)&(sub==1),coef,0.0)
    S_ref[...]=out
    for k in range(2):
        cp,lc=core_rows(k); cp.wait_recv(); lc.wait(); fwd_rows(k).wait_recv()
    for cond,cp in pend:
        if cond is None: cp.wait_send()
        else:
            @pl.when(cond)
            def _(): cp.wait_send()
def back_call(Gown,Gpart,W0,sel,P,probs,att,mid,accb,rows,gg,vec,w,rold,cold,vold,vmom,nb,picks):
    D=768; nz=nb//2; rp=w.shape[1]; T=rows.shape[0]; R=T//picks
    V=pltpu.VMEM; S=pltpu.SemaphoreType.DMA
    vm=pl.BlockSpec(memory_space=V); an=pl.BlockSpec(memory_space=pl.ANY)
    sd=jax.ShapeDtypeStruct
    order=list(BACK_ORDER)
    return pl.pallas_call(functools.partial(back_kernel,order,nz,rp,nb,picks),
        out_shape=(sd((3,rp,D),F32),sd((4,T,D),BF),sd((4,T,D),BF),sd((rp,128),F32),sd((8,D),F32),sd((8,128),F32),sd((16,128),F32),sd((8,128),F32)),
        in_specs=[an]*10+[vm]*7,out_specs=(vm,an,an)+(vm,)*5,
        scratch_shapes=[V((3,2,D,D),BF),V((3,2,D,D),BF),V((2,2,nz,rp,D),BF),V((2,nz,rp,D),BF),V((2,nz,rp,D),BF),V((2,nz,rp,D),BF),
            V((4,nz,rp,D),BF),V((4,nz,rp,D),BF),V((2,rp,D),BF),V((rp,D),BF),V((2,D,D),BF),
            V((4,D,D),BF),V((T,2*D),BF),V((4,T,D),BF),V((R,4,3,picks,picks),BF),V((4,T,192),BF),V((T,D),F32),V((T,D),F32),V((T,D),F32),
            V((T,D),BF),V((D,T),BF),V((D,T),BF),V((T,192),BF),V((D,192),F32),V((T,D),BF),
            V((nb,8,128),F32),V((3,8,128),F32),V((nb,8,D),F32),V((3,rp,128),F32),
            V((nb,8,128),F32),V((3,8,128),F32),V((rp,128),F32),V((8,D),F32),V((2,8,128),F32),V((nb,8,128),F32),V((8,D),F32),
            S((17,)),S((3,2)),S((3,2)),S((2,2,nz)),S((2,2,nz)),S((2,nz)),S((2,nz)),S((4,2,nz)),S((4,2,nz)),S((2,2,nz)),S((2,2,nz)),
            S((2,2)),S((2,2)),S((2,6)),S((2,6)),S((6,nb)),S((6,nb))],
        compiler_params=pltpu.CompilerParams(collective_id=1,has_side_effects=True,vmem_limit_bytes=58<<20),
        name="back")(Gown,Gpart,W0,sel,P,probs,att,mid,accb,rows,gg,vec,w,rold,cold,vold,vmom)


BF=jnp.bfloat16; F32=jnp.float32; D=768
def place_kernel(tok_ref, cot_ref, rows_ref, grads_ref, sel_ref, G_ref, w_ref, vold_ref, R_ref, C_ref, S_ref, V_ref, vdir_ref,
                 bo_ref, ig_ref, qg, qr, qc, qn, og, orr, oc, on, ug, ur, uc, un, dgr, dr, dc, dn, rg, rm, rn, gg, gmo, gn):
    length=tok_ref.shape[1]; picks=rows_ref.shape[1]
    pos=lax.broadcasted_iota(jnp.int32,(length,picks),0)
    hot=(pos==sel_ref[0]).astype(F32)
    cover=jnp.sum(hot,axis=1,keepdims=True)>0.5
    hot=hot.astype(BF)
    bo_ref[0]=jnp.where(cover,jnp.dot(hot,rows_ref[0],preferred_element_type=F32),tok_ref[0].astype(F32)).astype(BF)
    ig_ref[0]=jnp.where(cover,jnp.dot(hot,grads_ref[0],preferred_element_type=F32),cot_ref[0].astype(F32))
    @pl.when(pl.program_id(0)==0)
    def _():
        def new(i,s,j):
            g=G_ref[i,:,s]
            return g,w_ref[i,:,s].astype(F32)-S_ref[1:2,j:j+1]*(g*lax.rsqrt(R_ref[:,j:j+1]*C_ref[i:i+1,s]))
        for j in range(3):
            qg[j],qn[j]=new(0,slice(j*192,(j+1)*192),j)
            qc[j:j+1,:]=C_ref[0:1,j*192:(j+1)*192]
        g,n=new(0,slice(576,768),3); og[...]=g.T; on[...]=n.T
        g,n=new(1,slice(0,D),4); ug[...]=g; un[...]=n
        g,n=new(2,slice(0,D),5); dgr[...]=g.T; dn[...]=n.T
        Rt=R_ref[...].T
        qr[...]=Rt[0:3]; oc[...]=Rt[3:4]; ur[...]=Rt[4:5]; dc[...]=Rt[5:6]
        orr[...]=C_ref[0:1,576:768]; uc[...]=C_ref[1:2,:]; dr[...]=C_ref[2:3,:]
        rg[...]=V_ref[0:1,0:96]; gg[...]=V_ref[1:3,0:96]
        rm[...]=V_ref[8:9,0:96]; gmo[...]=V_ref[9:11,0:96]
        rn[...]=vold_ref[0:1,0:96]-S_ref[1:2,6:7]*vdir_ref[0:1,0:96]
        gn[0:1,:]=vold_ref[1:2,0:96]-S_ref[1:2,7:8]*vdir_ref[1:2,0:96]
        gn[1:2,:]=vold_ref[2:3,0:96]-S_ref[1:2,8:9]*vdir_ref[2:3,0:96]
def place_call(tokens,cot,allrows,allgrads,selrel,G,w,vold,R,C,S,V,vdir):
    rows,length,_=tokens.shape; picks=selrel.shape[2]
    allrows=allrows.reshape(rows,picks,D); allgrads=allgrads.reshape(rows,picks,D)
    sd=lambda *s: jax.ShapeDtypeStruct(s,F32)
    rp=w.shape[1]
    row=lambda *s: pl.BlockSpec((1,)+s,lambda i:(i,0,0))
    def whole(s):
        n=len(s); return pl.BlockSpec(s,lambda i:(0,)*n)
    small=[(3,rp,192),(3,rp),(3,192),(3,rp,192),(192,rp),(1,192),(1,rp),(192,rp),(rp,D),(1,rp),(1,D),(rp,D),(D,rp),(1,D),(1,rp),(D,rp),(1,rp),(1,rp),(1,rp),(2,rp),(2,rp),(2,rp)]
    return pl.pallas_call(place_kernel,grid=(rows,),
        out_shape=(jax.ShapeDtypeStruct(tokens.shape,BF),jax.ShapeDtypeStruct(cot.shape,F32))+tuple(sd(*s) for s in small),
        in_specs=[row(length,D),row(length,D),row(picks,D),row(picks,D),row(1,picks)]+[whole(a.shape) for a in (G,w,vold,R,C,S,V,vdir)],
        out_specs=(row(length,D),row(length,D))+tuple(whole(s) for s in small),
        compiler_params=pltpu.CompilerParams(vmem_limit_bytes=48<<20),
        name="place")(tokens,cot,allrows,allgrads,selrel,G,w,vold,R,C,S,V,vdir)


def tile_of(rows,height,width):
    padded=[jnp.pad(r.astype(F32),((0,0),(0,width-r.shape[1]))) for r in rows]
    v=jnp.concatenate(padded,axis=0)
    return jnp.pad(v,((0,height-v.shape[0]),(0,0)))

def local_fast(tokens,segments,selection,cotangent,qkv_weight,out_weight,up_weight,down_weight,router_weight,norm_gains,
               qkv_rows,qkv_cols,out_rows,out_cols,up_rows,up_cols,down_rows,down_cols,router_moment,gains_moment):
    nb=lax.axis_size("batch"); m=lax.axis_index("mp")
    length=tokens.shape[1]; picks=selection.shape[1]; rows=tokens.shape[0]; per=rows//4
    w=jnp.stack([jnp.concatenate([qkv_weight[0],qkv_weight[1],qkv_weight[2],out_weight.T],axis=1),up_weight,down_weight.T])
    vold=tile_of([router_weight[None],norm_gains],8,128)
    vmom=tile_of([router_moment[None],gains_moment],8,128)
    rold=tile_of([qkv_rows,out_cols[None],up_rows[None],down_cols[None]],128,qkv_rows.shape[1]).T
    cold=tile_of([qkv_cols.reshape(1,-1),],1,768)
    cold=tile_of([jnp.concatenate([qkv_cols.reshape(1,-1),out_rows[None]],axis=1),up_cols[None],down_rows[None]],8,768)
    mine=lax.dynamic_slice_in_dim(selection,m*per,per,0)
    segs=lax.dynamic_slice_in_dim(segments,m*per,per,0)
    begin=jnp.sum(segs[:,:,None]<jnp.arange(1,8)[None,None,:],axis=1)
    seg=jnp.sum(mine[:,:,None]>=begin[:,None,:],axis=2).astype(jnp.int32)
    W0,Gown,Gpart,sel,projected,probs,attended,middle,grad_mid,rows_low,grad_gate,vall=fore_call(
        w,vold,tokens,cotangent,selection[:,:,None],seg,nb,picks)
    Gs,allrows,allgrads,R,C,S,V,vdir=back_call(Gown,Gpart,W0,sel,projected,probs,attended,middle,grad_mid,rows_low,grad_gate,vall,
        w,rold,cold,vold,vmom,nb,picks)
    (bo,ig,qg,qr,qc,qn,og,orr,oc,on,ug,ur,uc,un,dgr,dr,dc,dn,rg,rm,rn,gg,gmo,gn)=place_call(
        tokens,cotangent,allrows,allgrads,(selection-m*length)[:,None,:],Gs,w,vold,R,C,S,V,vdir)
    return (bo,ig,qg,qr,qc,qn,og,orr[0],oc[0],on,ug,ur[0],uc[0],un,dgr,dr[0],dc[0],dn,rg[0],rm[0],rn[0],gg,gmo,gn,S[0,:9])

def chosen_local(mesh):
    return local_fast if (mesh.shape["batch"],mesh.shape["mp"])==(8,4) else local_any


def solution(mesh):
    in_specs = (
        P("batch", "mp", None),
        P("batch", None),
        P("batch", None),
        P("batch", "mp", None),
        P(None, "batch", "mp"),
        P("mp", "batch"),
        P("batch", "mp"),
        P("mp", "batch"),
        P("batch"),
        P(None, "batch"),
        P(None, "batch"),
        P(None, "mp"),
        P("mp"),
        P("batch"),
        P("batch"),
        P("mp"),
        P("mp"),
        P("batch"),
        P("batch"),
        P(None, "batch"),
    )
    out_specs = (
        P("batch", "mp", None),
        P("batch", "mp", None),
        P(None, "batch", "mp"),
        P(None, "batch"),
        P(None, "mp"),
        P(None, "batch", "mp"),
        P("mp", "batch"),
        P("mp"),
        P("batch"),
        P("mp", "batch"),
        P("batch", "mp"),
        P("batch"),
        P("mp"),
        P("batch", "mp"),
        P("mp", "batch"),
        P("mp"),
        P("batch"),
        P("mp", "batch"),
        P("batch"),
        P("batch"),
        P("batch"),
        P(None, "batch"),
        P(None, "batch"),
        P(None, "batch"),
        P(),
    )
    return jax.shard_map(chosen_local(mesh), mesh=mesh, in_specs=in_specs, out_specs=out_specs, check_vma=False)
```

```python
import functools

import jax
import jax.numpy as jnp
from jax import lax
from jax.experimental import pallas as pl
from jax.experimental.pallas import tpu as pltpu
from jax.sharding import PartitionSpec as P


D = 768
HEAD_DIM = 64
FF = 3072
MICRO = 2


EPS_NORM = 1e-06
EPS_SQUARE = 1e-30
DECAY = 0.5
CLIP_RMS = 0.3
RATE = 1.0
MASKED = -1e30


def rms_parts(values):
    inverse = lax.rsqrt(jnp.mean(values * values, axis=1, keepdims=True) + EPS_NORM)
    return (values * inverse, inverse)


def norm_back(grad_norm, gain_vec, scaled, inverse):
    grad_scaled = grad_norm * gain_vec
    grad_input = inverse * (
        grad_scaled - scaled * jnp.mean(grad_scaled * scaled, axis=1, keepdims=True)
    )
    return (grad_input, jnp.sum(grad_norm * scaled, axis=0))


def spread_into(values, index, pieces):
    size_piece = values.shape[-1]
    shape_full = values.shape[:-1] + (size_piece * pieces,)
    return lax.dynamic_update_slice_in_dim(
        jnp.zeros(shape_full, jnp.float32), values, index * size_piece, values.ndim - 1
    )


def own_piece(values, index, size_piece):
    return lax.dynamic_slice_in_dim(values, index * size_piece, size_piece, values.ndim - 1)


def factor_terms(gradient, row_old, col_old, row_index, row_count, col_index, col_count):
    square = gradient * gradient + EPS_SQUARE
    rows_here, cols_here = gradient.shape[-2:]
    row_term = (1.0 - DECAY) * jnp.sum(square, axis=-1) / (
        cols_here * col_count
    ) + DECAY * row_old * (col_index == 0)
    col_term = (1.0 - DECAY) * jnp.sum(square, axis=-2) / (
        rows_here * row_count
    ) + DECAY * col_old * (row_index == 0)
    return (
        spread_into(row_term, row_index, row_count),
        spread_into(col_term, col_index, col_count),
    )


def factor_direction(gradient, row_full, col_full, row_index, col_index):
    rows_here, cols_here = gradient.shape[-2:]
    row_mine = own_piece(row_full, row_index, rows_here)
    col_mine = own_piece(col_full, col_index, cols_here)
    mean_row = jnp.mean(row_full, axis=-1)[..., None, None]
    second = row_mine[..., :, None] * col_mine[..., None, :] / mean_row
    return (gradient * lax.rsqrt(second), row_mine, col_mine)


def local_any(
    tokens,
    segments,
    selection,
    cotangent,
    qkv_weight,
    out_weight,
    up_weight,
    down_weight,
    router_weight,
    norm_gains,
    qkv_rows,
    qkv_cols,
    out_rows,
    out_cols,
    up_rows,
    up_cols,
    down_rows,
    down_cols,
    router_moment,
    gains_moment,
):
    qkv_all, out_all, up_all, down_all, router_all, gains_all = (
        lax.all_gather(qkv_weight, "batch", axis=1, tiled=True),
        lax.all_gather(out_weight, "batch", axis=1, tiled=True),
        lax.all_gather(up_weight, "batch", axis=0, tiled=True),
        lax.all_gather(down_weight, "batch", axis=1, tiled=True),
        lax.all_gather(router_weight, "batch", axis=0, tiled=True),
        lax.all_gather(norm_gains, "batch", axis=1, tiled=True),
    )
    mp_index = lax.axis_index("mp")
    mp_count = lax.axis_size("mp")
    batch_index = lax.axis_index("batch")
    batch_count = lax.axis_size("batch")
    rows_dev, length_here, width_full = tokens.shape
    width_local = width_full // mp_count
    heads_local = qkv_all.shape[2] // HEAD_DIM
    per_micro = rows_dev // MICRO
    score_scale = HEAD_DIM ** (-0.5)
    gain_attn = gains_all[0].astype(jnp.float32)
    gain_mlp = gains_all[1].astype(jnp.float32)
    router_float = router_all.astype(jnp.float32)
    first_position = mp_index * length_here
    totals = None
    shards = None
    output_list = []
    grad_list = []
    for micro_index in range(MICRO):
        row_start = micro_index * per_micro
        row_stop = row_start + per_micro
        token_rows = tokens[row_start:row_stop]
        chosen = selection[row_start:row_stop]
        cot_rows = cotangent[row_start:row_stop]
        row_count, pick_count = chosen.shape
        token_count = row_count * pick_count
        local_position = chosen - first_position
        inside = (local_position >= 0) & (local_position < length_here)
        clipped = jnp.clip(local_position, 0, length_here - 1)
        zero_low = jnp.zeros((), jnp.bfloat16)
        token_term = jnp.where(
            inside[:, :, None],
            jnp.take_along_axis(token_rows, clipped[:, :, None], axis=1),
            zero_low,
        ).reshape(token_count, width_full)
        cot_term = jnp.where(
            inside[:, :, None], jnp.take_along_axis(cot_rows, clipped[:, :, None], axis=1), zero_low
        ).reshape(token_count, width_full)
        picked_float = lax.psum(token_term, "mp").astype(jnp.float32)
        cot_float = lax.psum(cot_term, "mp").astype(jnp.float32)
        picked_full = picked_float.astype(jnp.bfloat16)
        picked_local = lax.dynamic_slice_in_dim(picked_full, mp_index * width_local, width_local, 1)
        cot_local = lax.dynamic_slice_in_dim(cot_float, mp_index * width_local, width_local, 1)
        picked_segments = jnp.take_along_axis(segments[row_start:row_stop], chosen, axis=1)
        allowed = (chosen[:, None, None, :] <= chosen[:, None, :, None]) & (
            picked_segments[:, None, None, :] == picked_segments[:, None, :, None]
        )
        router_gate = jax.nn.sigmoid(
            jnp.dot(picked_full, router_all, preferred_element_type=jnp.float32)
        )
        scaled_attn, inverse_attn = rms_parts(picked_float)
        normed = (scaled_attn * gain_attn).astype(jnp.bfloat16)
        projected = jnp.einsum(
            "td,cde->cte", normed, qkv_all, preferred_element_type=jnp.float32
        ).astype(jnp.bfloat16)
        shaped = projected.reshape(3, row_count, pick_count, heads_local, HEAD_DIM)
        queries = shaped[0]
        key_rows = shaped[1]
        value_rows = shaped[2]
        scores = (
            jnp.einsum("rqhe,rkhe->rhqk", queries, key_rows, preferred_element_type=jnp.float32)
            * score_scale
        )
        masked = jnp.where(allowed, scores, MASKED)
        highest_score = jnp.max(masked, axis=-1, keepdims=True)
        exponent = jnp.exp(masked - highest_score)
        exp_total = jnp.sum(exponent, axis=-1, keepdims=True)
        log_total = highest_score + jnp.log(exp_total)
        attention_low = (exponent / exp_total).astype(jnp.bfloat16)
        attended = jnp.einsum(
            "rhqk,rkhe->rqhe", attention_low, value_rows, preferred_element_type=jnp.float32
        )
        attended = attended.reshape(token_count, heads_local * HEAD_DIM).astype(jnp.bfloat16)
        attn_local = lax.psum_scatter(
            jnp.dot(attended, out_all, preferred_element_type=jnp.float32),
            "mp",
            scatter_dimension=1,
            tiled=True,
        )
        middle_local = picked_local.astype(jnp.float32) + attn_local
        middle = lax.all_gather(middle_local, "mp", axis=1, tiled=True)
        scaled_mlp, inverse_mlp = rms_parts(middle)
        normed_mid = (scaled_mlp * gain_mlp).astype(jnp.bfloat16)
        hidden = jnp.dot(normed_mid, up_all, preferred_element_type=jnp.float32)
        active = jax.nn.gelu(hidden).astype(jnp.bfloat16)
        mlp_local = lax.psum_scatter(
            jnp.dot(active, down_all, preferred_element_type=jnp.float32).astype(jnp.bfloat16),
            "mp",
            scatter_dimension=1,
            tiled=True,
        ).astype(jnp.float32)
        branch_local = attn_local + mlp_local
        output_local = (
            picked_local.astype(jnp.float32) + router_gate[:, None] * branch_local
        ).astype(jnp.bfloat16)
        output_full = lax.all_gather(output_local, "mp", axis=1, tiled=True)
        grad_gate = lax.psum(jnp.sum(cot_local * branch_local, axis=1), "mp")
        direct = router_gate[:, None] * cot_float
        grad_mlp = direct.astype(jnp.bfloat16)
        down_part = jnp.einsum("tf,td->fd", active, grad_mlp, preferred_element_type=jnp.float32)
        grad_active = jnp.einsum(
            "td,fd->tf", grad_mlp, down_all, preferred_element_type=jnp.float32
        )
        gelu_values, gelu_pull = jax.vjp(jax.nn.gelu, hidden)
        grad_hidden = gelu_pull(grad_active)[0].astype(jnp.bfloat16)
        up_part = jnp.einsum(
            "td,tf->df", normed_mid, grad_hidden, preferred_element_type=jnp.float32
        )
        grad_normed_mid = lax.psum(
            jnp.einsum("tf,df->td", grad_hidden, up_all, preferred_element_type=jnp.float32), "mp"
        )
        grad_middle, gain_mlp_part = norm_back(grad_normed_mid, gain_mlp, scaled_mlp, inverse_mlp)
        grad_attn = (grad_middle + direct).astype(jnp.bfloat16)
        out_part = jnp.einsum("te,td->ed", attended, grad_attn, preferred_element_type=jnp.float32)
        grad_attended = jnp.einsum(
            "td,ed->te", grad_attn, out_all, preferred_element_type=jnp.float32
        ).astype(jnp.bfloat16)
        grad_attended = grad_attended.reshape(row_count, pick_count, heads_local, HEAD_DIM)
        scores_again = (
            jnp.einsum("rqhe,rkhe->rhqk", queries, key_rows, preferred_element_type=jnp.float32)
            * score_scale
        )
        attention = jnp.exp(jnp.where(allowed, scores_again, MASKED) - log_total)
        grad_values = jnp.einsum(
            "rhqk,rqhe->rkhe",
            attention.astype(jnp.bfloat16),
            grad_attended,
            preferred_element_type=jnp.float32,
        )
        grad_weights = jnp.einsum(
            "rqhe,rkhe->rhqk", grad_attended, value_rows, preferred_element_type=jnp.float32
        )
        grad_scores = (
            attention * (grad_weights - jnp.sum(attention * grad_weights, axis=-1, keepdims=True))
        ).astype(jnp.bfloat16)
        grad_queries = (
            jnp.einsum("rhqk,rkhe->rqhe", grad_scores, key_rows, preferred_element_type=jnp.float32)
            * score_scale
        )
        grad_keys = (
            jnp.einsum("rhqk,rqhe->rkhe", grad_scores, queries, preferred_element_type=jnp.float32)
            * score_scale
        )
        grad_projected = (
            jnp.stack([grad_queries, grad_keys, grad_values])
            .reshape(3, token_count, heads_local * HEAD_DIM)
            .astype(jnp.bfloat16)
        )
        qkv_part = jnp.einsum(
            "td,cte->cde", normed, grad_projected, preferred_element_type=jnp.float32
        )
        grad_normed = lax.psum(
            jnp.einsum(
                "cte,cde->td", grad_projected, qkv_all, preferred_element_type=jnp.float32
            ).astype(jnp.bfloat16),
            "mp",
        ).astype(jnp.float32)
        grad_norm_in, gain_attn_part = norm_back(grad_normed, gain_attn, scaled_attn, inverse_attn)
        grad_logit = grad_gate * router_gate * (1.0 - router_gate)
        router_part = jnp.dot(grad_logit, picked_float, precision=lax.Precision.HIGHEST)
        grad_full = cot_float + grad_middle + grad_norm_in + grad_logit[:, None] * router_float
        row_positions = jnp.arange(row_count)[:, None]
        write_index = jnp.where(inside, local_position, length_here)
        output_rows = token_rows.at[row_positions, write_index].set(
            output_full.reshape(row_count, pick_count, width_full), mode="drop"
        )
        grad_rows = (
            cot_rows.astype(jnp.float32)
            .at[row_positions, write_index]
            .set(grad_full.reshape(row_count, pick_count, width_full), mode="drop")
        )
        gradients = (
            qkv_part,
            out_part,
            up_part,
            down_part,
            router_part,
            jnp.stack([gain_attn_part, gain_mlp_part]),
        )
        gradients, output_rows, grad_rows = (gradients, output_rows, grad_rows)
        output_list.append(output_rows)
        grad_list.append(grad_rows)
        totals = gradients if totals is None else jax.tree.map(jnp.add, totals, gradients)
    shards = (
        lax.psum_scatter(totals[0], "batch", scatter_dimension=1, tiled=True),
        lax.psum_scatter(totals[1], "batch", scatter_dimension=1, tiled=True),
        lax.psum_scatter(totals[2], "batch", scatter_dimension=0, tiled=True),
        lax.psum_scatter(totals[3], "batch", scatter_dimension=1, tiled=True),
        lax.psum_scatter(totals[4], "batch", scatter_dimension=0, tiled=True),
        lax.psum_scatter(totals[5], "batch", scatter_dimension=1, tiled=True),
    )
    block_output = jnp.concatenate(output_list, axis=0)
    input_grad = jnp.concatenate(grad_list, axis=0)
    qkv_grad, out_grad, up_grad, down_grad, router_grad, gains_grad = shards
    first_mp = (mp_index == 0).astype(jnp.float32)
    qkv_old = qkv_weight.astype(jnp.float32)
    out_old = out_weight.astype(jnp.float32)
    up_old = up_weight.astype(jnp.float32)
    down_old = down_weight.astype(jnp.float32)
    router_old = router_weight.astype(jnp.float32)
    gains_old = norm_gains.astype(jnp.float32)
    qkv_row_term, qkv_col_term = factor_terms(
        qkv_grad, qkv_rows, qkv_cols, batch_index, batch_count, mp_index, mp_count
    )
    out_row_term, out_col_term = factor_terms(
        out_grad, out_rows, out_cols, mp_index, mp_count, batch_index, batch_count
    )
    up_row_term, up_col_term = factor_terms(
        up_grad, up_rows, up_cols, batch_index, batch_count, mp_index, mp_count
    )
    down_row_term, down_col_term = factor_terms(
        down_grad, down_rows, down_cols, mp_index, mp_count, batch_index, batch_count
    )
    weight_squares = jnp.concatenate(
        [
            jnp.sum(qkv_old * qkv_old, axis=(1, 2)),
            jnp.stack(
                [
                    jnp.sum(out_old * out_old),
                    jnp.sum(up_old * up_old),
                    jnp.sum(down_old * down_old),
                    first_mp * jnp.sum(router_old * router_old),
                ]
            ),
            first_mp * jnp.sum(gains_old * gains_old, axis=1),
        ]
    )
    (
        qkv_row_full,
        qkv_col_full,
        out_row_full,
        out_col_full,
        up_row_full,
        up_col_full,
        down_row_full,
        down_col_full,
        weight_sums,
    ) = lax.psum(
        (
            qkv_row_term,
            qkv_col_term,
            out_row_term,
            out_col_term,
            up_row_term,
            up_col_term,
            down_row_term,
            down_col_term,
            weight_squares,
        ),
        ("batch", "mp"),
    )
    qkv_dir, qkv_rows_new, qkv_cols_new = factor_direction(
        qkv_grad, qkv_row_full, qkv_col_full, batch_index, mp_index
    )
    out_dir, out_rows_new, out_cols_new = factor_direction(
        out_grad, out_row_full, out_col_full, mp_index, batch_index
    )
    up_dir, up_rows_new, up_cols_new = factor_direction(
        up_grad, up_row_full, up_col_full, batch_index, mp_index
    )
    down_dir, down_rows_new, down_cols_new = factor_direction(
        down_grad, down_row_full, down_col_full, mp_index, batch_index
    )
    router_moment_new = DECAY * router_moment + (1.0 - DECAY) * (
        router_grad * router_grad + EPS_SQUARE
    )
    router_dir = router_grad * lax.rsqrt(router_moment_new)
    gains_moment_new = DECAY * gains_moment + (1.0 - DECAY) * (gains_grad * gains_grad + EPS_SQUARE)
    gains_dir = gains_grad * lax.rsqrt(gains_moment_new)
    update_squares = jnp.concatenate(
        [
            jnp.sum(qkv_dir * qkv_dir, axis=(1, 2)),
            jnp.stack(
                [
                    jnp.sum(out_dir * out_dir),
                    jnp.sum(up_dir * up_dir),
                    jnp.sum(down_dir * down_dir),
                    first_mp * jnp.sum(router_dir * router_dir),
                ]
            ),
            first_mp * jnp.sum(gains_dir * gains_dir, axis=1),
        ]
    )
    update_sums = lax.psum(update_squares, ("batch", "mp"))
    entries = jnp.array([D * D, D * D, D * D, D * D, D * FF, FF * D, D, D, D], jnp.float32)
    update_rms = jnp.sqrt(update_sums / entries)
    weight_rms = jnp.sqrt(weight_sums / entries)
    factors = RATE * weight_rms / jnp.maximum(1.0, update_rms / CLIP_RMS)
    qkv_new = qkv_old - factors[0:3, None, None] * qkv_dir
    out_new = out_old - factors[3] * out_dir
    up_new = up_old - factors[4] * up_dir
    down_new = down_old - factors[5] * down_dir
    router_new = router_old - factors[6] * router_dir
    gains_new = gains_old - factors[7:9, None] * gains_dir
    return (
        block_output,
        input_grad,
        qkv_grad,
        qkv_rows_new,
        qkv_cols_new,
        qkv_new,
        out_grad,
        out_rows_new,
        out_cols_new,
        out_new,
        up_grad,
        up_rows_new,
        up_cols_new,
        up_new,
        down_grad,
        down_rows_new,
        down_cols_new,
        down_new,
        router_grad,
        router_moment_new,
        router_new,
        gains_grad,
        gains_moment_new,
        gains_new,
        update_rms,
    )


BF=jnp.bfloat16; F32=jnp.float32
EPS_NORM=1e-6; MASKED=-1e30; HD=64
GC=0.7978845608028654; GA=0.044715
def nn(a,b): return jnp.dot(a,b,preferred_element_type=F32)
def nt(a,b): return lax.dot_general(a,b,(((1,),(1,)),((),())),preferred_element_type=F32)
def tn(a,b): return lax.dot_general(a,b,(((0,),(0,)),((),())),preferred_element_type=F32)
def vectors(vec_ref):
    nb=vec_ref.shape[0]
    vec=jnp.concatenate([vec_ref[b,:,0:768//nb] for b in range(nb)],axis=1)
    return vec[0:1,:],vec[1:2,:],vec[2:3,:]
def root(v): return lax.rsqrt(jnp.mean(v*v,axis=1,keepdims=True)+EPS_NORM)


MESH=pl.DeviceIdType.MESH
class Plane:
    def __init__(s):
        s.b=lax.axis_index("batch"); s.m=lax.axis_index("mp")
        s.z=s.b//2; s.y=lax.rem(s.b,2); s.x=s.m//2; s.c=lax.rem(s.m,2)
        s.left=(s.b-2,s.m); s.right=(s.b+2,s.m)
        s.ypeer=(s.z*2+1-s.y,s.m); s.xpeer=(s.b,(1-s.x)*2+s.c); s.core=(s.b,s.x*2+1-s.c)


FORE_ORDER=(('S',1,'X',),('S',0,'L',),('S',0,'R',),('S',1,'Y',),('PK',0,0,),('S',2,'R',),('FY',0,0,2,0,),('FX',0,2,0,),('S',2,'L',),('PK',1,0,),('FY',2,0,2,0,),('ZA',0,1,0,),('ZA',0,0,0,),('FX',0,0,0,),('CMB',0,),('TX',0,1,),('FY',0,0,1,0,),('ZA',2,1,0,),('PK',0,1,),('ZA',0,1,1,),('FY',0,0,0,0,),('FY',0,0,1,1,),('YA2',1,0,),('TX',0,0,),('PK',1,1,),('FY',0,1,2,0,),('YA',0,0,2,0,),('PK',3,1,),('ZA',0,0,1,),('S',1,'Z',),('PK',2,0,),('PK',2,1,),('ZA',0,1,2,),('ZA',2,0,0,),('ZA',2,1,1,),('FY',0,0,1,2,),('YA',0,0,1,0,),('FY',0,0,0,1,),('FX',0,0,1,),('ZA',0,0,2,),('FY',0,0,0,2,),('FY',0,1,0,0,),('FX',0,1,2,),('YA',2,0,2,0,),('XA2',1,),('FX',0,1,1,),('ZA2',1,0,1,0,0,),('CMB',1,),('YA',0,0,0,0,),('FX',0,1,0,),('PK',3,0,),('FX',0,0,2,),('TX',1,1,),('ZA2',1,0,1,1,0,),('ZA',2,0,1,),('ZA2',1,0,0,0,0,),('YA',0,0,1,2,),('YA',0,0,0,2,),('FX',2,0,1,),('TX',1,0,),('ZA2',1,0,0,1,0,),('YA',0,0,1,1,),('YA',0,0,0,1,),('SEL',0,),('NRM',),('QKV',1,),('QKV',0,),('FY',0,1,0,1,),('FY',0,1,1,2,),('FY',0,1,1,1,),('HD',0,),('YA',0,1,0,0,),('FY',0,1,0,2,),('ZA',2,1,2,),('FX',2,1,2,),('ZA',2,0,2,),('FY',0,1,1,0,),('HD',1,),('FY',2,0,0,0,),('ZA2',1,0,0,1,1,),('FX',2,2,0,),('FX',2,1,1,),('FX',2,0,2,),('ZA2',1,0,0,0,1,),('YA',0,1,2,0,),('ZA2',1,0,1,1,1,),('FY',2,0,1,1,),('ZA2',1,0,1,0,1,),('YA2',1,1,),('FY',2,0,0,1,),('FY',2,0,0,2,),('ZA2',1,1,0,0,0,),('FY',2,0,1,0,),('ZA2',1,1,0,1,0,),('YA',0,1,1,1,),('YA',0,1,1,2,),('YA',0,1,0,1,),('FY',2,0,1,2,),('YA',0,1,1,0,),('YA',0,1,0,2,),('QKV',2,),('HD',2,),('QKV',3,),('HD',3,),('ZA2',1,0,0,0,2,),('ZA2',1,0,1,1,2,),('ZA2',1,0,0,1,2,),('ZA2',1,0,1,0,2,),('OUT',),('ML',0,0,),('ML',1,0,),('FY',2,1,0,1,),('YA',2,0,1,1,),('FX',2,0,0,),('YA',2,0,0,0,),('ZA2',1,1,1,0,0,),('ZA2',1,1,1,1,0,),('ZA2',1,1,0,0,1,),('YA',2,0,0,2,),('YA',2,0,1,0,),('YA',2,0,1,2,),('YA',2,0,0,1,),('ZA2',1,1,1,0,1,),('ZA2',1,1,0,1,1,),('FX',2,1,0,),('YA',2,1,0,1,),('SEL',1,),('GM',),('ML',0,2,),('FY',2,1,1,2,),('ZA2',1,1,1,1,1,),('FY',2,1,2,0,),('ML',0,5,),('ML',0,4,),('ML',1,1,),('ML',1,2,),('ZA2',1,1,1,0,2,),('ZA2',1,1,0,0,2,),('ZA2',1,1,1,1,2,),('ML',0,1,),('ZA2',1,1,0,1,2,),('FY',2,1,1,1,),('FY',2,1,0,2,),('FY',2,1,0,0,),('ML',1,4,),('ML',1,3,),('ML',1,5,),('ML',0,3,),('ML',2,0,),('FY',2,1,1,0,),('YA',2,1,0,2,),('ML',3,0,),('YA',2,1,2,0,),('YA',2,1,0,0,),('ML',2,1,),('YA',2,1,1,2,),('ML',3,1,),('YA',2,1,1,1,),('YA',2,1,1,0,),('ML',2,2,),('ML',2,5,),('ML',3,2,),('ML',3,4,),('ML',3,5,),('ML',2,3,),('ML',2,4,),('END',),('ML',3,3,))


def fore_kernel(order, nz, rp, picks, qkvw_ref, outw_ref, upw_ref, dnw_ref, router_ref, gains_ref, tok_ref, cot_ref, pick_ref, segm_ref,
                w_ref, W0_out, Gown, Gpart, sel_out, P_out, probs_out, att_out, mid_out, accb_out, rows_out, gg_ref, vall_ref,
                W, tokb, cotb, zbuf, ra, rb, rx, normed, P, probs, att, mid, ba, nm, gm, acc, accb, nmT, gmT, gst, v_ref, selT, segl, segT,
                tsem, csem, rsem, ssem, shS, shR, txS, txR, vs, vr, gS, gR, gL, osem):
    D=768; nb=2*nz; T=nm.shape[0]; length=tok_ref.shape[1]; R=T//picks
    p=Plane()
    bpeers=[(lax.rem(p.b+k,nb),p.m) for k in range(1,nb)]
    peers=bpeers+[p.xpeer,p.core]
    bar=pltpu.get_barrier_semaphore()
    for d in peers: pl.semaphore_signal(bar,inc=1,device_id=d,device_id_type=MESH)
    xo=1-p.x; yo=1-p.y; co=1-p.c
    groups=[xo*2+co,xo*2+p.c,p.x*2+co,p.m]
    def row_load(h,g,k):
        r=groups[g]*R+k; s=g*R+k
        src,dst,sem=((tok_ref,tokb,tsem),(cot_ref,cotb,csem))[h]
        return pltpu.make_async_copy(src.at[r],dst.at[s%(2*R)],sem.at[s])
    for h in (0,1):
        for g in (0,1):
            for k in range(R): row_load(h,g,k).start()
    mine=pl.ds(pl.multiple_of(p.b*rp,rp),rp)
    for j in range(3): w_ref[0,:,j*192:(j+1)*192]=qkvw_ref[j]
    w_ref[0,:,576:768]=outw_ref[...].astype(F32).T.astype(BF)
    w_ref[1]=upw_ref[...]
    w_ref[2]=dnw_ref[...]
    for i in range(3): W[i,p.m,mine]=w_ref[i]
    n96=D//nb
    v_ref[...]=jnp.concatenate([jnp.concatenate([router_ref[...].astype(F32),gains_ref[...].astype(F32),jnp.zeros((5,n96),F32)],axis=0),jnp.zeros((8,128-n96),F32)],axis=1)
    vall_ref[p.b]=v_ref[...]
    pl.semaphore_wait(bar,len(peers))
    pend=[]
    def remote(src,dst,s,r,dev):
        return pltpu.make_async_remote_copy(src_ref=src,dst_ref=dst,send_sem=s,recv_sem=r,device_id=dev,device_id_type=MESH)
    def start(cp,cond=None):
        if cond is None: cp.start()
        else:
            @pl.when(cond)
            def _(): cp.start()
        pend.append((cond,cp))
    def when(cond,f):
        if cond is None: f()
        else:
            @pl.when(cond)
            def _(): f()
    vcs=[remote(v_ref,vall_ref.at[p.b],vs.at[k],vr.at[k],d) for k,d in enumerate(bpeers)]
    for cp in vcs: start(cp)
    count=[0]*3
    def at(i,m,b): return W.at[i,m,pl.ds(pl.multiple_of(b*rp,rp),rp)]
    def fwd(i,m,b,dev,cond=None):
        s=count[i]; count[i]+=1
        start(remote(at(i,m,b),at(i,m,b),ssem.at[i,s],rsem.at[i,m,b],dev),cond)
    def arrived(i,m,b): remote(at(i,m,b),at(i,m,b),ssem.at[i,0],rsem.at[i,m,b],p.core).wait_recv()
    def mm(xr): return p.m if xr==0 else xo*2+p.c
    def zc(dr,k):
        if dr==2: return p.z,None
        return (p.z-1-k,p.z>k) if dr==0 else (p.z+1+k,p.z<nz-1-k)
    def both(a,b): return b if a is None else (a if b is None else a&b)
    def t_S(i,d):
        if d=="R": fwd(i,p.m,p.b,p.right,p.z<nz-1)
        elif d=="L": fwd(i,p.m,p.b,p.left,p.z>0)
        elif d=="X": fwd(i,p.m,p.b,p.xpeer)
        elif d=="Y": fwd(i,p.m,p.b,p.ypeer)
        else:
            fwd(i,p.m,p.b,p.right,p.z<nz-1); fwd(i,p.m,p.b,p.left,p.z>0)
    for i in range(3): fwd(i,p.m,p.b,p.core)
    def along(i,m,b,dr,cond):
        if dr==0: fwd(i,m,b,p.right,both(cond,p.z<nz-1))
        else: fwd(i,m,b,p.left,both(cond,p.z>0))
    def t_ZA(i,dr,k):
        z,c=zc(dr,k); b=z*2+p.y
        when(c,lambda: arrived(i,p.m,b))
        along(i,p.m,b,dr,c); fwd(i,p.m,b,p.core,c)
    def t_FX(i,dr,k):
        z,c=zc(dr,k); fwd(i,p.m,z*2+p.y,p.xpeer,c)
    def t_FY(i,xr,dr,k):
        z,c=zc(dr,k); b=z*2+p.y; m=mm(xr)
        if xr==1:
            when(c,lambda: arrived(i,m,b)); fwd(i,m,b,p.core,c)
        fwd(i,m,b,p.ypeer,c)
    def t_YA(i,xr,dr,k):
        z,c=zc(dr,k); b=z*2+yo; m=mm(xr)
        when(c,lambda: arrived(i,m,b)); fwd(i,m,b,p.core,c)
    def t_XA2(i):
        m=mm(1); arrived(i,m,p.b)
        fwd(i,m,p.b,p.ypeer); fwd(i,m,p.b,p.right,p.z<nz-1); fwd(i,m,p.b,p.left,p.z>0); fwd(i,m,p.b,p.core)
    def t_YA2(i,xr):
        m=mm(xr); b=p.z*2+yo; arrived(i,m,b)
        fwd(i,m,b,p.right,p.z<nz-1); fwd(i,m,b,p.left,p.z>0); fwd(i,m,b,p.core)
    def t_ZA2(i,xr,yr,dr,k):
        z,c=zc(dr,k); m=mm(xr); b=z*2+(p.y if yr==0 else yo)
        when(c,lambda: arrived(i,m,b))
        along(i,m,b,dr,c); fwd(i,m,b,p.core,c)
    ones=lax.broadcasted_iota(jnp.int32,(picks,8),1)
    def column(ref,r):
        return jnp.sum(jnp.where(ones==r,ref[...],0.0),axis=1,keepdims=True)
    def t_SG():
        sel=pick_ref[...]
        selT[...]=sel.astype(F32).T
        seg=segm_ref[...]
        own=jnp.zeros(sel.shape,F32)
        for q in range(1,8):
            begin=jnp.sum((seg<q).astype(F32),axis=1,keepdims=True)
            own=own+(sel.astype(F32)>=begin).astype(F32)
        segl[...]=own
        segT[...]=own.T
    begun=[]
    def t_PK(g,h):
        if not begun: begun.append(t_SG())
        for k in range(R):
            row_load(h,g,k).wait()
            col=column(selT,groups[g]*R+k).astype(jnp.int32)-p.m*length
            one=(col==lax.broadcasted_iota(jnp.int32,(picks,length),1)).astype(F32).astype(BF)
            buf=(tokb,cotb)[h]
            zbuf[g,k*picks:(k+1)*picks,h*D:(h+1)*D]=nn(one,buf[(g*R+k)%(2*R)]).astype(BF)
        if g<2:
            for k in range(R): row_load(h,g+2,k).start()
        if g==0: start(ship(0,h))
        if g==2: start(ship(1,h))
    cols=[slice(0,D),slice(D,2*D)]
    def ship(a,h):
        src=zbuf.at[2*a]; dst=(rb,ra)[a]
        return remote(src.at[:,cols[h]],dst.at[:,cols[h]],shS.at[a,h],shR.at[a,h],p.core)
    ch=T//2
    def tx(h,q):
        rs=pl.ds(q*ch,ch)
        return remote(zbuf.at[1,rs,cols[h]],rx.at[rs,cols[h]],txS.at[h,q],txR.at[h,q],p.xpeer)
    def t_CMB(h):
        ship(0,h).wait_recv()
        zbuf[1,:,cols[h]]=zbuf[1,:,cols[h]]+rb[:,cols[h]]
    def t_TX(h,q): start(tx(h,q))
    def t_SEL(h):
        ship(1,h).wait_recv()
        for q in (0,1): tx(h,q).wait_recv()
        zbuf[3,:,cols[h]]=zbuf[3,:,cols[h]]+ra[:,cols[h]]+rx[:,cols[h]]
    sel=zbuf.at[3]
    keep={}
    outs=[]
    def write(src,dst):
        cp=pltpu.make_async_copy(src,dst,osem.at[3+len(outs)]); cp.start(); outs.append(cp)
    def t_NRM():
        for cp in vcs: cp.wait_recv()
        router,gain0,gain1=vectors(vall_ref)
        keep["gain1"]=gain1
        x=sel[:,0:D].astype(F32)
        keep["gate"]=jax.nn.sigmoid(jnp.sum(x*router,axis=1,keepdims=True))
        normed[...]=(x*root(x)*gain0).astype(BF)
    def t_GM():
        gmv=(keep["gate"]*sel[:,D:].astype(F32)).astype(BF)
        gm[...]=gmv
        gmT[...]=gmv.T
        write(sel,sel_out)
    mis=[p.m,p.x*2+co,xo*2+p.c,xo*2+co]
    mlp=[p.x*2+co,p.m,xo*2+co,xo*2+p.c]
    def ready(i,m):
        for b in range(nb): arrived(i,m,b)
    scale=HD**-0.5
    def t_QKV(mi):
        m=mis[mi]
        if mi%2==1: ready(0,m)
        P[m]=nn(normed[...],W[0,m]).astype(BF)
    def t_HD(mi):
        m=mis[mi]
        @pl.loop(0,R)
        def _(r):
            qi=lax.broadcasted_iota(jnp.int32,(picks,picks),0); ki=lax.broadcasted_iota(jnp.int32,(picks,picks),1)
            ok=(ki<=qi)&(segl[pl.ds(p.m*R+r,1),:]==column(segT,p.m*R+r))
            rs=pl.ds(pl.multiple_of(r*picks,picks),picks)
            res=[]
            for j in range(3):
                o=j*HD
                q=P[m,rs,o:o+HD]; k=P[m,rs,192+o:192+o+HD]; v=P[m,rs,384+o:384+o+HD]
                s=jnp.where(ok,nt(q,k)*scale,MASKED)
                e=jnp.exp(s-jnp.max(s,axis=1,keepdims=True))
                pr=(e/jnp.sum(e,axis=1,keepdims=True)).astype(BF)
                probs[r,m,j]=pr
                res.append(nn(pr,v))
            att[m,rs,:]=jnp.concatenate(res,axis=1).astype(BF)
    def t_OUT():
        write(W.at[0],W0_out); write(P,P_out); write(probs,probs_out); write(att,att_out)
        a=nt(att[0],W[0,0,:,576:768])
        for m in range(1,4): a=a+nt(att[m],W[0,m,:,576:768])
        ba[...]=a
        mv=sel[:,0:D].astype(F32)+a
        mid[...]=mv
        write(mid,mid_out)
        nmv=(mv*root(mv)*keep["gain1"]).astype(BF)
        nm[...]=nmv
        nmT[...]=nmv.T
        acc[...]=jnp.zeros_like(acc)
        accb[...]=jnp.zeros_like(accb)
    def g_copy(i,mi):
        x=(p.x,p.x,xo,xo)[mi]; k=mi%2
        if k==1: return pltpu.make_async_copy(gst.at[k,i],Gown.at[i,x],gL.at[i,x])
        return remote(gst.at[k,i],Gpart.at[i,x],gS.at[i,x],gR.at[i,x],p.core)
    def g_done(i,mi):
        if mi%2==1: g_copy(i,mi).wait()
        else: g_copy(i,mi).wait_send()
    def g_out(i,mi,val):
        if mi>1: g_done(i,mi-2)
        gst[mi%2,i]=val.astype(BF)
        g_copy(i,mi).start()
    act,gh=tokb,cotb
    def t_ML(mi,part):
        m=mlp[mi]
        if part==0:
            if mi%2==0: ready(1,m)
            for t in range(3):
                cs=slice(t*256,(t+1)*256)
                h=nn(nm[...],W[1,m,:,cs])
                th=jnp.tanh(GC*(h+GA*h*h*h))
                act[mi,:,cs]=(0.5*h*(1.0+th)).astype(BF)
                gh[mi,:,cs]=(0.5*(1.0+th)+0.5*h*(1.0-th*th)*(GC*(1.0+3.0*GA*h*h))).astype(BF)
        elif part==1: g_out(1,mi,nn(gmT[...],act[mi]))
        elif part==2:
            if mi%2==0: ready(2,m)
            for t in range(3):
                cs=slice(t*256,(t+1)*256)
                gh[mi,:,cs]=(nn(gm[...],W[2,m,:,cs])*gh[mi,:,cs].astype(F32)).astype(BF)
        elif part==3: g_out(0,mi,nn(nmT[...],gh[mi]))
        elif part==4: acc[...]+=nt(act[mi],W[2,m])
        else: accb[...]+=nt(gh[mi],W[1,m])
    def t_END():
        write(accb,accb_out)
        br=ba[...]+acc[...]
        normed[...]=(sel[:,0:D].astype(F32)+keep["gate"]*br).astype(BF)
        write(normed,rows_out)
        gg_ref[...]=jnp.sum(sel[:,D:].astype(F32)*br,axis=1,keepdims=True)
    table=dict(S=t_S,ZA=t_ZA,FX=t_FX,FY=t_FY,YA=t_YA,XA2=t_XA2,YA2=t_YA2,ZA2=t_ZA2,PK=t_PK,CMB=t_CMB,TX=t_TX,SEL=t_SEL,NRM=t_NRM,GM=t_GM,QKV=t_QKV,HD=t_HD,OUT=t_OUT,ML=t_ML,END=t_END)
    for n in order: table[n[0]](*n[1:])
    for i in (0,1):
        for mi in (2,3): g_done(i,mi)
        for mi in (0,2): g_copy(i,mi).wait_recv()
    for cp in outs: cp.wait()
    for cond,cp in pend: when(cond,cp.wait_send)
def fore_call(qkv_weight,out_weight,up_weight,down_turned,router,gains,tokens,cot,selection,segments,nb,picks):
    nz=nb//2; rp=up_weight.shape[0]; rows,length,D=tokens.shape; R=rows//4; T=R*picks
    V=pltpu.VMEM; S=pltpu.SemaphoreType.DMA
    vm=pl.BlockSpec(memory_space=V); an=pl.BlockSpec(memory_space=pl.ANY)
    sd=jax.ShapeDtypeStruct
    return pl.pallas_call(functools.partial(fore_kernel,FORE_ORDER,nz,rp,picks),
        out_shape=(sd((3,rp,D),BF),sd((4,D,D),BF),sd((2,2,D,D),BF),sd((2,2,D,D),BF),sd((T,2*D),BF),sd((4,T,D),BF),sd((R,4,3,picks,picks),BF),sd((4,T,192),BF),
            sd((T,D),F32),sd((T,D),F32),sd((T,D),BF),sd((T,1),F32),sd((nb,8,128),F32)),
        in_specs=[vm]*6+[an,an,vm,vm],out_specs=(vm,)+(an,)*10+(vm,vm),
        scratch_shapes=[V((3,4,D,D),BF),V((2*R,length,D),BF),V((2*R,length,D),BF),V((4,T,2*D),BF),V((T,2*D),BF),V((T,2*D),BF),V((T,2*D),BF),
            V((T,D),BF),V((4,T,D),BF),V((R,4,3,picks,picks),BF),V((4,T,192),BF),V((T,D),F32),V((T,D),F32),V((T,D),BF),V((T,D),BF),
            V((T,D),F32),V((T,D),F32),V((D,T),BF),V((D,T),BF),V((2,2,D,D),BF),V((8,128),F32),V((picks,rows),F32),V((rows,picks),F32),V((picks,rows),F32),
            S((rows,)),S((rows,)),S((3,4,nb)),S((3,80)),S((2,2)),S((2,2)),S((2,2)),S((2,2)),S((nb,)),S((nb,)),S((2,2)),S((2,2)),S((2,2)),S((12,))],
        compiler_params=pltpu.CompilerParams(collective_id=0,has_side_effects=True,vmem_limit_bytes=60<<20),
        name="fore")(qkv_weight,out_weight,up_weight,down_turned,router,gains,tokens,cot,selection,segments)


BACK_ORDER=(('RO',2,),('AD',1,0,),('AD',1,1,),('YS',1,1,0,),('YS',1,1,1,),('RO',0,),('RO',3,),('YS',1,1,2,),('AD',2,1,),('YS',1,1,3,),('RO',1,),('YS',1,0,1,),('YS',1,0,2,),('ZL',6,),('ZR',11,),('C',0,),('AD',2,0,),('ZL',4,),('ZL',7,),('ZR',2,),('ZL',8,),('C',1,),('YR',1,1,0,),('C',2,),('C',3,),('ZL',10,),('ZL',11,),('ZR',0,),('C',4,),('C',5,),('C',6,),('C',7,),('ZR',3,),('C',8,),('C',9,),('C',10,),('YS',0,1,1,),('YR',1,1,3,),('ZR',1,),('YR',1,1,2,),('ZR',6,),('YS',0,1,0,),('YS',0,1,3,),('ZR',4,),('ZR',5,),('ZR',9,),('ZL',3,),('YS',0,1,2,),('YR',1,1,1,),('C',11,),('C',12,),('YS',1,0,0,),('YS',1,0,3,),('C',13,),('YR',0,1,1,),('ZL',0,),('C',14,),('C',15,),('ZR',7,),('YR',0,1,0,),('C',16,),('ZR',10,),('ZL',1,),('C',17,),('C',18,),('YR',0,1,3,),('C',19,),('ZL',2,),('C',20,),('YS',0,0,0,),('YS',0,0,3,),('C',21,),('ZL',5,),('ZL',9,),('YR',0,1,2,),('C',22,),('C',23,),('C',24,),('C',25,),('RG',0,),('YS',0,0,1,),('ZR',8,),('YR',1,0,1,),('YR',1,0,2,),('YR',1,0,0,),('XR',1,2,),('VS',),('LR',1,2,),('XR',1,1,),('XR',1,0,),('RG',1,),('RG',2,),('LR',1,1,),('F2',1,1,),('LL',1,0,),('VM',),('F2',0,0,),('YS',0,0,2,),('YR',1,0,3,),('XR',1,3,),('F2',1,0,),('F2',0,1,),('YR',0,0,0,),('XR',0,0,),('LL',0,0,),('LL',1,1,),('LR',1,3,),('YR',0,0,1,),('LL',1,2,),('YR',0,0,3,),('XR',0,3,),('XR',0,1,),('FY',1,),('LL',0,1,),('LR',0,3,),('RG',3,),('YR',0,0,2,),('XR',0,2,),('LL',0,2,),('FIN',1,),('ST',1,),('LR',0,2,),('LR',0,1,),('FY',0,),('FX',),('ST',2,),('FIN',0,),('ST',0,),('R1',),('RF',),('R2',),('R3',),('R4',))


EPS_SQUARE=1e-30; CLIP=0.3
ROW_CHUNKS=4
def back_kernel(order, nz, rp, nb, picks, Gown, Gpart, W_hbm, sel_hbm, P_hbm, probs_hbm, att_hbm, mid_hbm, accb_hbm, rows_hbm, gg_ref, vec_ref,
                w_ref, qr_ref, qc_ref, or_ref, oc_ref, ur_ref, uc_ref, dr_ref, dc_ref, router_ref, gains_ref, rmom_ref, gmom_ref,
                Gs_ref, out_ref, grad_ref, R_ref, C_ref, S_ref, V_ref, vdir_ref, vold_ref,
                Pl, RC, RY, RX, RLy, RRy, RLz, RRz, Fy, Fx, gst,
                W0, sel, P, probs, att, mid, accb, acc, ga, gaT, nT, gatt, gob, rows,
                vin, vmp, cin, rin, sin, smp, rloc, cloc, sloc, vsend, small, vmom_ref, rold_ref, cold_ref, rturn,
                loc, cS, cR, yS, yR, xS, xR, zS, zR, lS, lR, fS, fR, rS, rR, eS, eR):
    D=768; T=sel.shape[0]
    p=Plane()
    bpeers=[(lax.rem(p.b+k,nb),p.m) for k in range(1,nb)]
    mpeers=[(p.b,lax.rem(p.m+k,4)) for k in range(1,4)]
    bar=pltpu.get_barrier_semaphore()
    for d in bpeers+mpeers: pl.semaphore_signal(bar,inc=1,device_id=d,device_id_type=MESH)
    xo=1-p.x; yo=1-p.y; co=1-p.c
    loads={}
    def load(n,src,dst,k):
        loads[n]=pltpu.make_async_copy(src,dst,loc.at[k]); loads[n].start()
    own_blocks=[(i,x) for x in (0,1) for i in (2,1)]
    for k,(i,x) in enumerate(own_blocks):
        load((i,x),Gown.at[i-1,x],Pl.at[i,x],k)
        load((i,x,1),Gpart.at[i-1,x],RC.at[i,x],13+k)
    for k,(n,src,dst) in enumerate([(0,accb_hbm,accb),(1,mid_hbm,mid),(2,sel_hbm,sel),(3,W_hbm,W0),(4,att_hbm,att),(5,P_hbm,P),(6,probs_hbm,probs)]):
        load(n,src,dst,4+k)
    n96=D//nb
    def tile(rows):
        v=jnp.concatenate([r[...].astype(F32) for r in rows],axis=0)
        v=jnp.concatenate([v,jnp.zeros((8-v.shape[0],n96),F32)],axis=0)
        return jnp.concatenate([v,jnp.zeros((8,128-n96),F32)],axis=1)
    def line(ref): return jnp.concatenate([ref[k:k+1,:] for k in range(ref.shape[0])],axis=1)
    vold_ref[...]=tile([router_ref,gains_ref])
    vmom_ref[...]=tile([rmom_ref,gmom_ref])
    rold_ref[...]=jnp.concatenate([tile([qr_ref,oc_ref,ur_ref,dc_ref]).T[0:rp],jnp.zeros((rp,120),F32)],axis=1)
    cold_ref[...]=jnp.concatenate([jnp.concatenate([qc_ref[0:1],qc_ref[1:2],qc_ref[2:3],or_ref[...]],axis=1),line(uc_ref),line(dr_ref),jnp.zeros((5,D),F32)],axis=0)
    pl.semaphore_wait(bar,nb-1+3)
    pend=[]
    def remote(src,dst,s,r,dev):
        return pltpu.make_async_remote_copy(src_ref=src,dst_ref=dst,send_sem=s,recv_sem=r,device_id=dev,device_id_type=MESH)
    def start(cp): cp.start(); pend.append((None,cp))
    def part(ref,b): return ref.at[pl.ds(pl.multiple_of(b*rp,rp),rp)]
    def shard(i,x,b): return Pl.at[i,x,pl.ds(pl.multiple_of(b*rp,rp),rp)]
    def add(dst,*src):
        @pl.loop(0,rp,step=32)
        def _(k):
            ks=pl.ds(pl.multiple_of(k,32),32)
            v=dst[ks].astype(F32)
            for q in src: v=v+q[ks].astype(F32)
            dst[ks]=v.astype(BF)
    def core_copy(i,x,src): return remote(src,RC.at[i,x],cS.at[i,x],cR.at[i,x],p.core)
    def t_AD(i,x):
        loads[(i,x)].wait(); loads[(i,x,1)].wait()
        dst=Pl.at[i,x]; src=RC.at[i,x]
        @pl.loop(0,D,step=64)
        def _(k):
            ks=pl.ds(pl.multiple_of(k,64),64)
            dst[ks]=(dst[ks].astype(F32)+src[ks].astype(F32)).astype(BF)
    ax=lambda xr: p.x if xr==0 else xo
    ay=lambda yr: p.y if yr==0 else yo
    def ys_copy(g,xr,z): return remote(shard(g,ax(xr),z*2+yo),RY.at[g,ax(xr),z],yS.at[g,xr,z],yR.at[g,ax(xr),z],p.ypeer)
    def xs_copy(g,z): return remote(shard(g,xo,z*2+p.y),RX.at[g,z],xS.at[g,z],xR.at[g,z],p.xpeer)
    def t_YS(g,xr,z): start(ys_copy(g,xr,z))
    def t_YR(g,xr,z):
        ys_copy(g,xr,z).wait_recv()
        add(shard(g,ax(xr),z*2+p.y),RY.at[g,ax(xr),z])
        if xr==1: start(xs_copy(g,z))
    def t_XR(g,z):
        xs_copy(g,z).wait_recv(); add(shard(g,p.x,z*2+p.y),RX.at[g,z])
    def guarded(cond,cp,more,recv,dst):
        @pl.when(cond)
        def _():
            @pl.when(more)
            def _(): cp.wait_recv(); add(dst,recv)
            cp.start()
        pend.append((cond,cp))
    def t_LR(g,t):
        cp=remote(shard(g,p.x,t*2+p.y),RLy.at[g,t],lS.at[g,0,t],lR.at[g,0,t],p.right)
        guarded(p.z<t,cp,p.z>0,RLy.at[g,t],shard(g,p.x,t*2+p.y))
    def t_LL(g,t):
        cp=remote(shard(g,p.x,t*2+p.y),RRy.at[g,t],lS.at[g,1,t],lR.at[g,1,t],p.left)
        guarded(p.z>t,cp,p.z<nz-1,RRy.at[g,t],shard(g,p.x,t*2+p.y))
    def t_ZR(k):
        t=nz-1-k//4; c=k%4; sh=shard(2,c//2,t*2+c%2)
        cp=remote(sh,RLz.at[c,t],zS.at[c,0,t],zR.at[c,0,t],p.right)
        guarded(p.z<t,cp,p.z>0,RLz.at[c,t],sh)
    def t_ZL(k):
        t=k//4; c=k%4; sh=shard(2,c//2,t*2+c%2)
        cp=remote(sh,RRz.at[c,t],zS.at[c,1,t],zR.at[c,1,t],p.left)
        guarded(p.z>t,cp,p.z<nz-1,RRz.at[c,t],sh)
    def last(RL,RR,rl,rr,dst):
        @pl.when(p.z>0)
        def _(): rl.wait_recv(); add(dst,RL)
        @pl.when(p.z<nz-1)
        def _(): rr.wait_recv(); add(dst,RR)
    def fy_copy(xr): return remote(shard(2,ax(xr),p.z*2+yo),Fy.at[ax(xr)],fS.at[0,xr],fR.at[0,ax(xr)],p.ypeer)
    def fx_copy(): return remote(shard(2,xo,p.b),Fx,fS.at[1,0],fR.at[1,0],p.xpeer)
    def t_F2(xr,yr):
        c=ax(xr)*2+ay(yr); sh=shard(2,ax(xr),p.z*2+ay(yr))
        rl=remote(sh,RLz.at[c,p.z],zS.at[0,0,0],zR.at[c,0,p.z],p.right)
        rr=remote(sh,RRz.at[c,p.z],zS.at[0,1,0],zR.at[c,1,p.z],p.left)
        last(RLz.at[c,p.z],RRz.at[c,p.z],rl,rr,sh)
        if yr==1: start(fy_copy(xr))
    def t_FY(xr):
        fy_copy(xr).wait_recv(); add(shard(2,ax(xr),p.b),Fy.at[ax(xr)])
        if xr==1: start(fx_copy())
    def t_FX():
        fx_copy().wait_recv()
        Gs_ref[2]=shard(2,p.x,p.b)[...].astype(F32)+Fx[...].astype(F32)
    def t_FIN(g):
        sh=shard(g,p.x,p.b)
        Gs_ref[g]=sh[...].astype(F32)
        @pl.when(p.z>0)
        def _():
            remote(sh,RLy.at[g,p.z],lS.at[g,0,0],lR.at[g,0,p.z],p.right).wait_recv()
            Gs_ref[g]+=RLy[g,p.z].astype(F32)
        @pl.when(p.z<nz-1)
        def _():
            remote(sh,RRy.at[g,p.z],lS.at[g,1,0],lR.at[g,1,p.z],p.left).wait_recv()
            Gs_ref[g]+=RRy[g,p.z].astype(F32)
    ch=T//ROW_CHUNKS
    def row_copy(k,q):
        src,dst=((rows_hbm,out_ref),(rows,grad_ref))[k]
        return remote(src.at[pl.ds(q*ch,ch)],dst.at[p.m,pl.ds(q*ch,ch)],rS.at[k,q],rR.at[k,q],p.xpeer)
    xm=xo*2+p.c
    def core_rows(k):
        src,dst=((rows_hbm,out_ref),(rows,grad_ref))[k]
        return remote(src,dst.at[p.m],rS.at[k,4],rR.at[k,4],p.core),pltpu.make_async_copy(src,dst.at[p.m],loc.at[11+k])
    def fwd_rows(k):
        dst=(out_ref,grad_ref)[k]
        return remote(dst.at[xm],dst.at[xm],rS.at[k,5],rR.at[k,5],p.core)
    def t_RO(q):
        start(row_copy(0,q))
        if q==0:
            cp,lc=core_rows(0); start(cp); lc.start()
    def t_RG(q):
        start(row_copy(1,q))
        if q==0:
            cp,lc=core_rows(1); start(cp); lc.start()
    def t_RF():
        for k in range(2):
            for q in range(ROW_CHUNKS): row_copy(k,q).wait_recv()
            start(fwd_rows(k))
    router,gain0,gain1=vectors(vec_ref)
    scale=HD**-0.5
    ms=[xo*2+co,xo*2+p.c,p.x*2+co,p.x*2+p.c]
    keep={}
    def gate_of(): return jax.nn.sigmoid(jnp.sum(sel[:,0:D].astype(F32)*router,axis=1,keepdims=True))
    def back(e,gain,scaled,iv):
        eg=e*gain
        return iv*(eg-scaled*jnp.mean(eg*scaled,axis=1,keepdims=True)),jnp.sum(e*scaled,axis=0,keepdims=True)
    def c_first():
        for n in (0,1,2): loads[n].wait()
        iv=root(mid[...])
        gmid,g1=back(accb[...],gain1,mid[...]*iv,iv)
        small[2:3,:]=g1
        mid[...]=gmid
        gv=(gmid+gate_of()*sel[:,D:].astype(F32)).astype(BF)
        ga[...]=gv
        gaT[...]=gv.T
        xv=sel[:,0:D].astype(F32)
        nT[...]=(xv*root(xv)*gain0).astype(BF).T
        acc[...]=jnp.zeros_like(acc)
        for n in (3,4,5,6): loads[n].wait()
    def c_out(mi):
        m=ms[mi]
        gatt[...]=nn(ga[...],W0[m,:,576:768]).astype(BF)
        gob[...]=nn(gaT[...],att[m])
    def c_head(mi,j):
        m=ms[mi]; o=j*HD
        @pl.loop(0,T//picks)
        def _(r):
            rs=pl.ds(pl.multiple_of(r*picks,picks),picks)
            q=P[m,rs,o:o+HD]; k=P[m,rs,192+o:192+o+HD]; v=P[m,rs,384+o:384+o+HD]
            g=gatt[rs,o:o+HD]
            pr=probs[r,m,j]
            gp=nt(g,v)
            pf=pr.astype(F32)
            ds=(pf*(gp-jnp.sum(pf*gp,axis=1,keepdims=True))).astype(BF)
            P[m,rs,o:o+HD]=(nn(ds,k)*scale).astype(BF)
            P[m,rs,192+o:192+o+HD]=(tn(ds,q)*scale).astype(BF)
            P[m,rs,384+o:384+o+HD]=tn(pr,g).astype(BF)
    def c_block(mi):
        m=ms[mi]; x=(xo,xo,p.x,p.x)[mi]
        g=nn(nT[...],P[m,:,0:576])
        if mi%2==0:
            s=mi//2
            gst[s,:,0:576]=g.astype(BF); gst[s,:,576:768]=gob[...].astype(BF)
            start(core_copy(0,x,gst.at[s]))
        else:
            core_copy(0,x,gst.at[0]).wait_recv()
            Pl[0,x,:,0:576]=(g+RC[0,x,:,0:576].astype(F32)).astype(BF)
            Pl[0,x,:,576:768]=(gob[...]+RC[0,x,:,576:768].astype(F32)).astype(BF)
    def c_norm(mi):
        m=ms[mi]
        acc[...]+=nt(P[m,:,0:576],W0[m,:,0:576])
    vcs=[]
    def c_last():
        xv=sel[:,0:D].astype(F32); gate=gate_of()
        glog=gg_ref[...]*gate*(1.0-gate)
        iv=root(xv)
        gin,g0=back(acc[...],gain0,xv*iv,iv)
        small[0:1,:]=jnp.sum(glog*xv,axis=0,keepdims=True)
        small[1:2,:]=g0
        small[3:8,:]=jnp.zeros((5,D),F32)
        rows[...]=(sel[:,D:].astype(F32)+mid[...]+gin+glog*router).astype(BF)
        n=D//nb
        for k in range(nb):
            vsend[k]=jnp.concatenate([small[:,k*n:(k+1)*n],jnp.zeros((8,128-n),F32)],axis=1)
        for k,d in enumerate(bpeers):
            cp=remote(vsend.at[d[0]],vin.at[k],eS.at[0,k],eR.at[0,k],d); start(cp); vcs.append(cp)
    def t_C(i):
        if i==0: c_first()
        elif i<=20:
            mi,k=divmod(i-1,5)
            if k==0: c_out(mi)
            elif k<4: c_head(mi,k-1)
            else: c_block(mi)
        elif i<=24: c_norm(i-21)
        else: c_last()
    table=dict(YS=t_YS,YR=t_YR,XR=t_XR,LR=t_LR,LL=t_LL,ZR=t_ZR,ZL=t_ZL,F2=t_F2,FY=t_FY,FX=t_FX,FIN=t_FIN,RO=t_RO,RG=t_RG,RF=t_RF,C=t_C,AD=t_AD)
    lanes=lax.broadcasted_iota(jnp.int32,(8,128),1); sub=lax.broadcasted_iota(jnp.int32,(8,128),0)
    keep["tile"]=jnp.zeros((8,128),F32)
    def put(row,lane,val): keep["tile"]=keep["tile"]+jnp.where((lanes==lane)&(sub==row),val,0.0)
    def tot(v): return jnp.sum(jnp.sum(v,axis=0,keepdims=True),axis=1,keepdims=True)
    def blocks(i): return [(j,slice(j*192,(j+1)*192)) for j in range(4)] if i==0 else [(3+i,slice(0,D))]
    rlane=lax.broadcasted_iota(jnp.int32,(rp,128),1)
    def t_VS():
        for cp in vcs: cp.wait_recv()
        vs=vsend[p.b]
        for k in range(nb-1): vs=vs+vin[k]
        vsend[p.b]=vs
        keep["vms"]=[]
        for k,d in enumerate(mpeers):
            cp=remote(vsend.at[p.b],vmp.at[k],eS.at[1,k],eR.at[1,k],d); start(cp); keep["vms"].append(cp)
        for i in range(3):
            for (j,s) in blocks(i):
                wv=w_ref[i,:,s].astype(F32); put(2,j,tot(wv*wv))
        for j in range(3):
            wv=vold_ref[j:j+1,:]; put(2,6+j,tot(wv*wv)*0.25); put(0,6+j,1.0/(4*nb))
    def t_VM():
        for cp in keep["vms"]: cp.wait_recv()
        vs=vsend[p.b]
        for k in range(3): vs=vs+vmp[k]
        V_ref[0:8,:]=vs
        mom=0.5*vmom_ref[...]+0.5*(vs*vs+EPS_SQUARE)
        V_ref[8:16,:]=mom
        vd=jnp.where(lanes<D//nb,vs*lax.rsqrt(mom),0.0)
        vdir_ref[...]=vd
        for j in range(3): put(1,6+j,tot(vd[j:j+1]*vd[j:j+1])*0.25)
        cloc[...]=jnp.zeros_like(cloc)
        rloc[...]=jnp.zeros_like(rloc)
    def t_ST(i):
        sq=Gs_ref[i]; sq=sq*sq+EPS_SQUARE
        for (j,s) in blocks(i): rloc[...]+=jnp.where(rlane==j,jnp.sum(sq[:,s],axis=1,keepdims=True),0.0)
        line=jnp.sum(sq,axis=0,keepdims=True)
        for k in range(D//128): cloc[i*(D//128)+k:i*(D//128)+k+1,:]=line[:,k*128:(k+1)*128]
    def t_R1():
        rturn[...]=jnp.concatenate([rloc[...].T[0:8],jnp.zeros((8,128-rp),F32)],axis=1)
        ccs=[];rcs=[]
        for k,d in enumerate(bpeers):
            cp=remote(cloc,cin.at[k],eS.at[2,k],eR.at[2,k],d); start(cp); ccs.append(cp)
        for k,d in enumerate(mpeers):
            cp=remote(rturn,rin.at[k],eS.at[3,k],eR.at[3,k],d); start(cp); rcs.append(cp)
        keep["ccs"],keep["rcs"]=ccs,rcs
    def t_R2():
        for cp in keep["rcs"]: cp.wait_recv()
        rs=(rturn[...]+rin[0]+rin[1]+rin[2]).T[0:rp]
        rs=jnp.concatenate([rs,jnp.zeros((rp,120),F32)],axis=1)
        ncol=jnp.where(rlane>=4,1.0/3072.0,1.0/768.0)
        rnew=0.5*rold_ref[...]+0.5*rs*ncol
        R_ref[...]=rnew
        for cp in keep["ccs"]: cp.wait_recv()
        cs=cloc[...]
        for k in range(nb-1): cs=cs+cin[k]
        n6=D//128
        cs=jnp.concatenate([jnp.concatenate([cs[i*n6+k:i*n6+k+1] for k in range(n6)],axis=1) for i in range(3)]+[jnp.zeros((5,D),F32)],axis=0)
        cnew=0.5*cold_ref[...]+0.5*cs*(1.0/768.0)
        C_ref[...]=cnew
        cinv=1.0/cnew; rinv=1.0/rnew
        for i in range(3):
            g=Gs_ref[i]; g2=g*g*cinv[i:i+1,:]
            for (j,s) in blocks(i):
                put(1,j,tot(g2[:,s]*rinv[:,j:j+1]))
        for j in (0,1,2,4): put(0,j,tot(rnew[:,j:j+1])*(1.0/(768*4)))
        put(0,3,tot(cnew[0:1,576:768])*(1.0/(768*nb)))
        put(0,5,tot(cnew[2:3,:])*(1.0/(3072*nb)))
        tile=keep["tile"]
        sloc[0]=tile
        scs=[]
        for k,d in enumerate(bpeers):
            cp=remote(sloc.at[0],sin.at[k],eS.at[4,k],eR.at[4,k],d); start(cp); scs.append(cp)
        keep["scs"]=scs
    def t_R3():
        for cp in keep["scs"]: cp.wait_recv()
        tile=keep["tile"]
        for k in range(nb-1): tile=tile+sin[k]
        sloc[1]=tile
        scs=[]
        for k,d in enumerate(mpeers):
            cp=remote(sloc.at[1],smp.at[k],eS.at[5,k],eR.at[5,k],d); start(cp); scs.append(cp)
        keep["scs"]=scs; keep["tile"]=tile
    def t_R4():
        for cp in keep["scs"]: cp.wait_recv()
        tile=keep["tile"]
        for k in range(3): tile=tile+smp[k]
        lane=lanes[0:1]
        count=jnp.where(lane<4,768.0*768.0,jnp.where(lane<6,768.0*3072.0,768.0))
        live=lane<9
        mean=jnp.where(live,tile[0:1],1.0)
        urms=jnp.sqrt(mean*tile[1:2]/count)
        coef=jnp.sqrt(tile[2:3]/count)/jnp.maximum(1.0,urms/CLIP)*jnp.sqrt(mean)
        out=jnp.concatenate([urms,coef,jnp.zeros((6,128),F32)],axis=0)
        S_ref[...]=out
    table.update(VS=t_VS,VM=t_VM,ST=t_ST,R1=t_R1,R2=t_R2,R3=t_R3,R4=t_R4)
    for n in order: table[n[0]](*n[1:])
    for k in range(2):
        cp,lc=core_rows(k); cp.wait_recv(); lc.wait(); fwd_rows(k).wait_recv()
    for cond,cp in pend:
        if cond is None: cp.wait_send()
        else:
            @pl.when(cond)
            def _(): cp.wait_send()
def back_call(Gown,Gpart,W0,sel,P,probs,att,mid,accb,rows,gg,vec,w,olds,nb,picks):
    D=768; nz=nb//2; rp=w.shape[1]; T=rows.shape[0]; R=T//picks
    V=pltpu.VMEM; S=pltpu.SemaphoreType.DMA
    vm=pl.BlockSpec(memory_space=V); an=pl.BlockSpec(memory_space=pl.ANY)
    sd=jax.ShapeDtypeStruct
    order=list(BACK_ORDER)
    return pl.pallas_call(functools.partial(back_kernel,order,nz,rp,nb,picks),
        out_shape=(sd((3,rp,D),F32),sd((4,T,D),BF),sd((4,T,D),BF),sd((rp,128),F32),sd((8,D),F32),sd((8,128),F32),sd((16,128),F32),sd((8,128),F32),sd((8,128),F32)),
        in_specs=[an]*10+[vm]*(3+len(olds)),out_specs=(vm,an,an)+(vm,)*6,
        scratch_shapes=[V((3,2,D,D),BF),V((3,2,D,D),BF),V((2,2,nz,rp,D),BF),V((2,nz,rp,D),BF),V((2,nz,rp,D),BF),V((2,nz,rp,D),BF),
            V((4,nz,rp,D),BF),V((4,nz,rp,D),BF),V((2,rp,D),BF),V((rp,D),BF),V((2,D,D),BF),
            V((4,D,D),BF),V((T,2*D),BF),V((4,T,D),BF),V((R,4,3,picks,picks),BF),V((4,T,192),BF),V((T,D),F32),V((T,D),F32),V((T,D),F32),
            V((T,D),BF),V((D,T),BF),V((D,T),BF),V((T,192),BF),V((D,192),F32),V((T,D),BF),
            V((nb,8,128),F32),V((3,8,128),F32),V((nb,24,128),F32),V((3,8,128),F32),
            V((nb,8,128),F32),V((3,8,128),F32),V((rp,128),F32),V((24,128),F32),V((2,8,128),F32),V((nb,8,128),F32),V((8,D),F32),V((8,128),F32),V((rp,128),F32),V((8,D),F32),V((8,128),F32),
            S((17,)),S((3,2)),S((3,2)),S((2,2,nz)),S((2,2,nz)),S((2,nz)),S((2,nz)),S((4,2,nz)),S((4,2,nz)),S((2,2,nz)),S((2,2,nz)),
            S((2,2)),S((2,2)),S((2,6)),S((2,6)),S((6,nb)),S((6,nb))],
        compiler_params=pltpu.CompilerParams(collective_id=1,has_side_effects=True,vmem_limit_bytes=58<<20),
        name="back")(Gown,Gpart,W0,sel,P,probs,att,mid,accb,rows,gg,vec,w,*olds)


BF=jnp.bfloat16; F32=jnp.float32; D=768
OUT_SLOTS=3
def place_kernel(tok_ref, cot_ref, rows_ref, grads_ref, sel_ref, G_ref, w_ref, vold_ref, R_ref, C_ref, S_ref, V_ref, vdir_ref,
                 bo_ref, ig_ref, qg, qr, qc, qn, og, orr, oc, on, ug, ur, uc, un, dgr, dr, dc, dn, rg, rm, rn, gg, gmo, gn, ur_ms,
                 tokb, cotb, rowb, gradb, bob, igb, lsem, ssem):
    rows,length=tok_ref.shape[0:2]; picks=rows_ref.shape[1]
    def loads(r): return [pltpu.make_async_copy(src.at[r],dst.at[r],lsem.at[k,r]) for k,(src,dst) in enumerate(((tok_ref,tokb),(rows_ref,rowb),(cot_ref,cotb),(grads_ref,gradb)))]
    def stores(r,slot): return [pltpu.make_async_copy(src.at[slot],dst.at[r],ssem.at[k,slot]) for k,(src,dst) in enumerate(((bob,bo_ref),(igb,ig_ref)))]
    for r in range(rows):
        for cp in loads(r): cp.start()
    def new(i,s,j):
        g=G_ref[i,:,s]
        return g,w_ref[i,:,s].astype(F32)-S_ref[1:2,j:j+1]*(g*lax.rsqrt(R_ref[:,j:j+1]*C_ref[i:i+1,s]))
    for j in range(3):
        qg[j],qn[j]=new(0,slice(j*192,(j+1)*192),j)
        qc[j:j+1,:]=C_ref[0:1,j*192:(j+1)*192]
    g,n=new(0,slice(576,768),3); og[...]=g.T; on[...]=n.T
    g,n=new(1,slice(0,D),4); ug[...]=g; un[...]=n
    g,n=new(2,slice(0,D),5); dgr[...]=g; dn[...]=n
    Rt=R_ref[...].T
    qr[...]=Rt[0:3]; oc[...]=Rt[3:4]; ur[...]=Rt[4:5]; dc[...]=Rt[5:6]
    orr[...]=C_ref[0:1,576:768];
    for k in range(D//128):
        uc[k:k+1,:]=C_ref[1:2,k*128:(k+1)*128]; dr[k:k+1,:]=C_ref[2:3,k*128:(k+1)*128]
    ur_ms[...]=S_ref[0:1,0:9]
    rg[...]=V_ref[0:1,0:96]; gg[...]=V_ref[1:3,0:96]
    rm[...]=V_ref[8:9,0:96]; gmo[...]=V_ref[9:11,0:96]
    rn[...]=vold_ref[0:1,0:96]-S_ref[1:2,6:7]*vdir_ref[0:1,0:96]
    gn[0:1,:]=vold_ref[1:2,0:96]-S_ref[1:2,7:8]*vdir_ref[1:2,0:96]
    gn[1:2,:]=vold_ref[2:3,0:96]-S_ref[1:2,8:9]*vdir_ref[2:3,0:96]
    first=lax.axis_index("mp")*length
    @pl.loop(0,rows)
    def _(r):
        slot=lax.rem(r,OUT_SLOTS)
        pos=lax.broadcasted_iota(jnp.int32,(length,picks),0)
        hot=(pos==sel_ref[pl.ds(r,1),:]-first).astype(F32)
        cover=jnp.sum(hot,axis=1,keepdims=True)>0.5
        hot=hot.astype(BF)
        for cp in loads(r): cp.wait()
        @pl.when(r>=OUT_SLOTS)
        def _():
            for cp in stores(r-OUT_SLOTS,slot): cp.wait()
        bob[slot]=jnp.where(cover,jnp.dot(hot,rowb[r],preferred_element_type=F32),tokb[r].astype(F32)).astype(BF)
        igb[slot]=jnp.where(cover,jnp.dot(hot,gradb[r],preferred_element_type=F32),cotb[r].astype(F32))
        for cp in stores(r,slot): cp.start()
    for r in range(rows-OUT_SLOTS,rows):
        for cp in stores(r,r%OUT_SLOTS): cp.wait()
def place_call(tokens,cot,allrows,allgrads,selrel,G,w,vold,R,C,S,V,vdir):
    rows,length,_=tokens.shape; picks=selrel.shape[1]
    allrows=allrows.reshape(rows,picks,D); allgrads=allgrads.reshape(rows,picks,D)
    sd=lambda *s: jax.ShapeDtypeStruct(s,F32)
    rp=w.shape[1]
    small=[(3,rp,192),(3,rp),(3,192),(3,rp,192),(192,rp),(1,192),(1,rp),(192,rp),(rp,D),(1,rp),(D//128,128),(rp,D),(rp,D),(D//128,128),(1,rp),(rp,D),(1,rp),(1,rp),(1,rp),(2,rp),(2,rp),(2,rp),(1,9)]
    V_=pltpu.VMEM; vm=pl.BlockSpec(memory_space=V_); an=pl.BlockSpec(memory_space=pl.ANY)
    return pl.pallas_call(place_kernel,
        out_shape=(jax.ShapeDtypeStruct(tokens.shape,BF),jax.ShapeDtypeStruct(cot.shape,F32))+tuple(sd(*s) for s in small),
        in_specs=[an]*4+[vm]*9,out_specs=(an,an)+(vm,)*len(small),
        scratch_shapes=[V_((rows,length,D),BF),V_((rows,length,D),BF),V_((rows,picks,D),BF),V_((rows,picks,D),BF),V_((OUT_SLOTS,length,D),BF),V_((OUT_SLOTS,length,D),F32),
            pltpu.SemaphoreType.DMA((4,rows)),pltpu.SemaphoreType.DMA((2,OUT_SLOTS))],
        compiler_params=pltpu.CompilerParams(vmem_limit_bytes=60<<20),
        name="place")(tokens,cot,allrows,allgrads,selrel,G,w,vold,R,C,S,V,vdir)


def local_fast(tokens,segments,selection,cotangent,qkv_weight,out_weight,up_weight,down_weight,router_weight,norm_gains,
               qkv_rows,qkv_cols,out_rows,out_cols,up_rows,up_cols,down_rows,down_cols,router_moment,gains_moment):
    nb=lax.axis_size("batch"); picks=selection.shape[1]
    w,W0,Gown,Gpart,sel,projected,probs,attended,middle,grad_mid,rows_low,grad_gate,vall=fore_call(
        qkv_weight,out_weight,up_weight,down_weight.T,router_weight[None],norm_gains,tokens,cotangent,selection,segments,nb,picks)
    olds=(qkv_rows,qkv_cols,out_rows[None],out_cols[None],up_rows[None],up_cols.reshape(-1,128),down_rows.reshape(-1,128),down_cols[None],
          router_weight[None],norm_gains,router_moment[None],gains_moment)
    Gs,allrows,allgrads,R,C,S,V,vdir,vold=back_call(Gown,Gpart,W0,sel,projected,probs,attended,middle,grad_mid,rows_low,grad_gate,vall,w,olds,nb,picks)
    (bo,ig,qg,qr,qc,qn,og,orr,oc,on,ug,ur,uc,un,dgr,dr,dc,dn,rg,rm,rn,gg,gmo,gn,rms)=place_call(
        tokens,cotangent,allrows,allgrads,selection,Gs,w,vold,R,C,S,V,vdir)
    return (bo,ig,qg,qr,qc,qn,og,orr[0],oc[0],on,ug,ur[0],uc.reshape(-1),un,dgr.T,dr.reshape(-1),dc[0],dn.T,rg[0],rm[0],rn[0],gg,gmo,gn,rms[0])

def chosen_local(mesh):
    return local_fast if (mesh.shape["batch"],mesh.shape["mp"])==(8,4) else local_any


def solution(mesh):
    in_specs = (
        P("batch", "mp", None),
        P("batch", None),
        P("batch", None),
        P("batch", "mp", None),
        P(None, "batch", "mp"),
        P("mp", "batch"),
        P("batch", "mp"),
        P("mp", "batch"),
        P("batch"),
        P(None, "batch"),
        P(None, "batch"),
        P(None, "mp"),
        P("mp"),
        P("batch"),
        P("batch"),
        P("mp"),
        P("mp"),
        P("batch"),
        P("batch"),
        P(None, "batch"),
    )
    out_specs = (
        P("batch", "mp", None),
        P("batch", "mp", None),
        P(None, "batch", "mp"),
        P(None, "batch"),
        P(None, "mp"),
        P(None, "batch", "mp"),
        P("mp", "batch"),
        P("mp"),
        P("batch"),
        P("mp", "batch"),
        P("batch", "mp"),
        P("batch"),
        P("mp"),
        P("batch", "mp"),
        P("mp", "batch"),
        P("mp"),
        P("batch"),
        P("mp", "batch"),
        P("batch"),
        P("batch"),
        P("batch"),
        P(None, "batch"),
        P(None, "batch"),
        P(None, "batch"),
        P(),
    )
    return jax.shard_map(chosen_local(mesh), mesh=mesh, in_specs=in_specs, out_specs=out_specs, check_vma=False)
```

```python
import functools

import jax
import jax.numpy as jnp
from jax import lax
from jax.experimental import pallas as pl
from jax.experimental.pallas import tpu as pltpu
from jax.sharding import PartitionSpec as P


D = 768
HEAD_DIM = 64
FF = 3072
MICRO = 2


EPS_NORM = 1e-06
EPS_SQUARE = 1e-30
DECAY = 0.5
CLIP_RMS = 0.3
RATE = 1.0
MASKED = -1e30


def rms_parts(values):
    inverse = lax.rsqrt(jnp.mean(values * values, axis=1, keepdims=True) + EPS_NORM)
    return (values * inverse, inverse)


def norm_back(grad_norm, gain_vec, scaled, inverse):
    grad_scaled = grad_norm * gain_vec
    grad_input = inverse * (
        grad_scaled - scaled * jnp.mean(grad_scaled * scaled, axis=1, keepdims=True)
    )
    return (grad_input, jnp.sum(grad_norm * scaled, axis=0))


def spread_into(values, index, pieces):
    size_piece = values.shape[-1]
    shape_full = values.shape[:-1] + (size_piece * pieces,)
    return lax.dynamic_update_slice_in_dim(
        jnp.zeros(shape_full, jnp.float32), values, index * size_piece, values.ndim - 1
    )


def own_piece(values, index, size_piece):
    return lax.dynamic_slice_in_dim(values, index * size_piece, size_piece, values.ndim - 1)


def factor_terms(gradient, row_old, col_old, row_index, row_count, col_index, col_count):
    square = gradient * gradient + EPS_SQUARE
    rows_here, cols_here = gradient.shape[-2:]
    row_term = (1.0 - DECAY) * jnp.sum(square, axis=-1) / (
        cols_here * col_count
    ) + DECAY * row_old * (col_index == 0)
    col_term = (1.0 - DECAY) * jnp.sum(square, axis=-2) / (
        rows_here * row_count
    ) + DECAY * col_old * (row_index == 0)
    return (
        spread_into(row_term, row_index, row_count),
        spread_into(col_term, col_index, col_count),
    )


def factor_direction(gradient, row_full, col_full, row_index, col_index):
    rows_here, cols_here = gradient.shape[-2:]
    row_mine = own_piece(row_full, row_index, rows_here)
    col_mine = own_piece(col_full, col_index, cols_here)
    mean_row = jnp.mean(row_full, axis=-1)[..., None, None]
    second = row_mine[..., :, None] * col_mine[..., None, :] / mean_row
    return (gradient * lax.rsqrt(second), row_mine, col_mine)


def local_any(
    tokens,
    segments,
    selection,
    cotangent,
    qkv_weight,
    out_weight,
    up_weight,
    down_weight,
    router_weight,
    norm_gains,
    qkv_rows,
    qkv_cols,
    out_rows,
    out_cols,
    up_rows,
    up_cols,
    down_rows,
    down_cols,
    router_moment,
    gains_moment,
):
    qkv_all, out_all, up_all, down_all, router_all, gains_all = (
        lax.all_gather(qkv_weight, "batch", axis=1, tiled=True),
        lax.all_gather(out_weight, "batch", axis=1, tiled=True),
        lax.all_gather(up_weight, "batch", axis=0, tiled=True),
        lax.all_gather(down_weight, "batch", axis=1, tiled=True),
        lax.all_gather(router_weight, "batch", axis=0, tiled=True),
        lax.all_gather(norm_gains, "batch", axis=1, tiled=True),
    )
    mp_index = lax.axis_index("mp")
    mp_count = lax.axis_size("mp")
    batch_index = lax.axis_index("batch")
    batch_count = lax.axis_size("batch")
    rows_dev, length_here, width_full = tokens.shape
    width_local = width_full // mp_count
    heads_local = qkv_all.shape[2] // HEAD_DIM
    per_micro = rows_dev // MICRO
    score_scale = HEAD_DIM ** (-0.5)
    gain_attn = gains_all[0].astype(jnp.float32)
    gain_mlp = gains_all[1].astype(jnp.float32)
    router_float = router_all.astype(jnp.float32)
    first_position = mp_index * length_here
    totals = None
    shards = None
    output_list = []
    grad_list = []
    for micro_index in range(MICRO):
        row_start = micro_index * per_micro
        row_stop = row_start + per_micro
        token_rows = tokens[row_start:row_stop]
        chosen = selection[row_start:row_stop]
        cot_rows = cotangent[row_start:row_stop]
        row_count, pick_count = chosen.shape
        token_count = row_count * pick_count
        local_position = chosen - first_position
        inside = (local_position >= 0) & (local_position < length_here)
        clipped = jnp.clip(local_position, 0, length_here - 1)
        zero_low = jnp.zeros((), jnp.bfloat16)
        token_term = jnp.where(
            inside[:, :, None],
            jnp.take_along_axis(token_rows, clipped[:, :, None], axis=1),
            zero_low,
        ).reshape(token_count, width_full)
        cot_term = jnp.where(
            inside[:, :, None], jnp.take_along_axis(cot_rows, clipped[:, :, None], axis=1), zero_low
        ).reshape(token_count, width_full)
        picked_float = lax.psum(token_term, "mp").astype(jnp.float32)
        cot_float = lax.psum(cot_term, "mp").astype(jnp.float32)
        picked_full = picked_float.astype(jnp.bfloat16)
        picked_local = lax.dynamic_slice_in_dim(picked_full, mp_index * width_local, width_local, 1)
        cot_local = lax.dynamic_slice_in_dim(cot_float, mp_index * width_local, width_local, 1)
        picked_segments = jnp.take_along_axis(segments[row_start:row_stop], chosen, axis=1)
        allowed = (chosen[:, None, None, :] <= chosen[:, None, :, None]) & (
            picked_segments[:, None, None, :] == picked_segments[:, None, :, None]
        )
        router_gate = jax.nn.sigmoid(
            jnp.dot(picked_full, router_all, preferred_element_type=jnp.float32)
        )
        scaled_attn, inverse_attn = rms_parts(picked_float)
        normed = (scaled_attn * gain_attn).astype(jnp.bfloat16)
        projected = jnp.einsum(
            "td,cde->cte", normed, qkv_all, preferred_element_type=jnp.float32
        ).astype(jnp.bfloat16)
        shaped = projected.reshape(3, row_count, pick_count, heads_local, HEAD_DIM)
        queries = shaped[0]
        key_rows = shaped[1]
        value_rows = shaped[2]
        scores = (
            jnp.einsum("rqhe,rkhe->rhqk", queries, key_rows, preferred_element_type=jnp.float32)
            * score_scale
        )
        masked = jnp.where(allowed, scores, MASKED)
        highest_score = jnp.max(masked, axis=-1, keepdims=True)
        exponent = jnp.exp(masked - highest_score)
        exp_total = jnp.sum(exponent, axis=-1, keepdims=True)
        log_total = highest_score + jnp.log(exp_total)
        attention_low = (exponent / exp_total).astype(jnp.bfloat16)
        attended = jnp.einsum(
            "rhqk,rkhe->rqhe", attention_low, value_rows, preferred_element_type=jnp.float32
        )
        attended = attended.reshape(token_count, heads_local * HEAD_DIM).astype(jnp.bfloat16)
        attn_local = lax.psum_scatter(
            jnp.dot(attended, out_all, preferred_element_type=jnp.float32),
            "mp",
            scatter_dimension=1,
            tiled=True,
        )
        middle_local = picked_local.astype(jnp.float32) + attn_local
        middle = lax.all_gather(middle_local, "mp", axis=1, tiled=True)
        scaled_mlp, inverse_mlp = rms_parts(middle)
        normed_mid = (scaled_mlp * gain_mlp).astype(jnp.bfloat16)
        hidden = jnp.dot(normed_mid, up_all, preferred_element_type=jnp.float32)
        active = jax.nn.gelu(hidden).astype(jnp.bfloat16)
        mlp_local = lax.psum_scatter(
            jnp.dot(active, down_all, preferred_element_type=jnp.float32).astype(jnp.bfloat16),
            "mp",
            scatter_dimension=1,
            tiled=True,
        ).astype(jnp.float32)
        branch_local = attn_local + mlp_local
        output_local = (
            picked_local.astype(jnp.float32) + router_gate[:, None] * branch_local
        ).astype(jnp.bfloat16)
        output_full = lax.all_gather(output_local, "mp", axis=1, tiled=True)
        grad_gate = lax.psum(jnp.sum(cot_local * branch_local, axis=1), "mp")
        direct = router_gate[:, None] * cot_float
        grad_mlp = direct.astype(jnp.bfloat16)
        down_part = jnp.einsum("tf,td->fd", active, grad_mlp, preferred_element_type=jnp.float32)
        grad_active = jnp.einsum(
            "td,fd->tf", grad_mlp, down_all, preferred_element_type=jnp.float32
        )
        gelu_values, gelu_pull = jax.vjp(jax.nn.gelu, hidden)
        grad_hidden = gelu_pull(grad_active)[0].astype(jnp.bfloat16)
        up_part = jnp.einsum(
            "td,tf->df", normed_mid, grad_hidden, preferred_element_type=jnp.float32
        )
        grad_normed_mid = lax.psum(
            jnp.einsum("tf,df->td", grad_hidden, up_all, preferred_element_type=jnp.float32), "mp"
        )
        grad_middle, gain_mlp_part = norm_back(grad_normed_mid, gain_mlp, scaled_mlp, inverse_mlp)
        grad_attn = (grad_middle + direct).astype(jnp.bfloat16)
        out_part = jnp.einsum("te,td->ed", attended, grad_attn, preferred_element_type=jnp.float32)
        grad_attended = jnp.einsum(
            "td,ed->te", grad_attn, out_all, preferred_element_type=jnp.float32
        ).astype(jnp.bfloat16)
        grad_attended = grad_attended.reshape(row_count, pick_count, heads_local, HEAD_DIM)
        scores_again = (
            jnp.einsum("rqhe,rkhe->rhqk", queries, key_rows, preferred_element_type=jnp.float32)
            * score_scale
        )
        attention = jnp.exp(jnp.where(allowed, scores_again, MASKED) - log_total)
        grad_values = jnp.einsum(
            "rhqk,rqhe->rkhe",
            attention.astype(jnp.bfloat16),
            grad_attended,
            preferred_element_type=jnp.float32,
        )
        grad_weights = jnp.einsum(
            "rqhe,rkhe->rhqk", grad_attended, value_rows, preferred_element_type=jnp.float32
        )
        grad_scores = (
            attention * (grad_weights - jnp.sum(attention * grad_weights, axis=-1, keepdims=True))
        ).astype(jnp.bfloat16)
        grad_queries = (
            jnp.einsum("rhqk,rkhe->rqhe", grad_scores, key_rows, preferred_element_type=jnp.float32)
            * score_scale
        )
        grad_keys = (
            jnp.einsum("rhqk,rqhe->rkhe", grad_scores, queries, preferred_element_type=jnp.float32)
            * score_scale
        )
        grad_projected = (
            jnp.stack([grad_queries, grad_keys, grad_values])
            .reshape(3, token_count, heads_local * HEAD_DIM)
            .astype(jnp.bfloat16)
        )
        qkv_part = jnp.einsum(
            "td,cte->cde", normed, grad_projected, preferred_element_type=jnp.float32
        )
        grad_normed = lax.psum(
            jnp.einsum(
                "cte,cde->td", grad_projected, qkv_all, preferred_element_type=jnp.float32
            ).astype(jnp.bfloat16),
            "mp",
        ).astype(jnp.float32)
        grad_norm_in, gain_attn_part = norm_back(grad_normed, gain_attn, scaled_attn, inverse_attn)
        grad_logit = grad_gate * router_gate * (1.0 - router_gate)
        router_part = jnp.dot(grad_logit, picked_float, precision=lax.Precision.HIGHEST)
        grad_full = cot_float + grad_middle + grad_norm_in + grad_logit[:, None] * router_float
        row_positions = jnp.arange(row_count)[:, None]
        write_index = jnp.where(inside, local_position, length_here)
        output_rows = token_rows.at[row_positions, write_index].set(
            output_full.reshape(row_count, pick_count, width_full), mode="drop"
        )
        grad_rows = (
            cot_rows.astype(jnp.float32)
            .at[row_positions, write_index]
            .set(grad_full.reshape(row_count, pick_count, width_full), mode="drop")
        )
        gradients = (
            qkv_part,
            out_part,
            up_part,
            down_part,
            router_part,
            jnp.stack([gain_attn_part, gain_mlp_part]),
        )
        gradients, output_rows, grad_rows = (gradients, output_rows, grad_rows)
        output_list.append(output_rows)
        grad_list.append(grad_rows)
        totals = gradients if totals is None else jax.tree.map(jnp.add, totals, gradients)
    shards = (
        lax.psum_scatter(totals[0], "batch", scatter_dimension=1, tiled=True),
        lax.psum_scatter(totals[1], "batch", scatter_dimension=1, tiled=True),
        lax.psum_scatter(totals[2], "batch", scatter_dimension=0, tiled=True),
        lax.psum_scatter(totals[3], "batch", scatter_dimension=1, tiled=True),
        lax.psum_scatter(totals[4], "batch", scatter_dimension=0, tiled=True),
        lax.psum_scatter(totals[5], "batch", scatter_dimension=1, tiled=True),
    )
    block_output = jnp.concatenate(output_list, axis=0)
    input_grad = jnp.concatenate(grad_list, axis=0)
    qkv_grad, out_grad, up_grad, down_grad, router_grad, gains_grad = shards
    first_mp = (mp_index == 0).astype(jnp.float32)
    qkv_old = qkv_weight.astype(jnp.float32)
    out_old = out_weight.astype(jnp.float32)
    up_old = up_weight.astype(jnp.float32)
    down_old = down_weight.astype(jnp.float32)
    router_old = router_weight.astype(jnp.float32)
    gains_old = norm_gains.astype(jnp.float32)
    qkv_row_term, qkv_col_term = factor_terms(
        qkv_grad, qkv_rows, qkv_cols, batch_index, batch_count, mp_index, mp_count
    )
    out_row_term, out_col_term = factor_terms(
        out_grad, out_rows, out_cols, mp_index, mp_count, batch_index, batch_count
    )
    up_row_term, up_col_term = factor_terms(
        up_grad, up_rows, up_cols, batch_index, batch_count, mp_index, mp_count
    )
    down_row_term, down_col_term = factor_terms(
        down_grad, down_rows, down_cols, mp_index, mp_count, batch_index, batch_count
    )
    weight_squares = jnp.concatenate(
        [
            jnp.sum(qkv_old * qkv_old, axis=(1, 2)),
            jnp.stack(
                [
                    jnp.sum(out_old * out_old),
                    jnp.sum(up_old * up_old),
                    jnp.sum(down_old * down_old),
                    first_mp * jnp.sum(router_old * router_old),
                ]
            ),
            first_mp * jnp.sum(gains_old * gains_old, axis=1),
        ]
    )
    (
        qkv_row_full,
        qkv_col_full,
        out_row_full,
        out_col_full,
        up_row_full,
        up_col_full,
        down_row_full,
        down_col_full,
        weight_sums,
    ) = lax.psum(
        (
            qkv_row_term,
            qkv_col_term,
            out_row_term,
            out_col_term,
            up_row_term,
            up_col_term,
            down_row_term,
            down_col_term,
            weight_squares,
        ),
        ("batch", "mp"),
    )
    qkv_dir, qkv_rows_new, qkv_cols_new = factor_direction(
        qkv_grad, qkv_row_full, qkv_col_full, batch_index, mp_index
    )
    out_dir, out_rows_new, out_cols_new = factor_direction(
        out_grad, out_row_full, out_col_full, mp_index, batch_index
    )
    up_dir, up_rows_new, up_cols_new = factor_direction(
        up_grad, up_row_full, up_col_full, batch_index, mp_index
    )
    down_dir, down_rows_new, down_cols_new = factor_direction(
        down_grad, down_row_full, down_col_full, mp_index, batch_index
    )
    router_moment_new = DECAY * router_moment + (1.0 - DECAY) * (
        router_grad * router_grad + EPS_SQUARE
    )
    router_dir = router_grad * lax.rsqrt(router_moment_new)
    gains_moment_new = DECAY * gains_moment + (1.0 - DECAY) * (gains_grad * gains_grad + EPS_SQUARE)
    gains_dir = gains_grad * lax.rsqrt(gains_moment_new)
    update_squares = jnp.concatenate(
        [
            jnp.sum(qkv_dir * qkv_dir, axis=(1, 2)),
            jnp.stack(
                [
                    jnp.sum(out_dir * out_dir),
                    jnp.sum(up_dir * up_dir),
                    jnp.sum(down_dir * down_dir),
                    first_mp * jnp.sum(router_dir * router_dir),
                ]
            ),
            first_mp * jnp.sum(gains_dir * gains_dir, axis=1),
        ]
    )
    update_sums = lax.psum(update_squares, ("batch", "mp"))
    entries = jnp.array([D * D, D * D, D * D, D * D, D * FF, FF * D, D, D, D], jnp.float32)
    update_rms = jnp.sqrt(update_sums / entries)
    weight_rms = jnp.sqrt(weight_sums / entries)
    factors = RATE * weight_rms / jnp.maximum(1.0, update_rms / CLIP_RMS)
    qkv_new = qkv_old - factors[0:3, None, None] * qkv_dir
    out_new = out_old - factors[3] * out_dir
    up_new = up_old - factors[4] * up_dir
    down_new = down_old - factors[5] * down_dir
    router_new = router_old - factors[6] * router_dir
    gains_new = gains_old - factors[7:9, None] * gains_dir
    return (
        block_output,
        input_grad,
        qkv_grad,
        qkv_rows_new,
        qkv_cols_new,
        qkv_new,
        out_grad,
        out_rows_new,
        out_cols_new,
        out_new,
        up_grad,
        up_rows_new,
        up_cols_new,
        up_new,
        down_grad,
        down_rows_new,
        down_cols_new,
        down_new,
        router_grad,
        router_moment_new,
        router_new,
        gains_grad,
        gains_moment_new,
        gains_new,
        update_rms,
    )


BF=jnp.bfloat16; F32=jnp.float32
EPS_NORM=1e-6; MASKED=-1e30; HD=64
GC=0.7978845608028654; GA=0.044715
def nn(a,b): return jnp.dot(a,b,preferred_element_type=F32)
def nt(a,b): return lax.dot_general(a,b,(((1,),(1,)),((),())),preferred_element_type=F32)
def tn(a,b): return lax.dot_general(a,b,(((0,),(0,)),((),())),preferred_element_type=F32)
def vectors(vec_ref):
    nb=vec_ref.shape[0]
    vec=jnp.concatenate([vec_ref[b,:,0:768//nb] for b in range(nb)],axis=1)
    return vec[0:1,:],vec[1:2,:],vec[2:3,:]
def root(v): return lax.rsqrt(jnp.mean(v*v,axis=1,keepdims=True)+EPS_NORM)


MESH=pl.DeviceIdType.MESH
class Plane:
    def __init__(s):
        s.b=lax.axis_index("batch"); s.m=lax.axis_index("mp")
        s.z=s.b//2; s.y=lax.rem(s.b,2); s.x=s.m//2; s.c=lax.rem(s.m,2)
        s.left=(s.b-2,s.m); s.right=(s.b+2,s.m)
        s.ypeer=(s.z*2+1-s.y,s.m); s.xpeer=(s.b,(1-s.x)*2+s.c); s.core=(s.b,s.x*2+1-s.c)


FORE_ORDER=(('S',1,'X',),('S',0,'L',),('S',0,'R',),('S',1,'Y',),('PK',0,0,),('S',2,'R',),('FY',0,0,2,0,),('FX',0,2,0,),('S',2,'L',),('PK',1,0,),('FY',2,0,2,0,),('ZA',0,1,0,),('ZA',0,0,0,),('FX',0,0,0,),('CMB',0,),('TX',0,1,),('FY',0,0,1,0,),('ZA',2,1,0,),('PK',0,1,),('ZA',0,1,1,),('FY',0,0,0,0,),('FY',0,0,1,1,),('YA2',1,0,),('TX',0,0,),('PK',1,1,),('FY',0,1,2,0,),('YA',0,0,2,0,),('PK',3,1,),('ZA',0,0,1,),('S',1,'Z',),('PK',2,0,),('PK',2,1,),('ZA',0,1,2,),('ZA',2,0,0,),('ZA',2,1,1,),('FY',0,0,1,2,),('YA',0,0,1,0,),('FY',0,0,0,1,),('FX',0,0,1,),('ZA',0,0,2,),('FY',0,0,0,2,),('FY',0,1,0,0,),('FX',0,1,2,),('YA',2,0,2,0,),('XA2',1,),('FX',0,1,1,),('ZA2',1,0,1,0,0,),('CMB',1,),('YA',0,0,0,0,),('FX',0,1,0,),('PK',3,0,),('FX',0,0,2,),('TX',1,1,),('ZA2',1,0,1,1,0,),('ZA',2,0,1,),('ZA2',1,0,0,0,0,),('YA',0,0,1,2,),('YA',0,0,0,2,),('FX',2,0,1,),('TX',1,0,),('ZA2',1,0,0,1,0,),('YA',0,0,1,1,),('YA',0,0,0,1,),('SEL',0,),('NRM',),('QKV',1,),('QKV',0,),('FY',0,1,0,1,),('FY',0,1,1,2,),('FY',0,1,1,1,),('HD',0,),('YA',0,1,0,0,),('FY',0,1,0,2,),('ZA',2,1,2,),('FX',2,1,2,),('ZA',2,0,2,),('FY',0,1,1,0,),('HD',1,),('FY',2,0,0,0,),('ZA2',1,0,0,1,1,),('FX',2,2,0,),('FX',2,1,1,),('FX',2,0,2,),('ZA2',1,0,0,0,1,),('YA',0,1,2,0,),('ZA2',1,0,1,1,1,),('FY',2,0,1,1,),('ZA2',1,0,1,0,1,),('YA2',1,1,),('FY',2,0,0,1,),('FY',2,0,0,2,),('ZA2',1,1,0,0,0,),('FY',2,0,1,0,),('ZA2',1,1,0,1,0,),('YA',0,1,1,1,),('YA',0,1,1,2,),('YA',0,1,0,1,),('FY',2,0,1,2,),('YA',0,1,1,0,),('YA',0,1,0,2,),('QKV',2,),('HD',2,),('QKV',3,),('HD',3,),('ZA2',1,0,0,0,2,),('ZA2',1,0,1,1,2,),('ZA2',1,0,0,1,2,),('ZA2',1,0,1,0,2,),('OUT',),('ML',0,0,),('ML',1,0,),('FY',2,1,0,1,),('YA',2,0,1,1,),('FX',2,0,0,),('YA',2,0,0,0,),('ZA2',1,1,1,0,0,),('ZA2',1,1,1,1,0,),('ZA2',1,1,0,0,1,),('YA',2,0,0,2,),('YA',2,0,1,0,),('YA',2,0,1,2,),('YA',2,0,0,1,),('ZA2',1,1,1,0,1,),('ZA2',1,1,0,1,1,),('FX',2,1,0,),('YA',2,1,0,1,),('SEL',1,),('GM',),('ML',0,2,),('FY',2,1,1,2,),('ZA2',1,1,1,1,1,),('FY',2,1,2,0,),('ML',0,5,),('ML',0,4,),('ML',1,1,),('ML',1,2,),('ZA2',1,1,1,0,2,),('ZA2',1,1,0,0,2,),('ZA2',1,1,1,1,2,),('ML',0,1,),('ZA2',1,1,0,1,2,),('FY',2,1,1,1,),('FY',2,1,0,2,),('FY',2,1,0,0,),('ML',1,4,),('ML',1,3,),('ML',1,5,),('ML',0,3,),('ML',2,0,),('FY',2,1,1,0,),('YA',2,1,0,2,),('ML',3,0,),('YA',2,1,2,0,),('YA',2,1,0,0,),('ML',2,1,),('YA',2,1,1,2,),('ML',3,1,),('YA',2,1,1,1,),('YA',2,1,1,0,),('ML',2,2,),('ML',2,5,),('ML',3,2,),('ML',3,4,),('ML',3,5,),('ML',2,3,),('ML',2,4,),('END',),('ML',3,3,))


def fore_kernel(order, nz, rp, picks, qkvw_ref, outw_ref, upw_ref, dnw_ref, router_ref, gains_ref, tok_ref, cot_ref, pick_ref, segm_ref,
                w_ref, W0_out, Gown, Gpart, sel_out, P_out, probs_out, att_out, mid_out, accb_out, rows_out, gg_ref, vall_ref,
                W, tokb, cotb, zbuf, ra, rb, rx, normed, P, probs, att, mid, ba, nm, gm, acc, accb, nmT, gmT, gst, v_ref, selT, segl, segT,
                tsem, csem, rsem, ssem, shS, shR, txS, txR, vs, vr, gS, gR, gL, osem):
    D=768; nb=2*nz; T=nm.shape[0]; length=tok_ref.shape[1]; R=T//picks
    p=Plane()
    bpeers=[(lax.rem(p.b+k,nb),p.m) for k in range(1,nb)]
    peers=bpeers+[p.xpeer,p.core]
    bar=pltpu.get_barrier_semaphore()
    for d in peers: pl.semaphore_signal(bar,inc=1,device_id=d,device_id_type=MESH)
    xo=1-p.x; yo=1-p.y; co=1-p.c
    groups=[xo*2+co,xo*2+p.c,p.x*2+co,p.m]
    def row_load(h,g,k):
        r=groups[g]*R+k; s=g*R+k
        src,dst,sem=((tok_ref,tokb,tsem),(cot_ref,cotb,csem))[h]
        return pltpu.make_async_copy(src.at[r],dst.at[s%(2*R)],sem.at[s])
    for h in (0,1):
        for g in (0,1):
            for k in range(R): row_load(h,g,k).start()
    mine=pl.ds(pl.multiple_of(p.b*rp,rp),rp)
    for j in range(3): w_ref[0,:,j*192:(j+1)*192]=qkvw_ref[j]
    w_ref[0,:,576:768]=outw_ref[...].astype(F32).T.astype(BF)
    w_ref[1]=upw_ref[...]
    w_ref[2]=dnw_ref[...]
    for i in range(3): W[i,p.m,mine]=w_ref[i]
    n96=D//nb
    v_ref[...]=jnp.concatenate([jnp.concatenate([router_ref[...].astype(F32),gains_ref[...].astype(F32),jnp.zeros((5,n96),F32)],axis=0),jnp.zeros((8,128-n96),F32)],axis=1)
    vall_ref[p.b]=v_ref[...]
    pl.semaphore_wait(bar,len(peers))
    pend=[]
    def remote(src,dst,s,r,dev):
        return pltpu.make_async_remote_copy(src_ref=src,dst_ref=dst,send_sem=s,recv_sem=r,device_id=dev,device_id_type=MESH)
    def start(cp,cond=None):
        if cond is None: cp.start()
        else:
            @pl.when(cond)
            def _(): cp.start()
        pend.append((cond,cp))
    def when(cond,f):
        if cond is None: f()
        else:
            @pl.when(cond)
            def _(): f()
    vcs=[remote(v_ref,vall_ref.at[p.b],vs.at[k],vr.at[k],d) for k,d in enumerate(bpeers)]
    for cp in vcs: start(cp)
    count=[0]*3
    def at(i,m,b): return W.at[i,m,pl.ds(pl.multiple_of(b*rp,rp),rp)]
    def fwd(i,m,b,dev,cond=None):
        s=count[i]; count[i]+=1
        start(remote(at(i,m,b),at(i,m,b),ssem.at[i,s],rsem.at[i,m,b],dev),cond)
    def arrived(i,m,b): remote(at(i,m,b),at(i,m,b),ssem.at[i,0],rsem.at[i,m,b],p.core).wait_recv()
    def mm(xr): return p.m if xr==0 else xo*2+p.c
    def zc(dr,k):
        if dr==2: return p.z,None
        return (p.z-1-k,p.z>k) if dr==0 else (p.z+1+k,p.z<nz-1-k)
    def both(a,b): return b if a is None else (a if b is None else a&b)
    def t_S(i,d):
        if d=="R": fwd(i,p.m,p.b,p.right,p.z<nz-1)
        elif d=="L": fwd(i,p.m,p.b,p.left,p.z>0)
        elif d=="X": fwd(i,p.m,p.b,p.xpeer)
        elif d=="Y": fwd(i,p.m,p.b,p.ypeer)
        else:
            fwd(i,p.m,p.b,p.right,p.z<nz-1); fwd(i,p.m,p.b,p.left,p.z>0)
    for i in range(3): fwd(i,p.m,p.b,p.core)
    def along(i,m,b,dr,cond):
        if dr==0: fwd(i,m,b,p.right,both(cond,p.z<nz-1))
        else: fwd(i,m,b,p.left,both(cond,p.z>0))
    def t_ZA(i,dr,k):
        z,c=zc(dr,k); b=z*2+p.y
        when(c,lambda: arrived(i,p.m,b))
        along(i,p.m,b,dr,c); fwd(i,p.m,b,p.core,c)
    def t_FX(i,dr,k):
        z,c=zc(dr,k); fwd(i,p.m,z*2+p.y,p.xpeer,c)
    def t_FY(i,xr,dr,k):
        z,c=zc(dr,k); b=z*2+p.y; m=mm(xr)
        if xr==1:
            when(c,lambda: arrived(i,m,b)); fwd(i,m,b,p.core,c)
        fwd(i,m,b,p.ypeer,c)
    def t_YA(i,xr,dr,k):
        z,c=zc(dr,k); b=z*2+yo; m=mm(xr)
        when(c,lambda: arrived(i,m,b)); fwd(i,m,b,p.core,c)
    def t_XA2(i):
        m=mm(1); arrived(i,m,p.b)
        fwd(i,m,p.b,p.ypeer); fwd(i,m,p.b,p.right,p.z<nz-1); fwd(i,m,p.b,p.left,p.z>0); fwd(i,m,p.b,p.core)
    def t_YA2(i,xr):
        m=mm(xr); b=p.z*2+yo; arrived(i,m,b)
        fwd(i,m,b,p.right,p.z<nz-1); fwd(i,m,b,p.left,p.z>0); fwd(i,m,b,p.core)
    def t_ZA2(i,xr,yr,dr,k):
        z,c=zc(dr,k); m=mm(xr); b=z*2+(p.y if yr==0 else yo)
        when(c,lambda: arrived(i,m,b))
        along(i,m,b,dr,c); fwd(i,m,b,p.core,c)
    ones=lax.broadcasted_iota(jnp.int32,(picks,8),1)
    def column(ref,r):
        return jnp.sum(jnp.where(ones==r,ref[...],0.0),axis=1,keepdims=True)
    def t_SG():
        sel=pick_ref[...]
        selT[...]=sel.astype(F32).T
        seg=segm_ref[...]
        own=jnp.zeros(sel.shape,F32)
        for q in range(1,8):
            begin=jnp.sum((seg<q).astype(F32),axis=1,keepdims=True)
            own=own+(sel.astype(F32)>=begin).astype(F32)
        segl[...]=own
        segT[...]=own.T
    begun=[]
    def t_PK(g,h):
        if not begun: begun.append(t_SG())
        for k in range(R):
            row_load(h,g,k).wait()
            col=column(selT,groups[g]*R+k).astype(jnp.int32)-p.m*length
            one=(col==lax.broadcasted_iota(jnp.int32,(picks,length),1)).astype(F32).astype(BF)
            buf=(tokb,cotb)[h]
            zbuf[g,k*picks:(k+1)*picks,h*D:(h+1)*D]=nn(one,buf[(g*R+k)%(2*R)]).astype(BF)
        if g<2:
            for k in range(R): row_load(h,g+2,k).start()
        if g==0: start(ship(0,h))
        if g==2: start(ship(1,h))
    cols=[slice(0,D),slice(D,2*D)]
    def ship(a,h):
        src=zbuf.at[2*a]; dst=(rb,ra)[a]
        return remote(src.at[:,cols[h]],dst.at[:,cols[h]],shS.at[a,h],shR.at[a,h],p.core)
    ch=T//2
    def tx(h,q):
        rs=pl.ds(q*ch,ch)
        return remote(zbuf.at[1,rs,cols[h]],rx.at[rs,cols[h]],txS.at[h,q],txR.at[h,q],p.xpeer)
    def t_CMB(h):
        ship(0,h).wait_recv()
        zbuf[1,:,cols[h]]=zbuf[1,:,cols[h]]+rb[:,cols[h]]
    def t_TX(h,q): start(tx(h,q))
    def t_SEL(h):
        ship(1,h).wait_recv()
        for q in (0,1): tx(h,q).wait_recv()
        zbuf[3,:,cols[h]]=zbuf[3,:,cols[h]]+ra[:,cols[h]]+rx[:,cols[h]]
    sel=zbuf.at[3]
    keep={}
    outs=[]
    def write(src,dst):
        cp=pltpu.make_async_copy(src,dst,osem.at[3+len(outs)]); cp.start(); outs.append(cp)
    def t_NRM():
        for cp in vcs: cp.wait_recv()
        router,gain0,gain1=vectors(vall_ref)
        keep["gain1"]=gain1
        x=sel[:,0:D].astype(F32)
        keep["gate"]=jax.nn.sigmoid(jnp.sum(x*router,axis=1,keepdims=True))
        normed[...]=(x*root(x)*gain0).astype(BF)
    def t_GM():
        gmv=(keep["gate"]*sel[:,D:].astype(F32)).astype(BF)
        gm[...]=gmv
        gmT[...]=gmv.T
        write(sel,sel_out)
    mis=[p.m,p.x*2+co,xo*2+p.c,xo*2+co]
    mlp=[p.x*2+co,p.m,xo*2+co,xo*2+p.c]
    def ready(i,m):
        for b in range(nb): arrived(i,m,b)
    scale=HD**-0.5
    def t_QKV(mi):
        m=mis[mi]
        if mi%2==1: ready(0,m)
        P[m]=nn(normed[...],W[0,m]).astype(BF)
    def t_HD(mi):
        m=mis[mi]
        @pl.loop(0,R)
        def _(r):
            qi=lax.broadcasted_iota(jnp.int32,(picks,picks),0); ki=lax.broadcasted_iota(jnp.int32,(picks,picks),1)
            ok=(ki<=qi)&(segl[pl.ds(p.m*R+r,1),:]==column(segT,p.m*R+r))
            rs=pl.ds(pl.multiple_of(r*picks,picks),picks)
            res=[]
            for j in range(3):
                o=j*HD
                q=P[m,rs,o:o+HD]; k=P[m,rs,192+o:192+o+HD]; v=P[m,rs,384+o:384+o+HD]
                s=jnp.where(ok,nt(q,k)*scale,MASKED)
                e=jnp.exp(s-jnp.max(s,axis=1,keepdims=True))
                pr=(e/jnp.sum(e,axis=1,keepdims=True)).astype(BF)
                probs[r,m,j]=pr
                res.append(nn(pr,v))
            att[m,rs,:]=jnp.concatenate(res,axis=1).astype(BF)
    def t_OUT():
        write(W.at[0],W0_out); write(P,P_out); write(probs,probs_out); write(att,att_out)
        a=nt(att[0],W[0,0,:,576:768])
        for m in range(1,4): a=a+nt(att[m],W[0,m,:,576:768])
        ba[...]=a
        mv=sel[:,0:D].astype(F32)+a
        mid[...]=mv
        write(mid,mid_out)
        nmv=(mv*root(mv)*keep["gain1"]).astype(BF)
        nm[...]=nmv
        nmT[...]=nmv.T
        acc[...]=jnp.zeros_like(acc)
        accb[...]=jnp.zeros_like(accb)
    def g_copy(i,mi):
        x=(p.x,p.x,xo,xo)[mi]; k=mi%2
        if k==1: return pltpu.make_async_copy(gst.at[k,i],Gown.at[i,x],gL.at[i,x])
        return remote(gst.at[k,i],Gpart.at[i,x],gS.at[i,x],gR.at[i,x],p.core)
    def g_done(i,mi):
        if mi%2==1: g_copy(i,mi).wait()
        else: g_copy(i,mi).wait_send()
    def g_out(i,mi,val):
        if mi>1: g_done(i,mi-2)
        gst[mi%2,i]=val.astype(BF)
        g_copy(i,mi).start()
    act,gh=tokb,cotb
    def t_ML(mi,part):
        m=mlp[mi]
        if part==0:
            if mi%2==0: ready(1,m)
            for t in range(3):
                cs=slice(t*256,(t+1)*256)
                h=nn(nm[...],W[1,m,:,cs])
                th=jnp.tanh(GC*(h+GA*h*h*h))
                act[mi,:,cs]=(0.5*h*(1.0+th)).astype(BF)
                gh[mi,:,cs]=(0.5*(1.0+th)+0.5*h*(1.0-th*th)*(GC*(1.0+3.0*GA*h*h))).astype(BF)
        elif part==1: g_out(1,mi,nn(gmT[...],act[mi]))
        elif part==2:
            if mi%2==0: ready(2,m)
            for t in range(3):
                cs=slice(t*256,(t+1)*256)
                gh[mi,:,cs]=(nn(gm[...],W[2,m,:,cs])*gh[mi,:,cs].astype(F32)).astype(BF)
        elif part==3: g_out(0,mi,nn(nmT[...],gh[mi]))
        elif part==4: acc[...]+=nt(act[mi],W[2,m])
        else: accb[...]+=nt(gh[mi],W[1,m])
    def t_END():
        write(accb,accb_out)
        br=ba[...]+acc[...]
        normed[...]=(sel[:,0:D].astype(F32)+keep["gate"]*br).astype(BF)
        write(normed,rows_out)
        gg_ref[...]=jnp.sum(sel[:,D:].astype(F32)*br,axis=1,keepdims=True)
    table=dict(S=t_S,ZA=t_ZA,FX=t_FX,FY=t_FY,YA=t_YA,XA2=t_XA2,YA2=t_YA2,ZA2=t_ZA2,PK=t_PK,CMB=t_CMB,TX=t_TX,SEL=t_SEL,NRM=t_NRM,GM=t_GM,QKV=t_QKV,HD=t_HD,OUT=t_OUT,ML=t_ML,END=t_END)
    for n in order: table[n[0]](*n[1:])
    for i in (0,1):
        for mi in (2,3): g_done(i,mi)
        for mi in (0,2): g_copy(i,mi).wait_recv()
    for cp in outs: cp.wait()
    for cond,cp in pend: when(cond,cp.wait_send)
def fore_call(qkv_weight,out_weight,up_weight,down_turned,router,gains,tokens,cot,selection,segments,nb,picks):
    nz=nb//2; rp=up_weight.shape[0]; rows,length,D=tokens.shape; R=rows//4; T=R*picks
    V=pltpu.VMEM; S=pltpu.SemaphoreType.DMA
    vm=pl.BlockSpec(memory_space=V); an=pl.BlockSpec(memory_space=pl.ANY)
    sd=jax.ShapeDtypeStruct
    return pl.pallas_call(functools.partial(fore_kernel,FORE_ORDER,nz,rp,picks),
        out_shape=(sd((3,rp,D),BF),sd((4,D,D),BF),sd((2,2,D,D),BF),sd((2,2,D,D),BF),sd((T,2*D),BF),sd((4,T,D),BF),sd((R,4,3,picks,picks),BF),sd((4,T,192),BF),
            sd((T,D),F32),sd((T,D),F32),sd((T,D),BF),sd((T,1),F32),sd((nb,8,128),F32)),
        in_specs=[vm]*6+[an,an,vm,vm],out_specs=(vm,)+(an,)*10+(vm,vm),
        scratch_shapes=[V((3,4,D,D),BF),V((2*R,length,D),BF),V((2*R,length,D),BF),V((4,T,2*D),BF),V((T,2*D),BF),V((T,2*D),BF),V((T,2*D),BF),
            V((T,D),BF),V((4,T,D),BF),V((R,4,3,picks,picks),BF),V((4,T,192),BF),V((T,D),F32),V((T,D),F32),V((T,D),BF),V((T,D),BF),
            V((T,D),F32),V((T,D),F32),V((D,T),BF),V((D,T),BF),V((2,2,D,D),BF),V((8,128),F32),V((picks,rows),F32),V((rows,picks),F32),V((picks,rows),F32),
            S((rows,)),S((rows,)),S((3,4,nb)),S((3,80)),S((2,2)),S((2,2)),S((2,2)),S((2,2)),S((nb,)),S((nb,)),S((2,2)),S((2,2)),S((2,2)),S((12,))],
        compiler_params=pltpu.CompilerParams(collective_id=0,has_side_effects=True,vmem_limit_bytes=60<<20),
        name="fore")(qkv_weight,out_weight,up_weight,down_turned,router,gains,tokens,cot,selection,segments)


BACK_ORDER=(('RO',2,),('AD',1,0,),('AD',1,1,),('YS',1,1,0,),('YS',1,1,1,),('RO',0,),('RO',3,),('YS',1,1,2,),('AD',2,1,),('YS',1,1,3,),('RO',1,),('YS',1,0,1,),('WQ',),('YS',1,0,2,),('ZL',6,),('ZR',11,),('C',0,),('AD',2,0,),('ZL',4,),('ZL',7,),('ZR',2,),('ZL',8,),('C',1,),('YR',1,1,0,),('C',2,),('C',3,),('ZL',10,),('ZL',11,),('ZR',0,),('C',4,),('C',5,),('C',6,),('C',7,),('ZR',3,),('C',8,),('C',9,),('C',10,),('YS',0,1,1,),('YR',1,1,3,),('ZR',1,),('YR',1,1,2,),('ZR',6,),('YS',0,1,0,),('YS',0,1,3,),('ZR',4,),('ZR',5,),('ZR',9,),('ZL',3,),('YS',0,1,2,),('YR',1,1,1,),('C',11,),('C',12,),('YS',1,0,0,),('YS',1,0,3,),('C',13,),('YR',0,1,1,),('ZL',0,),('C',14,),('C',15,),('ZR',7,),('YR',0,1,0,),('C',16,),('ZR',10,),('ZL',1,),('C',17,),('C',18,),('YR',0,1,3,),('C',19,),('ZL',2,),('C',20,),('YS',0,0,0,),('YS',0,0,3,),('C',21,),('ZL',5,),('ZL',9,),('YR',0,1,2,),('C',22,),('C',23,),('C',24,),('C',25,),('RG',0,),('YS',0,0,1,),('ZR',8,),('YR',1,0,1,),('YR',1,0,2,),('YR',1,0,0,),('XR',1,2,),('LR',1,2,),('XR',1,1,),('XR',1,0,),('RG',1,),('RG',2,),('LR',1,1,),('F2',1,1,),('LL',1,0,),('F2',0,0,),('YS',0,0,2,),('YR',1,0,3,),('XR',1,3,),('F2',1,0,),('F2',0,1,),('YR',0,0,0,),('XR',0,0,),('LL',0,0,),('LL',1,1,),('LR',1,3,),('YR',0,0,1,),('LL',1,2,),('YR',0,0,3,),('XR',0,3,),('XR',0,1,),('FY',1,),('LL',0,1,),('LR',0,3,),('RG',3,),('YR',0,0,2,),('XR',0,2,),('LL',0,2,),('FIN',1,),('ST',1,),('LR',0,2,),('LR',0,1,),('FY',0,),('FX',),('ST',2,),('FIN',0,),('ST',0,),('VS',),('R1',),('VM',),('RF',),('R2',),('R3',),('R4',))


EPS_SQUARE=1e-30; CLIP=0.3
ROW_CHUNKS=4
def back_kernel(order, nz, rp, nb, picks, Gown, Gpart, W_hbm, sel_hbm, P_hbm, probs_hbm, att_hbm, mid_hbm, accb_hbm, rows_hbm, gg_ref, vec_ref,
                w_ref, qr_ref, qc_ref, or_ref, oc_ref, ur_ref, uc_ref, dr_ref, dc_ref, router_ref, gains_ref, rmom_ref, gmom_ref,
                Gs_ref, out_ref, grad_ref, R_ref, C_ref, S_ref, V_ref, vdir_ref, vold_ref,
                Pl, RC, RY, RX, RLy, RRy, RLz, RRz, Fy, Fx, gst,
                W0, sel, P, probs, att, mid, accb, acc, ga, gaT, nT, gatt, gob, rows,
                vin, vmp, cin, rin, sin, smp, rloc, cloc, sloc, vsend, small, vmom_ref, rold_ref, cold_ref, rturn,
                loc, cS, cR, yS, yR, xS, xR, zS, zR, lS, lR, fS, fR, rS, rR, eS, eR):
    D=768; T=sel.shape[0]
    p=Plane()
    bpeers=[(lax.rem(p.b+k,nb),p.m) for k in range(1,nb)]
    mpeers=[(p.b,lax.rem(p.m+k,4)) for k in range(1,4)]
    bar=pltpu.get_barrier_semaphore()
    for d in bpeers+mpeers: pl.semaphore_signal(bar,inc=1,device_id=d,device_id_type=MESH)
    xo=1-p.x; yo=1-p.y; co=1-p.c
    loads={}
    def load(n,src,dst,k):
        loads[n]=pltpu.make_async_copy(src,dst,loc.at[k]); loads[n].start()
    own_blocks=[(i,x) for x in (0,1) for i in (2,1)]
    for k,(i,x) in enumerate(own_blocks):
        load((i,x),Gown.at[i-1,x],Pl.at[i,x],k)
        load((i,x,1),Gpart.at[i-1,x],RC.at[i,x],13+k)
    for k,(n,src,dst) in enumerate([(0,accb_hbm,accb),(1,mid_hbm,mid),(2,sel_hbm,sel),(3,W_hbm,W0),(4,att_hbm,att),(5,P_hbm,P),(6,probs_hbm,probs)]):
        load(n,src,dst,4+k)
    n96=D//nb
    def tile(rows):
        v=jnp.concatenate([r[...].astype(F32) for r in rows],axis=0)
        v=jnp.concatenate([v,jnp.zeros((8-v.shape[0],n96),F32)],axis=0)
        return jnp.concatenate([v,jnp.zeros((8,128-n96),F32)],axis=1)
    def line(ref): return jnp.concatenate([ref[k:k+1,:] for k in range(ref.shape[0])],axis=1)
    vold_ref[...]=tile([router_ref,gains_ref])
    vmom_ref[...]=tile([rmom_ref,gmom_ref])
    rold_ref[...]=jnp.concatenate([tile([qr_ref,oc_ref,ur_ref,dc_ref]).T[0:rp],jnp.zeros((rp,120),F32)],axis=1)
    cold_ref[...]=jnp.concatenate([jnp.concatenate([qc_ref[0:1],qc_ref[1:2],qc_ref[2:3],or_ref[...]],axis=1),line(uc_ref),line(dr_ref),jnp.zeros((5,D),F32)],axis=0)
    pl.semaphore_wait(bar,nb-1+3)
    pend=[]
    def remote(src,dst,s,r,dev):
        return pltpu.make_async_remote_copy(src_ref=src,dst_ref=dst,send_sem=s,recv_sem=r,device_id=dev,device_id_type=MESH)
    def start(cp): cp.start(); pend.append((None,cp))
    def part(ref,b): return ref.at[pl.ds(pl.multiple_of(b*rp,rp),rp)]
    def shard(i,x,b): return Pl.at[i,x,pl.ds(pl.multiple_of(b*rp,rp),rp)]
    def add(dst,*src):
        @pl.loop(0,rp,step=32)
        def _(k):
            ks=pl.ds(pl.multiple_of(k,32),32)
            v=dst[ks].astype(F32)
            for q in src: v=v+q[ks].astype(F32)
            dst[ks]=v.astype(BF)
    def core_copy(i,x,src): return remote(src,RC.at[i,x],cS.at[i,x],cR.at[i,x],p.core)
    def t_AD(i,x):
        loads[(i,x)].wait(); loads[(i,x,1)].wait()
        dst=Pl.at[i,x]; src=RC.at[i,x]
        @pl.loop(0,D,step=64)
        def _(k):
            ks=pl.ds(pl.multiple_of(k,64),64)
            dst[ks]=(dst[ks].astype(F32)+src[ks].astype(F32)).astype(BF)
    ax=lambda xr: p.x if xr==0 else xo
    ay=lambda yr: p.y if yr==0 else yo
    def ys_copy(g,xr,z): return remote(shard(g,ax(xr),z*2+yo),RY.at[g,ax(xr),z],yS.at[g,xr,z],yR.at[g,ax(xr),z],p.ypeer)
    def xs_copy(g,z): return remote(shard(g,xo,z*2+p.y),RX.at[g,z],xS.at[g,z],xR.at[g,z],p.xpeer)
    def t_YS(g,xr,z): start(ys_copy(g,xr,z))
    def t_YR(g,xr,z):
        ys_copy(g,xr,z).wait_recv()
        add(shard(g,ax(xr),z*2+p.y),RY.at[g,ax(xr),z])
        if xr==1: start(xs_copy(g,z))
    def t_XR(g,z):
        xs_copy(g,z).wait_recv(); add(shard(g,p.x,z*2+p.y),RX.at[g,z])
    def guarded(cond,cp,more,recv,dst):
        @pl.when(cond)
        def _():
            @pl.when(more)
            def _(): cp.wait_recv(); add(dst,recv)
            cp.start()
        pend.append((cond,cp))
    def t_LR(g,t):
        cp=remote(shard(g,p.x,t*2+p.y),RLy.at[g,t],lS.at[g,0,t],lR.at[g,0,t],p.right)
        guarded(p.z<t,cp,p.z>0,RLy.at[g,t],shard(g,p.x,t*2+p.y))
    def t_LL(g,t):
        cp=remote(shard(g,p.x,t*2+p.y),RRy.at[g,t],lS.at[g,1,t],lR.at[g,1,t],p.left)
        guarded(p.z>t,cp,p.z<nz-1,RRy.at[g,t],shard(g,p.x,t*2+p.y))
    def t_ZR(k):
        t=nz-1-k//4; c=k%4; sh=shard(2,c//2,t*2+c%2)
        cp=remote(sh,RLz.at[c,t],zS.at[c,0,t],zR.at[c,0,t],p.right)
        guarded(p.z<t,cp,p.z>0,RLz.at[c,t],sh)
    def t_ZL(k):
        t=k//4; c=k%4; sh=shard(2,c//2,t*2+c%2)
        cp=remote(sh,RRz.at[c,t],zS.at[c,1,t],zR.at[c,1,t],p.left)
        guarded(p.z>t,cp,p.z<nz-1,RRz.at[c,t],sh)
    def last(RL,RR,rl,rr,dst):
        @pl.when(p.z>0)
        def _(): rl.wait_recv(); add(dst,RL)
        @pl.when(p.z<nz-1)
        def _(): rr.wait_recv(); add(dst,RR)
    def fy_copy(xr): return remote(shard(2,ax(xr),p.z*2+yo),Fy.at[ax(xr)],fS.at[0,xr],fR.at[0,ax(xr)],p.ypeer)
    def fx_copy(): return remote(shard(2,xo,p.b),Fx,fS.at[1,0],fR.at[1,0],p.xpeer)
    def t_F2(xr,yr):
        c=ax(xr)*2+ay(yr); sh=shard(2,ax(xr),p.z*2+ay(yr))
        rl=remote(sh,RLz.at[c,p.z],zS.at[0,0,0],zR.at[c,0,p.z],p.right)
        rr=remote(sh,RRz.at[c,p.z],zS.at[0,1,0],zR.at[c,1,p.z],p.left)
        last(RLz.at[c,p.z],RRz.at[c,p.z],rl,rr,sh)
        if yr==1: start(fy_copy(xr))
    def t_FY(xr):
        fy_copy(xr).wait_recv(); add(shard(2,ax(xr),p.b),Fy.at[ax(xr)])
        if xr==1: start(fx_copy())
    def t_FX():
        fx_copy().wait_recv()
        Gs_ref[2]=shard(2,p.x,p.b)[...].astype(F32)+Fx[...].astype(F32)
    def t_FIN(g):
        sh=shard(g,p.x,p.b)
        Gs_ref[g]=sh[...].astype(F32)
        @pl.when(p.z>0)
        def _():
            remote(sh,RLy.at[g,p.z],lS.at[g,0,0],lR.at[g,0,p.z],p.right).wait_recv()
            Gs_ref[g]+=RLy[g,p.z].astype(F32)
        @pl.when(p.z<nz-1)
        def _():
            remote(sh,RRy.at[g,p.z],lS.at[g,1,0],lR.at[g,1,p.z],p.left).wait_recv()
            Gs_ref[g]+=RRy[g,p.z].astype(F32)
    ch=T//ROW_CHUNKS
    def row_copy(k,q):
        src,dst=((rows_hbm,out_ref),(rows,grad_ref))[k]
        return remote(src.at[pl.ds(q*ch,ch)],dst.at[p.m,pl.ds(q*ch,ch)],rS.at[k,q],rR.at[k,q],p.xpeer)
    xm=xo*2+p.c
    def core_rows(k):
        src,dst=((rows_hbm,out_ref),(rows,grad_ref))[k]
        return remote(src,dst.at[p.m],rS.at[k,4],rR.at[k,4],p.core),pltpu.make_async_copy(src,dst.at[p.m],loc.at[11+k])
    def fwd_rows(k):
        dst=(out_ref,grad_ref)[k]
        return remote(dst.at[xm],dst.at[xm],rS.at[k,5],rR.at[k,5],p.core)
    def t_RO(q):
        start(row_copy(0,q))
        if q==0:
            cp,lc=core_rows(0); start(cp); lc.start()
    def t_RG(q):
        start(row_copy(1,q))
        if q==0:
            cp,lc=core_rows(1); start(cp); lc.start()
    def t_RF():
        for k in range(2):
            for q in range(ROW_CHUNKS): row_copy(k,q).wait_recv()
            start(fwd_rows(k))
    router,gain0,gain1=vectors(vec_ref)
    scale=HD**-0.5
    ms=[xo*2+co,xo*2+p.c,p.x*2+co,p.x*2+p.c]
    keep={}
    def gate_of(): return jax.nn.sigmoid(jnp.sum(sel[:,0:D].astype(F32)*router,axis=1,keepdims=True))
    def back(e,gain,scaled,iv):
        eg=e*gain
        return iv*(eg-scaled*jnp.mean(eg*scaled,axis=1,keepdims=True)),jnp.sum(e*scaled,axis=0,keepdims=True)
    def c_first():
        for n in (0,1,2): loads[n].wait()
        iv=root(mid[...])
        gmid,g1=back(accb[...],gain1,mid[...]*iv,iv)
        small[2:3,:]=g1
        mid[...]=gmid
        gv=(gmid+gate_of()*sel[:,D:].astype(F32)).astype(BF)
        ga[...]=gv
        gaT[...]=gv.T
        xv=sel[:,0:D].astype(F32)
        nT[...]=(xv*root(xv)*gain0).astype(BF).T
        acc[...]=jnp.zeros_like(acc)
        for n in (3,4,5,6): loads[n].wait()
    def c_out(mi):
        m=ms[mi]
        gatt[...]=nn(ga[...],W0[m,:,576:768]).astype(BF)
        gob[...]=nn(gaT[...],att[m])
    def c_head(mi,j):
        m=ms[mi]; o=j*HD
        @pl.loop(0,T//picks)
        def _(r):
            rs=pl.ds(pl.multiple_of(r*picks,picks),picks)
            q=P[m,rs,o:o+HD]; k=P[m,rs,192+o:192+o+HD]; v=P[m,rs,384+o:384+o+HD]
            g=gatt[rs,o:o+HD]
            pr=probs[r,m,j]
            gp=nt(g,v)
            pf=pr.astype(F32)
            ds=(pf*(gp-jnp.sum(pf*gp,axis=1,keepdims=True))).astype(BF)
            P[m,rs,o:o+HD]=(nn(ds,k)*scale).astype(BF)
            P[m,rs,192+o:192+o+HD]=(tn(ds,q)*scale).astype(BF)
            P[m,rs,384+o:384+o+HD]=tn(pr,g).astype(BF)
    def c_block(mi):
        m=ms[mi]; x=(xo,xo,p.x,p.x)[mi]
        g=nn(nT[...],P[m,:,0:576])
        if mi%2==0:
            s=mi//2
            gst[s,:,0:576]=g.astype(BF); gst[s,:,576:768]=gob[...].astype(BF)
            start(core_copy(0,x,gst.at[s]))
        else:
            core_copy(0,x,gst.at[0]).wait_recv()
            Pl[0,x,:,0:576]=(g+RC[0,x,:,0:576].astype(F32)).astype(BF)
            Pl[0,x,:,576:768]=(gob[...]+RC[0,x,:,576:768].astype(F32)).astype(BF)
    def c_norm(mi):
        m=ms[mi]
        acc[...]+=nt(P[m,:,0:576],W0[m,:,0:576])
    vcs=[]
    def c_last():
        xv=sel[:,0:D].astype(F32); gate=gate_of()
        glog=gg_ref[...]*gate*(1.0-gate)
        iv=root(xv)
        gin,g0=back(acc[...],gain0,xv*iv,iv)
        small[0:1,:]=jnp.sum(glog*xv,axis=0,keepdims=True)
        small[1:2,:]=g0
        small[3:8,:]=jnp.zeros((5,D),F32)
        rows[...]=(sel[:,D:].astype(F32)+mid[...]+gin+glog*router).astype(BF)
        n=D//nb
        for k in range(nb):
            vsend[k]=jnp.concatenate([small[:,k*n:(k+1)*n],jnp.zeros((8,128-n),F32)],axis=1)
        for k,d in enumerate(bpeers):
            cp=remote(vsend.at[d[0]],vin.at[k],eS.at[0,k],eR.at[0,k],d); start(cp); vcs.append(cp)
    def t_C(i):
        if i==0: c_first()
        elif i<=20:
            mi,k=divmod(i-1,5)
            if k==0: c_out(mi)
            elif k<4: c_head(mi,k-1)
            else: c_block(mi)
        elif i<=24: c_norm(i-21)
        else: c_last()
    table=dict(YS=t_YS,YR=t_YR,XR=t_XR,LR=t_LR,LL=t_LL,ZR=t_ZR,ZL=t_ZL,F2=t_F2,FY=t_FY,FX=t_FX,FIN=t_FIN,RO=t_RO,RG=t_RG,RF=t_RF,C=t_C,AD=t_AD)
    lanes=lax.broadcasted_iota(jnp.int32,(8,128),1); sub=lax.broadcasted_iota(jnp.int32,(8,128),0)
    keep["tile"]=jnp.zeros((8,128),F32)
    def put(row,lane,val): keep["tile"]=keep["tile"]+jnp.where((lanes==lane)&(sub==row),val,0.0)
    def tot(v): return jnp.sum(jnp.sum(v,axis=0,keepdims=True),axis=1,keepdims=True)
    def blocks(i): return [(j,slice(j*192,(j+1)*192)) for j in range(4)] if i==0 else [(3+i,slice(0,D))]
    rlane=lax.broadcasted_iota(jnp.int32,(rp,128),1)
    def t_WQ():
        for i in range(3):
            for (j,s) in blocks(i):
                wv=w_ref[i,:,s].astype(F32); put(2,j,tot(wv*wv))
        for j in range(3):
            wv=vold_ref[j:j+1,:]; put(2,6+j,tot(wv*wv)*0.25); put(0,6+j,1.0/(4*nb))
        cloc[...]=jnp.zeros_like(cloc)
        rloc[...]=jnp.zeros_like(rloc)
    def t_VS():
        for cp in vcs: cp.wait_recv()
        vs=vsend[p.b]
        for k in range(nb-1): vs=vs+vin[k]
        vsend[p.b]=vs
        keep["vms"]=[]
        for k,d in enumerate(mpeers):
            cp=remote(vsend.at[p.b],vmp.at[k],eS.at[1,k],eR.at[1,k],d); start(cp); keep["vms"].append(cp)
    def t_VM():
        for cp in keep["vms"]: cp.wait_recv()
        vs=vsend[p.b]
        for k in range(3): vs=vs+vmp[k]
        V_ref[0:8,:]=vs
        mom=0.5*vmom_ref[...]+0.5*(vs*vs+EPS_SQUARE)
        V_ref[8:16,:]=mom
        vd=jnp.where(lanes<D//nb,vs*lax.rsqrt(mom),0.0)
        vdir_ref[...]=vd
        for j in range(3): put(1,6+j,tot(vd[j:j+1]*vd[j:j+1])*0.25)
    def t_ST(i):
        sq=Gs_ref[i]; sq=sq*sq+EPS_SQUARE
        for (j,s) in blocks(i): rloc[...]+=jnp.where(rlane==j,jnp.sum(sq[:,s],axis=1,keepdims=True),0.0)
        line=jnp.sum(sq,axis=0,keepdims=True)
        for k in range(D//128): cloc[i*(D//128)+k:i*(D//128)+k+1,:]=line[:,k*128:(k+1)*128]
    def t_R1():
        rturn[...]=jnp.concatenate([rloc[...].T[0:8],jnp.zeros((8,128-rp),F32)],axis=1)
        ccs=[];rcs=[]
        for k,d in enumerate(bpeers):
            cp=remote(cloc,cin.at[k],eS.at[2,k],eR.at[2,k],d); start(cp); ccs.append(cp)
        for k,d in enumerate(mpeers):
            cp=remote(rturn,rin.at[k],eS.at[3,k],eR.at[3,k],d); start(cp); rcs.append(cp)
        keep["ccs"],keep["rcs"]=ccs,rcs
    def t_R2():
        for cp in keep["rcs"]: cp.wait_recv()
        rs=(rturn[...]+rin[0]+rin[1]+rin[2]).T[0:rp]
        rs=jnp.concatenate([rs,jnp.zeros((rp,120),F32)],axis=1)
        ncol=jnp.where(rlane>=4,1.0/3072.0,1.0/768.0)
        rnew=0.5*rold_ref[...]+0.5*rs*ncol
        R_ref[...]=rnew
        for cp in keep["ccs"]: cp.wait_recv()
        cs=cloc[...]
        for k in range(nb-1): cs=cs+cin[k]
        n6=D//128
        cs=jnp.concatenate([jnp.concatenate([cs[i*n6+k:i*n6+k+1] for k in range(n6)],axis=1) for i in range(3)]+[jnp.zeros((5,D),F32)],axis=0)
        cnew=0.5*cold_ref[...]+0.5*cs*(1.0/768.0)
        C_ref[...]=cnew
        cinv=1.0/cnew; rinv=1.0/rnew
        for i in range(3):
            g=Gs_ref[i]; g2=g*g*cinv[i:i+1,:]
            for (j,s) in blocks(i):
                put(1,j,tot(g2[:,s]*rinv[:,j:j+1]))
        for j in (0,1,2,4): put(0,j,tot(rnew[:,j:j+1])*(1.0/(768*4)))
        put(0,3,tot(cnew[0:1,576:768])*(1.0/(768*nb)))
        put(0,5,tot(cnew[2:3,:])*(1.0/(3072*nb)))
        tile=keep["tile"]
        sloc[0]=tile
        scs=[]
        for k,d in enumerate(bpeers):
            cp=remote(sloc.at[0],sin.at[k],eS.at[4,k],eR.at[4,k],d); start(cp); scs.append(cp)
        keep["scs"]=scs
    def t_R3():
        for cp in keep["scs"]: cp.wait_recv()
        tile=keep["tile"]
        for k in range(nb-1): tile=tile+sin[k]
        sloc[1]=tile
        scs=[]
        for k,d in enumerate(mpeers):
            cp=remote(sloc.at[1],smp.at[k],eS.at[5,k],eR.at[5,k],d); start(cp); scs.append(cp)
        keep["scs"]=scs; keep["tile"]=tile
    def t_R4():
        for cp in keep["scs"]: cp.wait_recv()
        tile=keep["tile"]
        for k in range(3): tile=tile+smp[k]
        lane=lanes[0:1]
        count=jnp.where(lane<4,768.0*768.0,jnp.where(lane<6,768.0*3072.0,768.0))
        live=lane<9
        mean=jnp.where(live,tile[0:1],1.0)
        urms=jnp.sqrt(mean*tile[1:2]/count)
        coef=jnp.sqrt(tile[2:3]/count)/jnp.maximum(1.0,urms/CLIP)*jnp.sqrt(mean)
        out=jnp.concatenate([urms,coef,jnp.zeros((6,128),F32)],axis=0)
        S_ref[...]=out
    table.update(WQ=t_WQ,VS=t_VS,VM=t_VM,ST=t_ST,R1=t_R1,R2=t_R2,R3=t_R3,R4=t_R4)
    for n in order: table[n[0]](*n[1:])
    for k in range(2):
        cp,lc=core_rows(k); cp.wait_recv(); lc.wait(); fwd_rows(k).wait_recv()
    for cond,cp in pend:
        if cond is None: cp.wait_send()
        else:
            @pl.when(cond)
            def _(): cp.wait_send()
def back_call(Gown,Gpart,W0,sel,P,probs,att,mid,accb,rows,gg,vec,w,olds,nb,picks):
    D=768; nz=nb//2; rp=w.shape[1]; T=rows.shape[0]; R=T//picks
    V=pltpu.VMEM; S=pltpu.SemaphoreType.DMA
    vm=pl.BlockSpec(memory_space=V); an=pl.BlockSpec(memory_space=pl.ANY)
    sd=jax.ShapeDtypeStruct
    order=list(BACK_ORDER)
    return pl.pallas_call(functools.partial(back_kernel,order,nz,rp,nb,picks),
        out_shape=(sd((3,rp,D),F32),sd((4,T,D),BF),sd((4,T,D),BF),sd((rp,128),F32),sd((8,D),F32),sd((8,128),F32),sd((16,128),F32),sd((8,128),F32),sd((8,128),F32)),
        in_specs=[an]*10+[vm]*(3+len(olds)),out_specs=(vm,an,an)+(vm,)*6,
        scratch_shapes=[V((3,2,D,D),BF),V((3,2,D,D),BF),V((2,2,nz,rp,D),BF),V((2,nz,rp,D),BF),V((2,nz,rp,D),BF),V((2,nz,rp,D),BF),
            V((4,nz,rp,D),BF),V((4,nz,rp,D),BF),V((2,rp,D),BF),V((rp,D),BF),V((2,D,D),BF),
            V((4,D,D),BF),V((T,2*D),BF),V((4,T,D),BF),V((R,4,3,picks,picks),BF),V((4,T,192),BF),V((T,D),F32),V((T,D),F32),V((T,D),F32),
            V((T,D),BF),V((D,T),BF),V((D,T),BF),V((T,192),BF),V((D,192),F32),V((T,D),BF),
            V((nb,8,128),F32),V((3,8,128),F32),V((nb,24,128),F32),V((3,8,128),F32),
            V((nb,8,128),F32),V((3,8,128),F32),V((rp,128),F32),V((24,128),F32),V((2,8,128),F32),V((nb,8,128),F32),V((8,D),F32),V((8,128),F32),V((rp,128),F32),V((8,D),F32),V((8,128),F32),
            S((17,)),S((3,2)),S((3,2)),S((2,2,nz)),S((2,2,nz)),S((2,nz)),S((2,nz)),S((4,2,nz)),S((4,2,nz)),S((2,2,nz)),S((2,2,nz)),
            S((2,2)),S((2,2)),S((2,6)),S((2,6)),S((6,nb)),S((6,nb))],
        compiler_params=pltpu.CompilerParams(collective_id=1,has_side_effects=True,vmem_limit_bytes=58<<20),
        name="back")(Gown,Gpart,W0,sel,P,probs,att,mid,accb,rows,gg,vec,w,*olds)


BF=jnp.bfloat16; F32=jnp.float32; D=768
OUT_SLOTS=3
def place_kernel(tok_ref, cot_ref, rows_ref, grads_ref, sel_ref, G_ref, w_ref, vold_ref, R_ref, C_ref, S_ref, V_ref, vdir_ref,
                 bo_ref, ig_ref, qg, qr, qc, qn, og, orr, oc, on, ug, ur, uc, un, dgr, dr, dc, dn, rg, rm, rn, gg, gmo, gn, ur_ms,
                 tokb, cotb, rowb, gradb, bob, igb, lsem, ssem):
    rows,length=tok_ref.shape[0:2]; picks=rows_ref.shape[1]
    def loads(r): return [pltpu.make_async_copy(src.at[r],dst.at[r],lsem.at[k,r]) for k,(src,dst) in enumerate(((tok_ref,tokb),(rows_ref,rowb),(cot_ref,cotb),(grads_ref,gradb)))]
    def stores(r,slot): return [pltpu.make_async_copy(src.at[slot],dst.at[r],ssem.at[k,slot]) for k,(src,dst) in enumerate(((bob,bo_ref),(igb,ig_ref)))]
    for r in range(rows):
        for cp in loads(r): cp.start()
    def new(i,s,j):
        g=G_ref[i,:,s]
        return g,w_ref[i,:,s].astype(F32)-S_ref[1:2,j:j+1]*(g*lax.rsqrt(R_ref[:,j:j+1]*C_ref[i:i+1,s]))
    for j in range(3):
        qg[j],qn[j]=new(0,slice(j*192,(j+1)*192),j)
        qc[j:j+1,:]=C_ref[0:1,j*192:(j+1)*192]
    g,n=new(0,slice(576,768),3); og[...]=g.T; on[...]=n.T
    g,n=new(1,slice(0,D),4); ug[...]=g; un[...]=n
    g,n=new(2,slice(0,D),5); dgr[...]=g; dn[...]=n
    Rt=R_ref[...].T
    qr[...]=Rt[0:3]; oc[...]=Rt[3:4]; ur[...]=Rt[4:5]; dc[...]=Rt[5:6]
    orr[...]=C_ref[0:1,576:768];
    for k in range(D//128):
        uc[k:k+1,:]=C_ref[1:2,k*128:(k+1)*128]; dr[k:k+1,:]=C_ref[2:3,k*128:(k+1)*128]
    ur_ms[...]=S_ref[0:1,0:9]
    rg[...]=V_ref[0:1,0:96]; gg[...]=V_ref[1:3,0:96]
    rm[...]=V_ref[8:9,0:96]; gmo[...]=V_ref[9:11,0:96]
    rn[...]=vold_ref[0:1,0:96]-S_ref[1:2,6:7]*vdir_ref[0:1,0:96]
    gn[0:1,:]=vold_ref[1:2,0:96]-S_ref[1:2,7:8]*vdir_ref[1:2,0:96]
    gn[1:2,:]=vold_ref[2:3,0:96]-S_ref[1:2,8:9]*vdir_ref[2:3,0:96]
    first=lax.axis_index("mp")*length
    @pl.loop(0,rows)
    def _(r):
        slot=lax.rem(r,OUT_SLOTS)
        pos=lax.broadcasted_iota(jnp.int32,(length,picks),0)
        hot=(pos==sel_ref[pl.ds(r,1),:]-first).astype(F32)
        cover=jnp.sum(hot,axis=1,keepdims=True)>0.5
        hot=hot.astype(BF)
        for cp in loads(r): cp.wait()
        @pl.when(r>=OUT_SLOTS)
        def _():
            for cp in stores(r-OUT_SLOTS,slot): cp.wait()
        bob[slot]=jnp.where(cover,jnp.dot(hot,rowb[r],preferred_element_type=F32),tokb[r].astype(F32)).astype(BF)
        igb[slot]=jnp.where(cover,jnp.dot(hot,gradb[r],preferred_element_type=F32),cotb[r].astype(F32))
        for cp in stores(r,slot): cp.start()
    for r in range(rows-OUT_SLOTS,rows):
        for cp in stores(r,r%OUT_SLOTS): cp.wait()
def place_call(tokens,cot,allrows,allgrads,selrel,G,w,vold,R,C,S,V,vdir):
    rows,length,_=tokens.shape; picks=selrel.shape[1]
    allrows=allrows.reshape(rows,picks,D); allgrads=allgrads.reshape(rows,picks,D)
    sd=lambda *s: jax.ShapeDtypeStruct(s,F32)
    rp=w.shape[1]
    small=[(3,rp,192),(3,rp),(3,192),(3,rp,192),(192,rp),(1,192),(1,rp),(192,rp),(rp,D),(1,rp),(D//128,128),(rp,D),(rp,D),(D//128,128),(1,rp),(rp,D),(1,rp),(1,rp),(1,rp),(2,rp),(2,rp),(2,rp),(1,9)]
    V_=pltpu.VMEM; vm=pl.BlockSpec(memory_space=V_); an=pl.BlockSpec(memory_space=pl.ANY)
    return pl.pallas_call(place_kernel,
        out_shape=(jax.ShapeDtypeStruct(tokens.shape,BF),jax.ShapeDtypeStruct(cot.shape,F32))+tuple(sd(*s) for s in small),
        in_specs=[an]*4+[vm]*9,out_specs=(an,an)+(vm,)*len(small),
        scratch_shapes=[V_((rows,length,D),BF),V_((rows,length,D),BF),V_((rows,picks,D),BF),V_((rows,picks,D),BF),V_((OUT_SLOTS,length,D),BF),V_((OUT_SLOTS,length,D),F32),
            pltpu.SemaphoreType.DMA((4,rows)),pltpu.SemaphoreType.DMA((2,OUT_SLOTS))],
        compiler_params=pltpu.CompilerParams(vmem_limit_bytes=60<<20),
        name="place")(tokens,cot,allrows,allgrads,selrel,G,w,vold,R,C,S,V,vdir)


def local_fast(tokens,segments,selection,cotangent,qkv_weight,out_weight,up_weight,down_weight,router_weight,norm_gains,
               qkv_rows,qkv_cols,out_rows,out_cols,up_rows,up_cols,down_rows,down_cols,router_moment,gains_moment):
    nb=lax.axis_size("batch"); picks=selection.shape[1]
    w,W0,Gown,Gpart,sel,projected,probs,attended,middle,grad_mid,rows_low,grad_gate,vall=fore_call(
        qkv_weight,out_weight,up_weight,down_weight.T,router_weight[None],norm_gains,tokens,cotangent,selection,segments,nb,picks)
    olds=(qkv_rows,qkv_cols,out_rows[None],out_cols[None],up_rows[None],up_cols.reshape(-1,128),down_rows.reshape(-1,128),down_cols[None],
          router_weight[None],norm_gains,router_moment[None],gains_moment)
    Gs,allrows,allgrads,R,C,S,V,vdir,vold=back_call(Gown,Gpart,W0,sel,projected,probs,attended,middle,grad_mid,rows_low,grad_gate,vall,w,olds,nb,picks)
    (bo,ig,qg,qr,qc,qn,og,orr,oc,on,ug,ur,uc,un,dgr,dr,dc,dn,rg,rm,rn,gg,gmo,gn,rms)=place_call(
        tokens,cotangent,allrows,allgrads,selection,Gs,w,vold,R,C,S,V,vdir)
    return (bo,ig,qg,qr,qc,qn,og,orr[0],oc[0],on,ug,ur[0],uc.reshape(-1),un,dgr.T,dr.reshape(-1),dc[0],dn.T,rg[0],rm[0],rn[0],gg,gmo,gn,rms[0])

def chosen_local(mesh):
    return local_fast if (mesh.shape["batch"],mesh.shape["mp"])==(8,4) else local_any


def solution(mesh):
    in_specs = (
        P("batch", "mp", None),
        P("batch", None),
        P("batch", None),
        P("batch", "mp", None),
        P(None, "batch", "mp"),
        P("mp", "batch"),
        P("batch", "mp"),
        P("mp", "batch"),
        P("batch"),
        P(None, "batch"),
        P(None, "batch"),
        P(None, "mp"),
        P("mp"),
        P("batch"),
        P("batch"),
        P("mp"),
        P("mp"),
        P("batch"),
        P("batch"),
        P(None, "batch"),
    )
    out_specs = (
        P("batch", "mp", None),
        P("batch", "mp", None),
        P(None, "batch", "mp"),
        P(None, "batch"),
        P(None, "mp"),
        P(None, "batch", "mp"),
        P("mp", "batch"),
        P("mp"),
        P("batch"),
        P("mp", "batch"),
        P("batch", "mp"),
        P("batch"),
        P("mp"),
        P("batch", "mp"),
        P("mp", "batch"),
        P("mp"),
        P("batch"),
        P("mp", "batch"),
        P("batch"),
        P("batch"),
        P("batch"),
        P(None, "batch"),
        P(None, "batch"),
        P(None, "batch"),
        P(),
    )
    return jax.shard_map(chosen_local(mesh), mesh=mesh, in_specs=in_specs, out_specs=out_specs, check_vma=False)
```
